32 devices in a mesh: fsdp: 8 (over z, x), ctx: 4 (over y, core).
Axes of the slice: x: 2, y: 2, z: 4, core: 2. Of those that a mesh axis runs over, the one named last changes fastest.
Arguments:
- tokens: bfloat16 [512, 4096], P('ctx'), may hold values from -6 to 6
- in_weight: bfloat16 [4096, 3, 4096], P('ctx', None, 'fsdp'), may hold values from -0.09375 to 0.09375
- conv_taps: float32 [7, 3, 4096], P(None, None, 'fsdp'), may hold values from -2 to 2
- decay_rate: float32 [16, 4096], P(None, 'fsdp'), may hold values from 3.90625e-05 to 0.05
- residue: float32 [16, 4096], P(None, 'fsdp'), may hold values from -1.5 to 1.5
- skip_gain: float32 [4096], P('fsdp'), may hold values from -3 to 3
- out_weight: bfloat16 [4096, 4096], P('ctx', 'fsdp'), may hold values from -0.09375 to 0.09375
- grad_mixed: bfloat16 [512, 4096], P('ctx'), may hold values from -6 to 6
Outputs:
- mixed: bfloat16 [512, 4096], P('ctx', 'fsdp')
- grad_tokens: bfloat16 [512, 4096], P('ctx', 'fsdp')
- grad_in_weight: float32 [4096, 3, 4096], P('ctx', None, 'fsdp')
- grad_out_weight: float32 [4096, 4096], P('ctx', 'fsdp')
The draws below stay inside these ranges and needn't reach their ends.
All inputs are finite; a program needn't handle non-finite values.
Results may differ from the reference program's by a relative error of at most 0.014.
Values may be sent and summed in bfloat16 or wider, within the bound.
No kernel may reach another device: no remote copies, remote signals or barrier semaphores. Data moves between devices by JAX's collectives and lax.ppermute only.
A program may use at most 128 MiB of HBM per device.

```python
import math
import jax
import jax.numpy as jnp
from jax import lax

D = 4096
C = 4096
POLES = 16
TAPS = 7
TOK_DEV = 128
TOKENS = 512
N_FSDP = 8
N_CTX = 4


def with_spikes(values, own_key, source, target, shards_of, factor):
    owner, partner = [(jnp.arange(values.shape[position]) // (values.shape[position] // shards_of)).reshape([-1 if axis == position else 1 for axis in range(values.ndim)]) for position in (source, target)]
    chosen = jax.random.permutation(own_key, shards_of)[partner]
    strong = (owner == chosen) | (owner == (partner + shards_of // 2) % shards_of)
    return jnp.where(strong, factor * values, values)


def block_scale(key, dims, shards, smallest, high):
    loudness, own = 1.0, jax.random.fold_in(key, 6)
    for position, blocks in shards:
        heights = jnp.exp(jax.random.uniform(jax.random.fold_in(own, position), (blocks,), jnp.float32, smallest / len(shards), high / len(shards)))
        loudness = loudness * jnp.repeat(heights, dims[position] // blocks).reshape([-1 if axis == position else 1 for axis in range(len(dims))])
    return loudness


def centred(key, shape, spread, bound, cuts=(), kind=jnp.bfloat16):
    array = spread * jax.random.normal(key, shape, jnp.float32)
    if cuts:
        array = array * block_scale(key, shape, cuts, -0.22, 0.18)
    return jnp.clip(array, -bound, bound).astype(kind)


def noise_with(rng, extent, deviation, reach, shards, heavy, kind=jnp.bfloat16):
    values = deviation * jax.random.normal(rng, extent, jnp.float32)
    if shards:
        values = values * block_scale(rng, extent, shards, -0.22, 0.18)
    return jnp.clip(with_spikes(values, jax.random.fold_in(rng, 3), *heavy), -reach, reach).astype(kind)


def setup_inputs(seed: int = 0) -> dict:
    keys = jax.random.split(jax.random.key(seed), 9)
    return {
        "tokens": noise_with(keys[0], (TOKENS, D), 1.0, 6.0, ((0, 4),), (0, 1, 4, 2.0)),
        "in_weight": centred(keys[1], (D, 3, C), D ** -0.5, 0.09375, ((0, 4), (2, 8))),
        "conv_taps": centred(keys[2], (TAPS, 3, C), TAPS ** -0.5, 2.0, ((2, 8),), jnp.float32),
        "decay_rate": jnp.clip(jnp.exp(math.log(0.05) - 7.1546154 * jax.random.uniform(keys[3], (POLES, C), jnp.float32) ** block_scale(keys[3], (POLES, C), ((1, 8),), -0.2, 0.2)), 3.9062499126885086e-05, 0.05),
        "residue": centred(keys[4], (POLES, C), POLES ** -0.5, 1.5, ((1, 8),), jnp.float32),
        "skip_gain": centred(keys[5], (C,), 0.5, 3.0, ((0, 8),), jnp.float32),
        "out_weight": centred(keys[6], (D, C), C ** -0.5, 0.09375, ((0, 4), (1, 8))),
        "grad_mixed": noise_with(keys[7], (TOKENS, D), 1.0, 6.0, ((0, 4),), (0, 1, 4, 2.0)),
    }


def pole_terms(decay_rate, residue):
    return (jnp.exp(-decay_rate), residue * jnp.sqrt(-jnp.expm1(-2.0 * decay_rate)))

def rounded(values):
    return lax.optimization_barrier(values.astype(jnp.bfloat16)).astype(jnp.float32)

def causal_mix(values, conv_taps):
    length = values.shape[0]
    total = jnp.zeros(values.shape, jnp.float32)
    for lag in range(TAPS):
        moved = jnp.pad(values, ((lag, 0), (0, 0), (0, 0)))[:length]
        total = total + conv_taps[lag] * moved
    return total

def anti_mix(values, conv_taps):
    length = values.shape[0]
    total = jnp.zeros(values.shape, jnp.float32)
    for lag in range(TAPS):
        moved = jnp.pad(values, ((0, lag), (0, 0), (0, 0)))[lag:lag + length]
        total = total + conv_taps[lag] * moved
    return total

def modal_filter(signal, decay, gain, skip_gain, backward):

    def advance(state, entry):
        state = decay * state + entry[None, :]
        return (state, lax.optimization_barrier(jnp.sum(gain * state, axis=0)) + skip_gain * entry)
    _, result = lax.scan(advance, jnp.zeros(decay.shape, jnp.float32), signal, reverse=backward)
    return result

def reference(tokens, in_weight, conv_taps, decay_rate, residue, skip_gain, out_weight, grad_mixed):
    decay, gain = pole_terms(decay_rate, residue)
    feats = jnp.dot(tokens, in_weight.reshape(D, 3 * C), preferred_element_type=jnp.float32)
    feats = feats.astype(jnp.bfloat16).reshape(TOKENS, 3, C)
    mixed_in = causal_mix(feats.astype(jnp.float32), conv_taps)
    query = mixed_in[:, 0]
    key = mixed_in[:, 1]
    value = mixed_in[:, 2]
    signal = key * value
    long_out = modal_filter(signal, decay, gain, skip_gain, False)
    gated = (query * long_out).astype(jnp.bfloat16)
    width = C // N_FSDP
    channel_blocks = jnp.arange(N_FSDP, dtype=jnp.int32)

    def output_block(total, index):
        start = index * width
        part_gated = lax.dynamic_slice_in_dim(gated, start, width, 1)
        part_weight = lax.dynamic_slice_in_dim(out_weight, start, width, 1)
        term = lax.dot_general(part_gated, part_weight, (((1,), (1,)), ((), ())), preferred_element_type=jnp.float32)
        return (total + rounded(term), None)
    mixed, _ = lax.scan(output_block, jnp.zeros((TOKENS, D), jnp.float32), channel_blocks)
    mixed = mixed.astype(jnp.bfloat16)
    grad_gated = jnp.dot(grad_mixed, out_weight, preferred_element_type=jnp.float32)
    grad_query = grad_gated * long_out
    grad_long = grad_gated * query
    grad_signal = modal_filter(grad_long, decay, gain, skip_gain, True)
    grad_mixin = jnp.stack([grad_query, grad_signal * value, grad_signal * key], axis=1)
    grad_feats = anti_mix(grad_mixin, conv_taps).astype(jnp.bfloat16)

    def input_block(total, index):
        start = index * width
        part_grad = lax.dynamic_slice_in_dim(grad_feats, start, width, 2).reshape(TOKENS, 3 * width)
        part_weight = lax.dynamic_slice_in_dim(in_weight, start, width, 2).reshape(D, 3 * width)
        term = lax.dot_general(part_grad, part_weight, (((1,), (1,)), ((), ())), preferred_element_type=jnp.float32)
        return (total + rounded(term), None)
    grad_tokens, _ = lax.scan(input_block, jnp.zeros((TOKENS, D), jnp.float32), channel_blocks)
    grad_tokens = grad_tokens.astype(jnp.bfloat16)
    flat_grad = grad_feats.reshape(TOKENS, 3 * C)

    def weight_block(totals, index):
        start = index * TOK_DEV
        part_tokens = lax.dynamic_slice_in_dim(tokens, start, TOK_DEV, 0)
        part_feats = lax.dynamic_slice_in_dim(flat_grad, start, TOK_DEV, 0)
        part_cotangent = lax.dynamic_slice_in_dim(grad_mixed, start, TOK_DEV, 0)
        part_gated = lax.dynamic_slice_in_dim(gated, start, TOK_DEV, 0)
        term_in = lax.dot_general(part_tokens, part_feats, (((0,), (0,)), ((), ())), preferred_element_type=jnp.float32)
        term_out = lax.dot_general(part_cotangent, part_gated, (((0,), (0,)), ((), ())), preferred_element_type=jnp.float32)
        return ((totals[0] + rounded(term_in), totals[1] + rounded(term_out)), None)
    start_totals = (jnp.zeros((D, 3 * C), jnp.float32), jnp.zeros((D, C), jnp.float32))
    (grad_in, grad_out), _ = lax.scan(weight_block, start_totals, jnp.arange(N_CTX, dtype=jnp.int32))
    return (mixed, grad_tokens, grad_in.reshape(D, 3, C), grad_out)
```

```python
import functools

import jax
import jax.numpy as jnp
from jax import lax
from jax.experimental import pallas as pl
from jax.experimental.pallas import tpu as pltpu
from jax.sharding import PartitionSpec as P

BF16 = jnp.bfloat16
F32 = jnp.float32
LANES = 128
CHUNKS = 8
MARGIN = 8
VMEM_LIMIT = 48 * 1024 * 1024


def call(body, outs, scratch=(), flops=0, nbytes=0):
    return pl.pallas_call(
        body,
        out_shape=outs,
        scratch_shapes=list(scratch),
        compiler_params=pltpu.CompilerParams(vmem_limit_bytes=VMEM_LIMIT),
        cost_estimate=pl.CostEstimate(flops=flops, bytes_accessed=nbytes, transcendentals=0),
    )


def flipped(value, axis, mask):
    count = lax.axis_size(axis)
    return lax.ppermute(value, axis, [(source, source ^ mask) for source in range(count)])


def block_at(index, size):
    return pl.ds(pl.multiple_of(index * size, size), size)


def dot(left, right, contract):
    return lax.dot_general(left, right, ((contract[:1], contract[1:]), ((), ())), preferred_element_type=F32)


def shifted(value, steps, backward):
    rows = lax.broadcasted_iota(jnp.int32, value.shape, 0)
    if backward:
        return jnp.where(rows < CHUNKS - steps, pltpu.roll(value, CHUNKS - steps, 0), 0.0)
    return jnp.where(rows >= steps, pltpu.roll(value, steps, 0), 0.0)


def modal_scan(source, target, decay, spread, gain, backward):
    poles, width = decay.shape
    steps = source.shape[0] // CHUNKS
    wide = lambda table, n: jnp.broadcast_to(table[n : n + 1, :], (CHUNKS, width))
    decays = [wide(decay, n) for n in range(poles)]

    def rows(i):
        return pl.ds(steps - 1 - i if backward else i, CHUNKS, stride=steps)

    def gather_up(i, states):
        entry = source[rows(i), :]
        return tuple(d * s + entry for d, s in zip(decays, states))

    zero = jnp.zeros((CHUNKS, width), F32)
    ends = lax.fori_loop(0, steps, gather_up, (zero,) * poles, unroll=4)
    states = []
    for n in range(poles):
        factor = wide(spread, n)
        state = shifted(ends[n], 1, backward)
        reach = 1
        while reach < CHUNKS:
            state = state + factor * shifted(state, reach, backward)
            factor = factor * factor
            reach *= 2
        states.append(state)
    gains = [wide(gain, n) for n in range(poles)]

    def advance(i, states):
        entry = source[rows(i), :]
        states = tuple(d * s + entry for d, s in zip(decays, states))
        terms = [g * s for g, s in zip(gains, states)]
        while len(terms) > 1:
            terms = [a + b for a, b in zip(terms[::2], terms[1::2])]
        target[rows(i), :] = terms[0]
        return states

    lax.fori_loop(0, steps, advance, tuple(states), unroll=2)


def row_blocks(length):
    size = 64 if length % 64 == 0 else length
    return [(start, size) for start in range(0, length, size)]


def forward_body(parts, kinds, taps, decay, spread, gain, skip, query, key, value, long_out, gated, feats, signal, summed):
    length, width = query.shape
    blocks = row_blocks(length)
    for j in range(3):
        feats[j, :MARGIN, :] = jnp.zeros((MARGIN, width), F32)
        for start, size in blocks:
            total = kinds(parts, j, pl.ds(start, size))
            feats[j, MARGIN + start : MARGIN + start + size, :] = total.astype(BF16).astype(F32)
    for start, size in blocks:
        mixed = []
        for j in range(3):
            total = taps[0, j : j + 1, :] * feats[j, MARGIN + start : MARGIN + start + size, :]
            for lag in range(1, taps.shape[0]):
                first = MARGIN + start - lag
                total = total + taps[lag, j : j + 1, :] * feats[j, first : first + size, :]
            mixed.append(total)
        at = slice(start, start + size)
        query[at, :], key[at, :], value[at, :] = mixed
        signal[at, :] = mixed[1] * mixed[2]
    modal_scan(signal, summed, decay[...], spread[...], gain[...], False)
    for start, size in blocks:
        at = slice(start, start + size)
        result = summed[at, :] + skip[...] * signal[at, :]
        long_out[at, :] = result
        gated[at, :] = (query[at, :] * result).astype(BF16)


def backward_body(parts, kinds, taps, decay, spread, gain, skip, query, key, value, long_out, grads, mixin, grad_long, summed):
    length, width = query.shape
    blocks = row_blocks(length)
    for start, size in blocks:
        at = slice(start, start + size)
        grad_gated = kinds(parts, 0, pl.ds(start, size))
        mixin[0, at, :] = grad_gated * long_out[at, :]
        grad_long[at, :] = grad_gated * query[at, :]
    modal_scan(grad_long, summed, decay[...], spread[...], gain[...], True)
    for start, size in blocks:
        at = slice(start, start + size)
        grad_signal = summed[at, :] + skip[...] * grad_long[at, :]
        mixin[1, at, :] = grad_signal * value[at, :]
        mixin[2, at, :] = grad_signal * key[at, :]
    for j in range(3):
        mixin[j, length : length + MARGIN, :] = jnp.zeros((MARGIN, width), F32)
        for start, size in blocks:
            total = taps[0, j : j + 1, :] * mixin[j, start : start + size, :]
            for lag in range(1, taps.shape[0]):
                total = total + taps[lag, j : j + 1, :] * mixin[j, start + lag : start + lag + size, :]
            grads[j, start : start + size, :] = total.astype(BF16)


def sum_of_three(parts, j, at):
    own, near, far = parts
    return own[j, at, :] + near[0, j, at, :].astype(F32) + far[j, at, :].astype(F32)


def plain(parts, j, at):
    return parts[0][j, at, :].astype(F32)


def filter_forward(parts, kinds, tables, length, width):
    count = len(parts)

    def body(*refs):
        forward_body(refs[:count], kinds, *refs[count:])

    wide = jax.ShapeDtypeStruct((length, width), F32)
    return call(
        body,
        (wide, wide, wide, wide, jax.ShapeDtypeStruct((length, width), BF16)),
        [
            pltpu.VMEM((3, MARGIN + length, width), F32),
            pltpu.VMEM((length, width), F32),
            pltpu.VMEM((length, width), F32),
        ],
        flops=200 * length * width,
        nbytes=40 * length * width,
    )(*parts, *tables)


def filter_backward(parts, kinds, tables, saved, length, width):
    count = len(parts)

    def body(*refs):
        backward_body(refs[:count], kinds, *refs[count:])

    return call(
        body,
        jax.ShapeDtypeStruct((3, length, width), BF16),
        [
            pltpu.VMEM((3, length + MARGIN, width), F32),
            pltpu.VMEM((length, width), F32),
            pltpu.VMEM((length, width), F32),
        ],
        flops=200 * length * width,
        nbytes=40 * length * width,
    )(*parts, *tables, *saved)


def own_columns(rows):
    me = lax.axis_index("ctx")
    count = lax.axis_size("ctx")
    width = rows.shape[1] // count
    part = lambda mask: lax.dynamic_slice_in_dim(rows, (me ^ mask) * width, width, 1)
    return [part(0)] + [flipped(part(mask), "ctx", mask) for mask in range(1, count)]


def project(pieces, weight):
    groups, depth, channels = weight.shape
    part = pieces[0].shape[0]
    length = 4 * part
    width = channels // 4

    def body(a, b, c, d, weight, own, far, give, held, product):
        me = lax.axis_index("ctx")
        for mask, piece in enumerate((a, b, c, d)):
            held[block_at(me ^ mask, part), :] = piece[...]
        for j in range(groups):
            product[...] = dot(held[...], weight[j], (1, 0))
            own[j] = product[:, block_at(me, width)]
            far[j] = product[:, block_at(me ^ 2, width)].astype(BF16)
            give[0, j] = product[:, block_at(me ^ 1, width)].astype(BF16)
            give[1, j] = product[:, block_at(me ^ 3, width)].astype(BF16)

    return call(
        body,
        (
            jax.ShapeDtypeStruct((groups, length, width), F32),
            jax.ShapeDtypeStruct((groups, length, width), BF16),
            jax.ShapeDtypeStruct((2, groups, length, width), BF16),
        ),
        [pltpu.VMEM((length, depth), BF16), pltpu.VMEM((length, channels), F32)],
        flops=2 * length * depth * channels * groups,
        nbytes=2 * (length * depth + groups * depth * channels + 2 * groups * length * channels),
    )(*pieces, weight)


def channel_sums(pieces, weight):
    own, far, give = project(pieces, weight)
    near = flipped(give, "ctx", 1)
    passed = (far.astype(F32) + near[1].astype(F32)).astype(BF16)
    return own, near, flipped(passed, "ctx", 2)


def all_channels(value):
    far = flipped(value, "ctx", 2)
    return value, far, flipped(jnp.stack([value, far]), "ctx", 1)


def output_halves(gathered, weight):
    own, far, near = gathered
    groups, length, width = own.shape
    depth = weight.shape[1]
    half = depth // 2
    channels = 4 * width

    def body(own, far, near, weight, whole, keep, give):
        me = lax.axis_index("ctx")
        side = lax.axis_index("fsdp") & 1
        for j in range(groups):
            whole[j, :, block_at(me, width)] = own[j]
            whole[j, :, block_at(me ^ 2, width)] = far[j]
            whole[j, :, block_at(me ^ 1, width)] = near[0, j]
            whole[j, :, block_at(me ^ 3, width)] = near[1, j]
        for part, out in ((1 - side, give), (side, keep)):
            total = None
            for j in range(groups):
                term = dot(whole[j], weight[j, block_at(part, half), :], (1, 1))
                total = term if total is None else total + term
            out[...] = total.astype(BF16)

    return call(
        body,
        (
            jax.ShapeDtypeStruct((groups, length, channels), BF16),
            jax.ShapeDtypeStruct((length, half), BF16),
            jax.ShapeDtypeStruct((length, half), BF16),
        ),
        flops=2 * length * depth * channels * groups,
        nbytes=2 * (groups * length * channels * 2 + groups * depth * channels + length * depth),
    )(own, far, near, weight)


def split_sum(keep, given):
    length, width = keep.shape
    part = length // 4

    def body(keep, given, *outs):
        place = lax.axis_index("fsdp") >> 1
        for mask, out in enumerate(outs):
            at = block_at(place ^ mask, part)
            out[...] = (keep[at, :].astype(F32) + given[at, :].astype(F32)).astype(BF16)

    return call(
        body, (jax.ShapeDtypeStruct((part, width), BF16),) * 4, flops=length * width, nbytes=6 * length * width
    )(keep, given)


def to_placement(value):
    count = lax.axis_size("ctx")
    ratio = lax.axis_size("fsdp") // count
    pairs = []
    for f in range(ratio * count):
        for k in range(count):
            target = (k * ratio + f % ratio, f // ratio)
            pairs.append((f * count + k, target[0] * count + target[1]))
    return lax.ppermute(value, ("fsdp", "ctx"), pairs)


def block_sums(keep, give):
    blocks = split_sum(keep, flipped(give, "fsdp", 1))
    total = blocks[0].astype(F32)
    for mask in range(1, 4):
        total = total + flipped(blocks[mask], "fsdp", 2 * mask).astype(F32)
    return to_placement(total.astype(BF16))


def four_by_eight(tokens, weights, tables, out_weight, grad_mixed):
    length, width = 4 * tokens.shape[0], weights.shape[2] // 4
    token_pieces = own_columns(tokens)
    grad_pieces = own_columns(grad_mixed)
    feats = channel_sums(token_pieces, weights)
    *saved, gated = filter_forward(feats, sum_of_three, tables, length, width)
    grad_gated = channel_sums(grad_pieces, out_weight[None])
    whole_gated, keep, give = output_halves(all_channels(gated[None]), out_weight[None])
    mixed = block_sums(keep, give)
    grads = filter_backward(grad_gated, sum_of_three, tables, saved, length, width)
    whole_grads, keep, give = output_halves(all_channels(grads), weights)
    grad_tokens = block_sums(keep, give)
    me = lax.axis_index("ctx")

    def in_order(pieces):
        part = pieces[0].shape[0]
        whole = jnp.zeros((length, pieces[0].shape[1]), BF16)
        for mask, piece in enumerate(pieces):
            whole = lax.dynamic_update_slice_in_dim(whole, piece, (me ^ mask) * part, 0)
        return whole

    grad_in = jnp.einsum("td,jtc->jdc", in_order(token_pieces), whole_grads, preferred_element_type=F32)
    grad_out = jnp.einsum("td,tc->dc", in_order(grad_pieces), whole_gated[0], preferred_element_type=F32)
    return mixed, grad_tokens, grad_in, grad_out


def any_mesh(tokens, weights, tables, out_weight, grad_mixed):
    count = lax.axis_size("ctx")
    columns = lambda rows: lax.all_to_all(rows, "ctx", split_axis=1, concat_axis=0, tiled=True)
    whole_tokens, whole_cotangents = columns(tokens), columns(grad_mixed)
    length, width = whole_tokens.shape[0], weights.shape[2] // count

    def channel_sums(rows, weight):
        partial = jnp.einsum("td,jdc->jtc", rows, weight, preferred_element_type=F32)
        return lax.psum_scatter(partial.astype(BF16), "ctx", scatter_dimension=2, tiled=True)

    def block_sums(values, weight):
        partial = jnp.einsum("jtc,jdc->td", values, weight, preferred_element_type=F32)
        ratio = lax.axis_size("fsdp") // count
        pieces = partial.astype(BF16).reshape(count, length // count, ratio, -1).transpose(0, 2, 1, 3)
        pieces = pieces.reshape(count * ratio, length // count, -1)
        return to_placement(lax.psum_scatter(pieces, "fsdp", scatter_dimension=0, tiled=True)[0])

    feats = channel_sums(whole_tokens, weights)
    grad_gated = channel_sums(whole_cotangents, out_weight[None])
    *saved, gated = filter_forward((feats,), plain, tables, length, width)
    grads = filter_backward((grad_gated,), plain, tables, saved, length, width)
    whole_gated = lax.all_gather(gated, "ctx", axis=1, tiled=True)
    whole_grads = lax.all_gather(grads, "ctx", axis=2, tiled=True)
    mixed = block_sums(whole_gated[None], out_weight[None])
    grad_tokens = block_sums(whole_grads, weights)
    grad_in = jnp.einsum("td,jtc->jdc", whole_tokens, whole_grads, preferred_element_type=F32)
    grad_out = jnp.einsum("td,tc->dc", whole_cotangents, whole_gated, preferred_element_type=F32)
    return mixed, grad_tokens, grad_in, grad_out


def per_device(tokens, in_weight, conv_taps, decay_rate, residue, skip_gain, out_weight, grad_mixed):
    count, blocks = lax.axis_size("ctx"), lax.axis_size("fsdp")
    weights = in_weight.transpose(1, 0, 2)
    length = count * tokens.shape[0]
    width = weights.shape[2] // count
    mine = lambda table: lax.dynamic_slice_in_dim(table, lax.axis_index("ctx") * width, width, table.ndim - 1)
    rate = mine(decay_rate)
    gain = mine(residue) * jnp.sqrt(-jnp.expm1(-2.0 * rate))
    tables = (mine(conv_taps), jnp.exp(-rate), jnp.exp(-rate * (length // CHUNKS)), gain, mine(skip_gain[None]))
    tuned = count == 4 and blocks == 8 and width % LANES == 0
    plan = four_by_eight if tuned else any_mesh
    mixed, grad_tokens, grad_in, grad_out = plan(tokens, weights, tables, out_weight, grad_mixed)
    return mixed, grad_tokens, grad_in.transpose(1, 0, 2), grad_out


def solution(mesh):
    return jax.shard_map(
        per_device,
        mesh=mesh,
        in_specs=(
            P("ctx", None),
            P("ctx", None, "fsdp"),
            P(None, None, "fsdp"),
            P(None, "fsdp"),
            P(None, "fsdp"),
            P("fsdp"),
            P("ctx", "fsdp"),
            P("ctx", None),
        ),
        out_specs=(P("ctx", "fsdp"), P("ctx", "fsdp"), P("ctx", None, "fsdp"), P("ctx", "fsdp")),
        check_vma=False,
    )
```

```python
import functools

import jax
import jax.numpy as jnp
from jax import lax
from jax.experimental import pallas as pl
from jax.experimental.pallas import tpu as pltpu
from jax.sharding import PartitionSpec as P

BF16 = jnp.bfloat16
F32 = jnp.float32
LANES = 128
CHUNKS = 8
MARGIN = 8
VMEM_LIMIT = 48 * 1024 * 1024


VMEM = pl.BlockSpec(memory_space=pltpu.VMEM)


def call(body, outs, scratch=(), in_specs=None, flops=0, nbytes=0):
    return pl.pallas_call(
        body,
        out_shape=outs,
        **({} if in_specs is None else {"in_specs": in_specs}),
        scratch_shapes=list(scratch),
        compiler_params=pltpu.CompilerParams(vmem_limit_bytes=VMEM_LIMIT),
        cost_estimate=pl.CostEstimate(flops=flops, bytes_accessed=nbytes, transcendentals=0),
    )


def flipped(value, axis, mask):
    count = lax.axis_size(axis)
    return lax.ppermute(value, axis, [(source, source ^ mask) for source in range(count)])


def block_at(index, size):
    return pl.ds(pl.multiple_of(index * size, size), size)


def dot(left, right, contract):
    return lax.dot_general(left, right, ((contract[:1], contract[1:]), ((), ())), preferred_element_type=F32)


def shifted(value, steps, backward):
    rows = lax.broadcasted_iota(jnp.int32, value.shape, 0)
    if backward:
        return jnp.where(rows < CHUNKS - steps, pltpu.roll(value, CHUNKS - steps, 0), 0.0)
    return jnp.where(rows >= steps, pltpu.roll(value, steps, 0), 0.0)


def modal_scan(source, target, decay, spread, gain, backward):
    poles, width = decay.shape
    steps = source.shape[0] // CHUNKS
    wide = lambda table, n: jnp.broadcast_to(table[n : n + 1, :], (CHUNKS, width))
    decays = [wide(decay, n) for n in range(poles)]

    def rows(i):
        return pl.ds(steps - 1 - i if backward else i, CHUNKS, stride=steps)

    def gather_up(i, states):
        entry = source[rows(i), :]
        return tuple(d * s + entry for d, s in zip(decays, states))

    zero = jnp.zeros((CHUNKS, width), F32)
    ends = lax.fori_loop(0, steps, gather_up, (zero,) * poles, unroll=4)
    states = []
    for n in range(poles):
        factor = wide(spread, n)
        state = shifted(ends[n], 1, backward)
        reach = 1
        while reach < CHUNKS:
            state = state + factor * shifted(state, reach, backward)
            factor = factor * factor
            reach *= 2
        states.append(state)
    gains = [wide(gain, n) for n in range(poles)]

    def advance(i, states):
        entry = source[rows(i), :]
        states = tuple(d * s + entry for d, s in zip(decays, states))
        terms = [g * s for g, s in zip(gains, states)]
        while len(terms) > 1:
            terms = [a + b for a, b in zip(terms[::2], terms[1::2])]
        target[rows(i), :] = terms[0]
        return states

    lax.fori_loop(0, steps, advance, tuple(states), unroll=2)


def row_blocks(length):
    size = 64 if length % 64 == 0 else length
    return [(start, size) for start in range(0, length, size)]


def forward_body(parts, kinds, taps, decay, spread, gain, skip, query, key, value, long_out, gated, feats, signal, summed):
    length, width = query.shape
    blocks = row_blocks(length)
    for j in range(3):
        feats[j, :MARGIN, :] = jnp.zeros((MARGIN, width), F32)
        for start, size in blocks:
            total = kinds(parts, j, pl.ds(start, size))
            feats[j, MARGIN + start : MARGIN + start + size, :] = total.astype(BF16).astype(F32)
    for start, size in blocks:
        mixed = []
        for j in range(3):
            total = taps[j, 0:1, :] * feats[j, MARGIN + start : MARGIN + start + size, :]
            for lag in range(1, taps.shape[1]):
                first = MARGIN + start - lag
                total = total + taps[j, lag : lag + 1, :] * feats[j, first : first + size, :]
            mixed.append(total)
        at = slice(start, start + size)
        query[at, :], key[at, :], value[at, :] = mixed
        signal[at, :] = mixed[1] * mixed[2]
    modal_scan(signal, summed, decay[...], spread[...], gain[...], False)
    for start, size in blocks:
        at = slice(start, start + size)
        result = summed[at, :] + skip[...] * signal[at, :]
        long_out[at, :] = result
        gated[at, :] = (query[at, :] * result).astype(BF16)


def backward_body(parts, kinds, taps, decay, spread, gain, skip, query, key, value, long_out, grads, mixin, grad_long, summed):
    length, width = query.shape
    blocks = row_blocks(length)
    for start, size in blocks:
        at = slice(start, start + size)
        grad_gated = kinds(parts, 0, pl.ds(start, size))
        mixin[0, at, :] = grad_gated * long_out[at, :]
        grad_long[at, :] = grad_gated * query[at, :]
    modal_scan(grad_long, summed, decay[...], spread[...], gain[...], True)
    for start, size in blocks:
        at = slice(start, start + size)
        grad_signal = summed[at, :] + skip[...] * grad_long[at, :]
        mixin[1, at, :] = grad_signal * value[at, :]
        mixin[2, at, :] = grad_signal * key[at, :]
    for j in range(3):
        mixin[j, length : length + MARGIN, :] = jnp.zeros((MARGIN, width), F32)
        for start, size in blocks:
            total = taps[j, 0:1, :] * mixin[j, start : start + size, :]
            for lag in range(1, taps.shape[1]):
                total = total + taps[j, lag : lag + 1, :] * mixin[j, start + lag : start + lag + size, :]
            grads[j, start : start + size, :] = total.astype(BF16)


def sum_of_three(parts, j, at):
    own, near, far = parts
    return own[j, at, :] + near[j, at, :].astype(F32) + far[j, at, :].astype(F32)


def plain(parts, j, at):
    return parts[0][j, at, :].astype(F32)


def filter_forward(parts, kinds, tables, length, width):
    count = len(parts)

    def body(*refs):
        forward_body(refs[:count], kinds, *refs[count:])

    wide = jax.ShapeDtypeStruct((length, width), F32)
    return call(
        body,
        (wide, wide, wide, wide, jax.ShapeDtypeStruct((length, width), BF16)),
        [
            pltpu.VMEM((3, MARGIN + length, width), F32),
            pltpu.VMEM((length, width), F32),
            pltpu.VMEM((length, width), F32),
        ],
        flops=200 * length * width,
        nbytes=40 * length * width,
    )(*parts, *tables)


def filter_backward(parts, kinds, tables, saved, length, width):
    count = len(parts)

    def body(*refs):
        backward_body(refs[:count], kinds, *refs[count:])

    return call(
        body,
        jax.ShapeDtypeStruct((3, length, width), BF16),
        [
            pltpu.VMEM((3, length + MARGIN, width), F32),
            pltpu.VMEM((length, width), F32),
            pltpu.VMEM((length, width), F32),
        ],
        flops=200 * length * width,
        nbytes=40 * length * width,
    )(*parts, *tables, *saved)


HBM = pl.BlockSpec(memory_space=pl.ANY)


def own_columns(rows):
    me = lax.axis_index("ctx")
    side = lax.axis_index("fsdp") & 1
    width = rows.shape[1] // 4
    part = lambda mask: lax.dynamic_slice_in_dim(rows, (me ^ mask) * width, width, 1)
    pairs = [(4 * f + k, 4 * f + (k ^ 2 ^ (f & 1))) for f in range(8) for k in range(4)]
    fetched = lax.ppermute(part(2 ^ side), ("fsdp", "ctx"), pairs)
    return part(0), flipped(part(1), "ctx", 1), fetched, flipped(fetched, "fsdp", 1)


def project(pieces, weight, after=()):
    groups, depth, channels = weight.shape
    part = pieces[0].shape[0]
    length = 4 * part
    width = channels // 4

    def body(a, b, c, d, weight, *refs):
        held, own, far, give, give_far, product = refs[len(after) :]
        me = lax.axis_index("ctx")
        side = lax.axis_index("fsdp") & 1
        for mask, piece in ((0, a), (1, b), (2 ^ side, c), (3 ^ side, d)):
            held[block_at(me ^ mask, part), :] = piece[...]
        for j in range(groups):
            product[...] = dot(held[...], weight[j], (1, 0))
            own[j] = product[:, block_at(me, width)]
            far[j] = product[:, block_at(me ^ 2, width)].astype(BF16)
            give[j] = product[:, block_at(me ^ 1, width)].astype(BF16)
            give_far[j] = product[:, block_at(me ^ 3, width)].astype(BF16)

    sums = jax.ShapeDtypeStruct((groups, length, width), BF16)
    return call(
        body,
        (
            jax.ShapeDtypeStruct((length, depth), BF16),
            jax.ShapeDtypeStruct((groups, length, width), F32),
            sums,
            sums,
            sums,
        ),
        [pltpu.VMEM((length, channels), F32)],
        in_specs=[VMEM] * 5 + [HBM] * len(after),
    )(*pieces, weight, *after)


def add_pair(left, right, after):
    def body(left, right, *refs):
        refs[-1][...] = (left[...].astype(F32) + right[...].astype(F32)).astype(BF16)

    return call(body, jax.ShapeDtypeStruct(left.shape, BF16), in_specs=[VMEM] * 2 + [HBM] * len(after))(
        left, right, *after
    )


def channel_sums(projected, after=()):
    own, far, give, give_far = projected
    passed = add_pair(far, flipped(give_far, "ctx", 1), after)
    return own, flipped(give, "ctx", 1), flipped(passed, "ctx", 2)


def all_channels(value):
    far = flipped(value, "ctx", 2)
    return value, far, flipped(value, "ctx", 1), flipped(far, "ctx", 1)


def output_halves(gathered, weight, after=()):
    groups, length, width = gathered[0].shape
    depth = weight.shape[1]
    piece = depth // 4
    channels = 4 * width
    side = lambda: lax.axis_index("fsdp") & 1

    def product(whole, weight, index):
        total = None
        for j in range(groups):
            term = dot(whole[j], weight[j, block_at(index, piece), :], (1, 1))
            total = term if total is None else total + term
        return total.astype(BF16)

    def first_body(own, far, near, near_far, weight, *refs):
        whole, give = refs[len(after) :]
        me = lax.axis_index("ctx")
        for j in range(groups):
            for mask, value in ((0, own), (2, far), (1, near), (3, near_far)):
                whole[j, :, block_at(me ^ mask, width)] = value[j]
        give[...] = product(whole, weight, 2 - 2 * side())

    def second_body(whole, weight, give, keep, keep_second):
        give[...] = product(whole, weight, 3 - 2 * side())
        keep[...] = product(whole, weight, 2 * side())
        keep_second[...] = product(whole, weight, 2 * side() + 1)

    part = jax.ShapeDtypeStruct((length, piece), BF16)
    whole, give = call(
        first_body,
        (jax.ShapeDtypeStruct((groups, length, channels), BF16), part),
        in_specs=[VMEM] * 5 + [HBM] * len(after),
    )(*gathered, weight, *after)
    give_second, keep, keep_second = call(second_body, (part,) * 3)(whole, weight)
    return whole, (keep, keep_second), (give, give_second)


def split_sum(keep, given, after=()):
    length, width = keep.shape
    part = length // 4

    def body(keep, given, *refs):
        place = lax.axis_index("fsdp") >> 1
        for mask, out in enumerate(refs[len(after) :]):
            at = block_at(place ^ mask, part)
            out[...] = (keep[at, :].astype(F32) + given[at, :].astype(F32)).astype(BF16)

    return call(
        body, (jax.ShapeDtypeStruct((part, width), BF16),) * 4, in_specs=[VMEM] * 2 + [HBM] * len(after)
    )(keep, given, *after)


def placed(block, mask):
    pairs = []
    for f in range(8):
        for k in range(4):
            z, x = f // 2, f % 2
            pairs.append((4 * f + k, 4 * (2 * k + x) + (z ^ mask)))
    return lax.ppermute(block, ("fsdp", "ctx"), pairs)


def join(quarters):
    part, width = quarters[0][0].shape

    def body(*refs):
        out = refs[-1]
        for half in range(2):
            total = refs[4 * half][...].astype(F32)
            for ref in refs[4 * half + 1 : 4 * half + 4]:
                total = total + ref[...].astype(F32)
            out[:, half * width : (half + 1) * width] = total.astype(BF16)

    return call(body, jax.ShapeDtypeStruct((part, 2 * width), BF16))(*quarters[0], *quarters[1])


def block_sums(keeps, givens):
    quarters = []
    for keep, given in zip(keeps, givens):
        blocks = split_sum(keep, given)
        quarters.append([placed(block, mask) for mask, block in enumerate(blocks)])
    return join(quarters)


def weight_gradient(rows, values):
    length, depth = rows.shape
    groups, _, channels = values.shape
    tile = 256

    def body(rows, values, out):
        out[0] = dot(rows[...], values[0], (0, 0))

    return pl.pallas_call(
        body,
        out_shape=jax.ShapeDtypeStruct((groups, depth, channels), F32),
        grid=(groups, depth // tile),
        in_specs=[
            pl.BlockSpec((length, tile), lambda j, i: (0, i)),
            pl.BlockSpec((1, length, channels), lambda j, i: (j, 0, 0)),
        ],
        out_specs=pl.BlockSpec((1, tile, channels), lambda j, i: (j, i, 0)),
        compiler_params=pltpu.CompilerParams(vmem_limit_bytes=VMEM_LIMIT),
        cost_estimate=pl.CostEstimate(
            flops=2 * length * depth * channels * groups,
            bytes_accessed=4 * groups * depth * channels,
            transcendentals=0,
        ),
    )(rows, values)


def four_by_eight(tokens, weights, tables, out_weight, grad_mixed):
    length, width = 4 * tokens.shape[0], weights.shape[2] // 4
    token_pieces = own_columns(tokens)
    grad_pieces = own_columns(grad_mixed)
    whole_tokens, *projected = project(token_pieces, weights, grad_pieces[2:3])
    feats = channel_sums(projected, grad_pieces[3:])
    whole_cotangents, *projected = project(grad_pieces, out_weight[None])
    grad_gated = channel_sums(projected)
    *saved, gated = filter_forward(feats, sum_of_three, tables, length, width)
    whole_gated, keeps, gives = output_halves(all_channels(gated[None]), out_weight[None])
    givens = [flipped(give, "fsdp", 1) for give in gives]
    mixed = block_sums(keeps, givens)
    grads = filter_backward(grad_gated, sum_of_three, tables, saved, length, width)
    whole_grads, keeps, gives = output_halves(all_channels(grads), weights, givens[:1])
    grad_tokens = block_sums(keeps, [flipped(give, "fsdp", 1) for give in gives])
    grad_in = weight_gradient(whole_tokens, whole_grads)
    grad_out = weight_gradient(whole_cotangents, whole_gated)[0]
    return mixed, grad_tokens, grad_in, grad_out


def to_placement(value):
    count = lax.axis_size("ctx")
    ratio = lax.axis_size("fsdp") // count
    pairs = []
    for f in range(ratio * count):
        for k in range(count):
            target = (k * ratio + f % ratio, f // ratio)
            pairs.append((f * count + k, target[0] * count + target[1]))
    return lax.ppermute(value, ("fsdp", "ctx"), pairs)


def any_mesh(tokens, weights, tables, out_weight, grad_mixed):
    count = lax.axis_size("ctx")
    columns = lambda rows: lax.all_to_all(rows, "ctx", split_axis=1, concat_axis=0, tiled=True)
    whole_tokens, whole_cotangents = columns(tokens), columns(grad_mixed)
    length, width = whole_tokens.shape[0], weights.shape[2] // count

    def channel_sums(rows, weight):
        partial = jnp.einsum("td,jdc->jtc", rows, weight, preferred_element_type=F32)
        return lax.psum_scatter(partial.astype(BF16), "ctx", scatter_dimension=2, tiled=True)

    def block_sums(values, weight):
        partial = jnp.einsum("jtc,jdc->td", values, weight, preferred_element_type=F32)
        ratio = lax.axis_size("fsdp") // count
        pieces = partial.astype(BF16).reshape(count, length // count, ratio, -1).transpose(0, 2, 1, 3)
        pieces = pieces.reshape(count * ratio, length // count, -1)
        return to_placement(lax.psum_scatter(pieces, "fsdp", scatter_dimension=0, tiled=True)[0])

    feats = channel_sums(whole_tokens, weights)
    grad_gated = channel_sums(whole_cotangents, out_weight[None])
    *saved, gated = filter_forward((feats,), plain, tables, length, width)
    grads = filter_backward((grad_gated,), plain, tables, saved, length, width)
    whole_gated = lax.all_gather(gated, "ctx", axis=1, tiled=True)
    whole_grads = lax.all_gather(grads, "ctx", axis=2, tiled=True)
    mixed = block_sums(whole_gated[None], out_weight[None])
    grad_tokens = block_sums(whole_grads, weights)
    grad_in = jnp.einsum("td,jtc->jdc", whole_tokens, whole_grads, preferred_element_type=F32)
    grad_out = jnp.einsum("td,tc->dc", whole_cotangents, whole_gated, preferred_element_type=F32)
    return mixed, grad_tokens, grad_in, grad_out


def per_device(tokens, in_weight, conv_taps, decay_rate, residue, skip_gain, out_weight, grad_mixed):
    count, blocks = lax.axis_size("ctx"), lax.axis_size("fsdp")
    weights = in_weight.transpose(1, 0, 2)
    length = count * tokens.shape[0]
    width = weights.shape[2] // count
    mine = lambda table: lax.dynamic_slice_in_dim(table, lax.axis_index("ctx") * width, width, table.ndim - 1)
    rate = mine(decay_rate)
    gain = mine(residue) * jnp.sqrt(-jnp.expm1(-2.0 * rate))
    tables = (mine(conv_taps.transpose(1, 0, 2)), jnp.exp(-rate), jnp.exp(-rate * (length // CHUNKS)), gain, mine(skip_gain[None]))
    tuned = count == 4 and blocks == 8 and width % LANES == 0
    plan = four_by_eight if tuned else any_mesh
    mixed, grad_tokens, grad_in, grad_out = plan(tokens, weights, tables, out_weight, grad_mixed)
    return mixed, grad_tokens, grad_in.transpose(1, 0, 2), grad_out


def solution(mesh):
    return jax.shard_map(
        per_device,
        mesh=mesh,
        in_specs=(
            P("ctx", None),
            P("ctx", None, "fsdp"),
            P(None, None, "fsdp"),
            P(None, "fsdp"),
            P(None, "fsdp"),
            P("fsdp"),
            P("ctx", "fsdp"),
            P("ctx", None),
        ),
        out_specs=(P("ctx", "fsdp"), P("ctx", "fsdp"), P("ctx", None, "fsdp"), P("ctx", "fsdp")),
        check_vma=False,
    )
```

```python
import functools

import jax
import jax.numpy as jnp
from jax import lax
from jax.experimental import pallas as pl
from jax.experimental.pallas import tpu as pltpu
from jax.sharding import PartitionSpec as P

BF16 = jnp.bfloat16
F32 = jnp.float32
LANES = 128
CHUNKS = 8
MARGIN = 8
VMEM_LIMIT = 16 * 1024 * 1024


VMEM = pl.BlockSpec(memory_space=pltpu.VMEM)
HBM = pl.BlockSpec(memory_space=pl.ANY)


def call(body, outs, scratch=(), in_specs=None, flops=0, nbytes=0):
    return pl.pallas_call(
        body,
        out_shape=outs,
        **({} if in_specs is None else {"in_specs": in_specs}),
        scratch_shapes=list(scratch),
        compiler_params=pltpu.CompilerParams(vmem_limit_bytes=VMEM_LIMIT),
        cost_estimate=pl.CostEstimate(flops=flops, bytes_accessed=nbytes, transcendentals=0),
    )


def flipped(value, axis, mask):
    count = lax.axis_size(axis)
    return lax.ppermute(value, axis, [(source, source ^ mask) for source in range(count)])


def block_at(index, size):
    return pl.ds(pl.multiple_of(index * size, size), size)


def to_placement(value):
    count = lax.axis_size("ctx")
    ratio = lax.axis_size("fsdp") // count
    pairs = []
    for f in range(ratio * count):
        for k in range(count):
            target = (k * ratio + f % ratio, f // ratio)
            pairs.append((f * count + k, target[0] * count + target[1]))
    return lax.ppermute(value, ("fsdp", "ctx"), pairs)


def dot(left, right, contract):
    return lax.dot_general(left, right, ((contract[:1], contract[1:]), ((), ())), preferred_element_type=F32)


def shifted(value, steps, backward):
    rows = lax.broadcasted_iota(jnp.int32, value.shape, 0)
    if backward:
        return jnp.where(rows < CHUNKS - steps, pltpu.roll(value, CHUNKS - steps, 0), 0.0)
    return jnp.where(rows >= steps, pltpu.roll(value, steps, 0), 0.0)


def modal_scan(source, target, decay, spread, gain, backward):
    poles, width = decay.shape
    steps = source.shape[0] // CHUNKS
    wide = lambda table, n: jnp.broadcast_to(table[n : n + 1, :], (CHUNKS, width))
    decays = [wide(decay, n) for n in range(poles)]

    def rows(i):
        return pl.ds(steps - 1 - i if backward else i, CHUNKS, stride=steps)

    def gather_up(i, states):
        entry = source[rows(i), :]
        return tuple(d * s + entry for d, s in zip(decays, states))

    zero = jnp.zeros((CHUNKS, width), F32)
    ends = lax.fori_loop(0, steps, gather_up, (zero,) * poles, unroll=4)
    states = []
    for n in range(poles):
        factor = wide(spread, n)
        state = shifted(ends[n], 1, backward)
        reach = 1
        while reach < CHUNKS:
            state = state + factor * shifted(state, reach, backward)
            factor = factor * factor
            reach *= 2
        states.append(state)
    gains = [wide(gain, n) for n in range(poles)]

    def advance(i, states):
        entry = source[rows(i), :]
        states = tuple(d * s + entry for d, s in zip(decays, states))
        terms = [g * s for g, s in zip(gains, states)]
        while len(terms) > 1:
            terms = [a + b for a, b in zip(terms[::2], terms[1::2])]
        target[rows(i), :] = terms[0]
        return states

    lax.fori_loop(0, steps, advance, tuple(states), unroll=2)


def row_blocks(length):
    size = 64 if length % 64 == 0 else length
    return [(start, size) for start in range(0, length, size)]


def forward_body(parts, kinds, taps, decay, spread, gain, skip, query, key, value, long_out, gated, feats, signal, summed):
    length, width = query.shape
    blocks = row_blocks(length)
    for j in range(3):
        feats[j, :MARGIN, :] = jnp.zeros((MARGIN, width), F32)
        for start, size in blocks:
            total = kinds(parts, j, pl.ds(start, size))
            feats[j, MARGIN + start : MARGIN + start + size, :] = total.astype(BF16).astype(F32)
    for start, size in blocks:
        mixed = []
        for j in range(3):
            total = taps[j, 0:1, :] * feats[j, MARGIN + start : MARGIN + start + size, :]
            for lag in range(1, taps.shape[1]):
                first = MARGIN + start - lag
                total = total + taps[j, lag : lag + 1, :] * feats[j, first : first + size, :]
            mixed.append(total)
        at = slice(start, start + size)
        query[at, :], key[at, :], value[at, :] = mixed
        signal[at, :] = mixed[1] * mixed[2]
    modal_scan(signal, summed, decay[...], spread[...], gain[...], False)
    for start, size in blocks:
        at = slice(start, start + size)
        result = summed[at, :] + skip[...] * signal[at, :]
        long_out[at, :] = result
        gated[at, :] = (query[at, :] * result).astype(BF16)


def backward_body(parts, kinds, taps, decay, spread, gain, skip, query, key, value, long_out, grads, mixin, grad_long, summed):
    length, width = query.shape
    blocks = row_blocks(length)
    for start, size in blocks:
        at = slice(start, start + size)
        grad_gated = kinds(parts, 0, pl.ds(start, size))
        mixin[0, at, :] = grad_gated * long_out[at, :]
        grad_long[at, :] = grad_gated * query[at, :]
    modal_scan(grad_long, summed, decay[...], spread[...], gain[...], True)
    for start, size in blocks:
        at = slice(start, start + size)
        grad_signal = summed[at, :] + skip[...] * grad_long[at, :]
        mixin[1, at, :] = grad_signal * value[at, :]
        mixin[2, at, :] = grad_signal * key[at, :]
    for j in range(3):
        mixin[j, length : length + MARGIN, :] = jnp.zeros((MARGIN, width), F32)
        for start, size in blocks:
            total = taps[j, 0:1, :] * mixin[j, start : start + size, :]
            for lag in range(1, taps.shape[1]):
                total = total + taps[j, lag : lag + 1, :] * mixin[j, start + lag : start + lag + size, :]
            grads[j, start : start + size, :] = total.astype(BF16)


def sum_of_three(parts, j, at):
    own, near, far = parts
    return own[j, at, :] + near[j, at, :].astype(F32) + far[j, at, :].astype(F32)


def plain(parts, j, at):
    return parts[0][j, at, :].astype(F32)


def filter_forward(parts, kinds, tables, length, width):
    count = len(parts)

    def body(*refs):
        forward_body(refs[:count], kinds, *refs[count:])

    wide = jax.ShapeDtypeStruct((length, width), F32)
    return call(
        body,
        (wide, wide, wide, wide, jax.ShapeDtypeStruct((length, width), BF16)),
        [
            pltpu.VMEM((3, MARGIN + length, width), F32),
            pltpu.VMEM((length, width), F32),
            pltpu.VMEM((length, width), F32),
        ],
    )(*parts, *tables)


def filter_backward(parts, kinds, tables, saved, length, width, after=()):
    count = len(parts)
    inputs = count + len(tables) + len(saved)

    def body(*refs):
        backward_body(refs[:count], kinds, *refs[count:inputs], *refs[inputs + len(after) :])

    return call(
        body,
        jax.ShapeDtypeStruct((3, length, width), BF16),
        [
            pltpu.VMEM((3, length + MARGIN, width), F32),
            pltpu.VMEM((length, width), F32),
            pltpu.VMEM((length, width), F32),
        ],
        in_specs=[VMEM] * inputs + [HBM] * len(after),
    )(*parts, *tables, *saved, *after)


def later(value, after):
    def body(value, after, out):
        pass

    return pl.pallas_call(
        body,
        out_shape=jax.ShapeDtypeStruct(value.shape, value.dtype),
        in_specs=[HBM, HBM],
        out_specs=HBM,
        input_output_aliases={0: 0},
    )(value, after)


def own_columns(rows, after=None):
    me = lax.axis_index("ctx")
    side = lax.axis_index("fsdp") & 1
    width = rows.shape[1] // 4
    part = lambda mask: lax.dynamic_slice_in_dim(rows, (me ^ mask) * width, width, 1)
    pairs = [(4 * f + k, 4 * f + (k ^ 2 ^ (f & 1))) for f in range(8) for k in range(4)]
    fetch = part(2 ^ side) if after is None else later(part(2 ^ side), after)
    fetched = lax.ppermute(fetch, ("fsdp", "ctx"), pairs)
    return part(0), flipped(part(1), "ctx", 1), fetched, flipped(fetched, "fsdp", 1)


def project(pieces, weight, after=()):
    groups, depth, channels = weight.shape
    part = pieces[0].shape[0]
    length = 4 * part
    width = channels // 4

    def body(a, b, c, d, weight, *refs):
        held, own, far, give, give_far, product = refs[len(after) :]
        me = lax.axis_index("ctx")
        side = lax.axis_index("fsdp") & 1
        for mask, piece in ((0, a), (1, b), (2 ^ side, c), (3 ^ side, d)):
            held[block_at(me ^ mask, part), :] = piece[...]
        for j in range(groups):
            product[...] = dot(held[...], weight[j], (1, 0))
            own[j] = product[:, block_at(me, width)]
            far[j] = product[:, block_at(me ^ 2, width)].astype(BF16)
            give[j] = product[:, block_at(me ^ 1, width)].astype(BF16)
            give_far[j] = product[:, block_at(me ^ 3, width)].astype(BF16)

    sums = jax.ShapeDtypeStruct((groups, length, width), BF16)
    return call(
        body,
        (
            jax.ShapeDtypeStruct((length, depth), BF16),
            jax.ShapeDtypeStruct((groups, length, width), F32),
            sums,
            sums,
            sums,
        ),
        [pltpu.VMEM((length, channels), F32)],
        in_specs=[VMEM] * 5 + [HBM] * len(after),
    )(*pieces, weight, *after)


def add_pair(left, right, after):
    def body(left, right, *refs):
        refs[-1][...] = (left[...].astype(F32) + right[...].astype(F32)).astype(BF16)

    return call(body, jax.ShapeDtypeStruct(left.shape, BF16), in_specs=[VMEM] * 2 + [HBM] * len(after))(
        left, right, *after
    )


def channel_sums(projected, after=()):
    own, far, give, give_far = projected
    passed = add_pair(far, flipped(give_far, "ctx", 1), after)
    return own, flipped(give, "ctx", 1), flipped(passed, "ctx", 2)


def all_channels(value):
    far = flipped(value, "ctx", 2)
    return value, far, flipped(value, "ctx", 1), flipped(far, "ctx", 1)


def output_pieces(gathered, weight, after=()):
    groups, length, width = gathered[0].shape
    piece = weight.shape[1] // 4
    part = length // 4
    channels = 4 * width

    def product(whole, weight, at, index):
        total = None
        for j in range(groups):
            term = dot(whole[j, at, :], weight[j, block_at(index, piece), :], (1, 1))
            total = term if total is None else total + term
        return total.astype(BF16)

    def pieces(whole, weight, side, low, first, second):
        first[...] = product(whole, weight, slice(None), 2 * side)
        for high in range(2):
            rows = slice(high * part, (high + 1) * part)
            for s in range(2):
                columns = slice(s * piece, (s + 1) * piece)
                second[rows, columns] = product(whole, weight, block_at(2 * high + low, part), 2 * s + 1)

    def first_body(own, far, near, near_far, weight, *refs):
        whole, first, second = refs[len(after) :]
        me = lax.axis_index("ctx")
        place = lax.axis_index("fsdp")
        for j in range(groups):
            for mask, value in ((0, own), (2, far), (1, near), (3, near_far)):
                whole[j, :, block_at(me ^ mask, width)] = value[j]
        pieces(whole, weight, 1 - (place & 1), 1 - ((place >> 1) & 1), first, second)

    def second_body(whole, weight, first, second):
        place = lax.axis_index("fsdp")
        pieces(whole, weight, place & 1, (place >> 1) & 1, first, second)

    parts = (jax.ShapeDtypeStruct((length, piece), BF16), jax.ShapeDtypeStruct((2 * part, 2 * piece), BF16))
    whole, *gives = call(
        first_body,
        (jax.ShapeDtypeStruct((groups, length, channels), BF16), *parts),
        in_specs=[VMEM] * 5 + [HBM] * len(after),
    )(*gathered, weight, *after)
    keeps = call(second_body, parts)(whole, weight)
    return whole, keeps, gives


def exchange(gives):
    return flipped(gives[0], "fsdp", 1), flipped(gives[1], "fsdp", 2)


def block_sums(keeps, givens):
    length, piece = keeps[0].shape
    part = length // 4
    both = lambda keep, given, rows, columns: keep[rows, columns].astype(F32) + given[rows, columns].astype(F32)

    def second_body(keep_x, given_x, keep_z, given_z, give_z, give_x, next_z, next_x):
        place = lax.axis_index("fsdp")
        side, low = place & 1, (place >> 1) & 1
        for high in range(2):
            rows = slice(high * part, (high + 1) * part)
            take = lambda bit: both(keep_x, given_x, block_at(2 * high + bit, part), slice(None))
            give_z[rows, :] = take(1 - low).astype(BF16)
            next_z[rows, :] = take(low)
        take = lambda bit: both(keep_z, given_z, slice(None), block_at(bit, piece))
        give_x[...] = take(1 - side).astype(BF16)
        next_x[...] = take(side)

    square = lambda kind: jax.ShapeDtypeStruct((2 * part, piece), kind)
    give_z, give_x, next_z, next_x = call(second_body, (square(BF16), square(BF16), square(F32), square(F32)))(
        keeps[0], givens[0], keeps[1], givens[1]
    )

    def third_body(keep_z, given_z, keep_x, given_x, give, keep):
        high = lax.axis_index("fsdp") >> 2
        for bit, out in ((1 - high, give), (high, keep)):
            at = block_at(bit, part)
            for half, (mine, other) in enumerate(((keep_z, given_z), (keep_x, given_x))):
                columns = slice(half * piece, (half + 1) * piece)
                out[:, columns] = both(mine, other, at, slice(None)).astype(out.dtype)

    block = lambda kind: jax.ShapeDtypeStruct((part, 2 * piece), kind)
    give, keep = call(third_body, (block(BF16), block(F32)))(
        next_z, flipped(give_z, "fsdp", 2), next_x, flipped(give_x, "fsdp", 1)
    )

    def last_body(keep, given, out):
        out[...] = (keep[...] + given[...].astype(F32)).astype(BF16)

    return to_placement(call(last_body, block(BF16))(keep, flipped(give, "fsdp", 4)))


def weight_gradient(rows, values):
    length, depth = rows.shape
    groups, _, channels = values.shape
    tile = 256

    def body(rows, values, out):
        out[0] = dot(rows[...], values[0], (0, 0))

    return pl.pallas_call(
        body,
        out_shape=jax.ShapeDtypeStruct((groups, depth, channels), F32),
        grid=(groups, depth // tile),
        in_specs=[
            pl.BlockSpec((length, tile), lambda j, i: (0, i)),
            pl.BlockSpec((1, length, channels), lambda j, i: (j, 0, 0)),
        ],
        out_specs=pl.BlockSpec((1, tile, channels), lambda j, i: (j, i, 0)),
        compiler_params=pltpu.CompilerParams(vmem_limit_bytes=VMEM_LIMIT),
        cost_estimate=pl.CostEstimate(
            flops=2 * length * depth * channels * groups,
            bytes_accessed=4 * groups * depth * channels,
            transcendentals=0,
        ),
    )(rows, values)


def four_by_eight(tokens, weights, tables, out_weight, grad_mixed):
    length, width = 4 * tokens.shape[0], weights.shape[2] // 4
    token_pieces = own_columns(tokens)
    grad_pieces = own_columns(grad_mixed, token_pieces[2])
    whole_tokens, *projected = project(token_pieces, weights, grad_pieces[2:3])
    feats = channel_sums(projected)
    whole_cotangents, *projected = project(grad_pieces, out_weight[None])
    grad_gated = channel_sums(projected)
    *saved, gated = filter_forward(feats, sum_of_three, tables, length, width)
    all_gated = all_channels(gated[None])
    whole_gated, keeps, gives = output_pieces(all_gated, out_weight[None])
    givens = exchange(gives)
    mixed = block_sums(keeps, givens)
    grads = filter_backward(grad_gated, sum_of_three, tables, saved, length, width, all_gated[1:2])
    whole_grads, keeps, gives = output_pieces(all_channels(grads), weights, givens)
    grad_tokens = block_sums(keeps, exchange(gives))
    grad_in = weight_gradient(whole_tokens, whole_grads)
    grad_out = weight_gradient(whole_cotangents, whole_gated)[0]
    return mixed, grad_tokens, grad_in, grad_out


def any_mesh(tokens, weights, tables, out_weight, grad_mixed):
    count = lax.axis_size("ctx")
    columns = lambda rows: lax.all_to_all(rows, "ctx", split_axis=1, concat_axis=0, tiled=True)
    whole_tokens, whole_cotangents = columns(tokens), columns(grad_mixed)
    length, width = whole_tokens.shape[0], weights.shape[2] // count

    def channel_sums(rows, weight):
        partial = jnp.einsum("td,jdc->jtc", rows, weight, preferred_element_type=F32)
        return lax.psum_scatter(partial.astype(BF16), "ctx", scatter_dimension=2, tiled=True)

    def block_sums(values, weight):
        partial = jnp.einsum("jtc,jdc->td", values, weight, preferred_element_type=F32)
        ratio = lax.axis_size("fsdp") // count
        pieces = partial.astype(BF16).reshape(count, length // count, ratio, -1).transpose(0, 2, 1, 3)
        pieces = pieces.reshape(count * ratio, length // count, -1)
        return to_placement(lax.psum_scatter(pieces, "fsdp", scatter_dimension=0, tiled=True)[0])

    feats = channel_sums(whole_tokens, weights)
    grad_gated = channel_sums(whole_cotangents, out_weight[None])
    *saved, gated = filter_forward((feats,), plain, tables, length, width)
    grads = filter_backward((grad_gated,), plain, tables, saved, length, width)
    whole_gated = lax.all_gather(gated, "ctx", axis=1, tiled=True)
    whole_grads = lax.all_gather(grads, "ctx", axis=2, tiled=True)
    mixed = block_sums(whole_gated[None], out_weight[None])
    grad_tokens = block_sums(whole_grads, weights)
    grad_in = jnp.einsum("td,jtc->jdc", whole_tokens, whole_grads, preferred_element_type=F32)
    grad_out = jnp.einsum("td,tc->dc", whole_cotangents, whole_gated, preferred_element_type=F32)
    return mixed, grad_tokens, grad_in, grad_out


def per_device(tokens, in_weight, conv_taps, decay_rate, residue, skip_gain, out_weight, grad_mixed):
    count, blocks = lax.axis_size("ctx"), lax.axis_size("fsdp")
    weights = in_weight.transpose(1, 0, 2)
    length = count * tokens.shape[0]
    width = weights.shape[2] // count
    mine = lambda table: lax.dynamic_slice_in_dim(table, lax.axis_index("ctx") * width, width, table.ndim - 1)
    rate = mine(decay_rate)
    gain = mine(residue) * jnp.sqrt(-jnp.expm1(-2.0 * rate))
    tables = (mine(conv_taps.transpose(1, 0, 2)), jnp.exp(-rate), jnp.exp(-rate * (length // CHUNKS)), gain, mine(skip_gain[None]))
    tuned = count == 4 and blocks == 8 and width % LANES == 0
    plan = four_by_eight if tuned else any_mesh
    mixed, grad_tokens, grad_in, grad_out = plan(tokens, weights, tables, out_weight, grad_mixed)
    return mixed, grad_tokens, grad_in.transpose(1, 0, 2), grad_out


def solution(mesh):
    return jax.shard_map(
        per_device,
        mesh=mesh,
        in_specs=(
            P("ctx", None),
            P("ctx", None, "fsdp"),
            P(None, None, "fsdp"),
            P(None, "fsdp"),
            P(None, "fsdp"),
            P("fsdp"),
            P("ctx", "fsdp"),
            P("ctx", None),
        ),
        out_specs=(P("ctx", "fsdp"), P("ctx", "fsdp"), P("ctx", None, "fsdp"), P("ctx", "fsdp")),
        check_vma=False,
    )
```

```python
import functools

import jax
import jax.numpy as jnp
from jax import lax
from jax.experimental import pallas as pl
from jax.experimental.pallas import tpu as pltpu
from jax.sharding import PartitionSpec as P

BF16 = jnp.bfloat16
F32 = jnp.float32
LANES = 128
CHUNKS = 8
MARGIN = 8
VMEM_LIMIT = 16 * 1024 * 1024
FLOPS_PER_US = 1_150_000_000


VMEM = pl.BlockSpec(memory_space=pltpu.VMEM)
HBM = pl.BlockSpec(memory_space=pl.ANY)


def cost(us):
    return pl.CostEstimate(flops=int(us * FLOPS_PER_US), bytes_accessed=0, transcendentals=0)


def call(body, outs, scratch=(), in_specs=None, us=0.5):
    return pl.pallas_call(
        body,
        out_shape=outs,
        **({} if in_specs is None else {"in_specs": in_specs}),
        scratch_shapes=list(scratch),
        compiler_params=pltpu.CompilerParams(vmem_limit_bytes=VMEM_LIMIT),
        cost_estimate=cost(us),
    )


def flipped(value, axis, mask):
    count = lax.axis_size(axis)
    return lax.ppermute(value, axis, [(source, source ^ mask) for source in range(count)])


def block_at(index, size):
    return pl.ds(pl.multiple_of(index * size, size), size)


def to_placement(value):
    count = lax.axis_size("ctx")
    ratio = lax.axis_size("fsdp") // count
    pairs = []
    for f in range(ratio * count):
        for k in range(count):
            target = (k * ratio + f % ratio, f // ratio)
            pairs.append((f * count + k, target[0] * count + target[1]))
    return lax.ppermute(value, ("fsdp", "ctx"), pairs)


def dot(left, right, contract):
    return lax.dot_general(left, right, ((contract[:1], contract[1:]), ((), ())), preferred_element_type=F32)


def shifted(value, steps, backward):
    rows = lax.broadcasted_iota(jnp.int32, value.shape, 0)
    if backward:
        return jnp.where(rows < CHUNKS - steps, pltpu.roll(value, CHUNKS - steps, 0), 0.0)
    return jnp.where(rows >= steps, pltpu.roll(value, steps, 0), 0.0)


def modal_scan(source, target, decay, spread, gain, backward):
    poles, width = decay.shape
    steps = source.shape[0] // CHUNKS
    wide = lambda table, n: jnp.broadcast_to(table[n : n + 1, :], (CHUNKS, width))
    decays = [wide(decay, n) for n in range(poles)]

    def rows(i):
        return pl.ds(steps - 1 - i if backward else i, CHUNKS, stride=steps)

    def gather_up(i, states):
        entry = source[rows(i), :]
        return tuple(d * s + entry for d, s in zip(decays, states))

    zero = jnp.zeros((CHUNKS, width), F32)
    ends = lax.fori_loop(0, steps, gather_up, (zero,) * poles, unroll=4)
    states = []
    for n in range(poles):
        factor = wide(spread, n)
        state = shifted(ends[n], 1, backward)
        reach = 1
        while reach < CHUNKS:
            state = state + factor * shifted(state, reach, backward)
            factor = factor * factor
            reach *= 2
        states.append(state)
    gains = [wide(gain, n) for n in range(poles)]

    def advance(i, states):
        entry = source[rows(i), :]
        states = tuple(d * s + entry for d, s in zip(decays, states))
        terms = [g * s for g, s in zip(gains, states)]
        while len(terms) > 1:
            terms = [a + b for a, b in zip(terms[::2], terms[1::2])]
        target[rows(i), :] = terms[0]
        return states

    lax.fori_loop(0, steps, advance, tuple(states), unroll=2)


def row_blocks(length):
    size = 64 if length % 64 == 0 else length
    return [(start, size) for start in range(0, length, size)]


def forward_body(parts, kinds, taps, decay, spread, gain, skip, query, key, value, long_out, gated, feats, signal, summed):
    length, width = query.shape
    blocks = row_blocks(length)
    for j in range(3):
        feats[j, :MARGIN, :] = jnp.zeros((MARGIN, width), F32)
        for start, size in blocks:
            row, total = kinds(parts, j, start, size)
            feats[j, pl.ds(MARGIN + row, size), :] = total.astype(BF16).astype(F32)
    for start, size in blocks:
        mixed = []
        for j in range(3):
            total = taps[j, 0:1, :] * feats[j, MARGIN + start : MARGIN + start + size, :]
            for lag in range(1, taps.shape[1]):
                first = MARGIN + start - lag
                total = total + taps[j, lag : lag + 1, :] * feats[j, first : first + size, :]
            mixed.append(total)
        at = slice(start, start + size)
        query[at, :], key[at, :], value[at, :] = mixed
        signal[at, :] = mixed[1] * mixed[2]
    modal_scan(signal, summed, decay[...], spread[...], gain[...], False)
    for start, size in blocks:
        at = slice(start, start + size)
        result = summed[at, :] + skip[...] * signal[at, :]
        long_out[at, :] = result
        gated[at, :] = (query[at, :] * result).astype(BF16)


def backward_body(parts, kinds, taps, decay, spread, gain, skip, query, key, value, long_out, grads, mixin, grad_long, summed):
    length, width = query.shape
    blocks = row_blocks(length)
    for start, size in blocks:
        row, grad_gated = kinds(parts, 0, start, size)
        at = pl.ds(row, size)
        mixin[0, at, :] = grad_gated * long_out[at, :]
        grad_long[at, :] = grad_gated * query[at, :]
    modal_scan(grad_long, summed, decay[...], spread[...], gain[...], True)
    for start, size in blocks:
        at = slice(start, start + size)
        grad_signal = summed[at, :] + skip[...] * grad_long[at, :]
        mixin[1, at, :] = grad_signal * value[at, :]
        mixin[2, at, :] = grad_signal * key[at, :]
    for j in range(3):
        mixin[j, length : length + MARGIN, :] = jnp.zeros((MARGIN, width), F32)
        for start, size in blocks:
            total = taps[j, 0:1, :] * mixin[j, start : start + size, :]
            for lag in range(1, taps.shape[1]):
                total = total + taps[j, lag : lag + 1, :] * mixin[j, start + lag : start + lag + size, :]
            grads[j, start : start + size, :] = total.astype(BF16)


def sum_of_three(parts, j, start, size):
    half = parts[0].shape[1]
    other, local = divmod(start, half)
    own, near, far = parts[3 * other : 3 * other + 3]
    at = slice(local, local + size)
    total = own[j, at, :] + near[j, at, :].astype(F32) + far[j, at, :].astype(F32)
    return pl.multiple_of(((lax.axis_index("ctx") >> 1) ^ other) * half + local, MARGIN), total


def plain(parts, j, start, size):
    return start, parts[0][j, start : start + size, :].astype(F32)


def filter_forward(parts, kinds, tables, length, width):
    count = len(parts)

    def body(*refs):
        forward_body(refs[:count], kinds, *refs[count:])

    wide = jax.ShapeDtypeStruct((length, width), F32)
    return call(
        body,
        (wide, wide, wide, wide, jax.ShapeDtypeStruct((length, width), BF16)),
        [
            pltpu.VMEM((3, MARGIN + length, width), F32),
            pltpu.VMEM((length, width), F32),
            pltpu.VMEM((length, width), F32),
        ],
        us=3.2,
    )(*parts, *tables)


def filter_backward(parts, kinds, tables, saved, length, width, after=()):
    count = len(parts)
    inputs = count + len(tables) + len(saved)

    def body(*refs):
        backward_body(refs[:count], kinds, *refs[count:inputs], *refs[inputs + len(after) :])

    return call(
        body,
        jax.ShapeDtypeStruct((3, length, width), BF16),
        [
            pltpu.VMEM((3, length + MARGIN, width), F32),
            pltpu.VMEM((length, width), F32),
            pltpu.VMEM((length, width), F32),
        ],
        in_specs=[VMEM] * inputs + [HBM] * len(after),
        us=2.1,
    )(*parts, *tables, *saved, *after)


def later(value, after):
    def body(value, after, out):
        pass

    return pl.pallas_call(
        body,
        out_shape=jax.ShapeDtypeStruct(value.shape, value.dtype),
        in_specs=[HBM, HBM],
        out_specs=HBM,
        input_output_aliases={0: 0},
    )(value, after)


def column_blocks(rows):
    length, width = rows.shape[0], rows.shape[1] // 4

    def body(rows, own, near, far, arrived):
        me = lax.axis_index("ctx")
        side = lax.axis_index("fsdp") & 1
        copies = []
        for n, (mask, out) in enumerate(((2 ^ side, far), (1, near), (0, own))):
            copies.append(pltpu.make_async_copy(rows.at[:, block_at(me ^ mask, width)], out, arrived.at[n]))
            copies[-1].start()
        for copy in copies:
            copy.wait()

    block = jax.ShapeDtypeStruct((length, width), rows.dtype)
    return call(body, (block,) * 3, [pltpu.SemaphoreType.DMA((3,))], in_specs=[HBM], us=0.7)(rows)


def fetched(block):
    pairs = [(4 * f + k, 4 * f + (k ^ 2 ^ (f & 1))) for f in range(8) for k in range(4)]
    return lax.ppermute(block, ("fsdp", "ctx"), pairs)


def project(pieces, other, weight):
    groups, depth, channels = weight.shape
    part = pieces[0].shape[0]
    length = 2 * part
    width = channels // 4

    def body(first, second, weight, own, far, give, give_far, held, product):
        me = lax.axis_index("ctx")
        core = (me ^ lax.axis_index("fsdp")) & 1 if other else me & 1
        held[block_at(core, part), :] = first[...]
        held[block_at(1 - core, part), :] = second[...]
        for j in range(groups):
            product[...] = dot(held[...], weight[j], (1, 0))
            own[j] = product[:, block_at(me, width)]
            far[j] = product[:, block_at(me ^ 2, width)].astype(BF16)
            give[j] = product[:, block_at(me ^ 1, width)].astype(BF16)
            give_far[j] = product[:, block_at(me ^ 3, width)].astype(BF16)

    sums = jax.ShapeDtypeStruct((groups, length, width), BF16)
    return call(
        body,
        (jax.ShapeDtypeStruct((groups, length, width), F32), sums, sums, sums),
        [pltpu.VMEM((length, depth), BF16), pltpu.VMEM((length, channels), F32)],
        us=0.7 * groups,
    )(*pieces, weight)


def add_far(left, right):
    def body(left, right, out):
        out[...] = (left[...].astype(F32) + right[...].astype(F32)).astype(BF16)

    return call(body, jax.ShapeDtypeStruct(left.shape, BF16))(left, right)


def channel_sums(pieces, other, weight):
    own, far, give, give_far = project(pieces, other, weight)
    passed = add_far(far, flipped(give_far, "ctx", 1))
    return own, flipped(give, "ctx", 1), flipped(passed, "ctx", 2)


def by_token(here, there):
    return here[0], here[1], there[2], there[0], there[1], here[2]


def all_channels(value, after=None):
    value = value if after is None else later(value, after)
    far = flipped(value, "ctx", 2)
    return value, far, flipped(value, "ctx", 1), flipped(far, "ctx", 1)


def output_pieces(gathered, weight, after=()):
    groups, length, width = gathered[0].shape
    piece = weight.shape[1] // 4
    part = length // 4
    channels = 4 * width

    def product(whole, weight, at, index):
        total = None
        for j in range(groups):
            term = dot(whole[j, at, :], weight[j, block_at(index, piece), :], (1, 1))
            total = term if total is None else total + term
        return total.astype(BF16)

    def pieces(whole, weight, side, low, first, second):
        first[...] = product(whole, weight, slice(None), 2 * side)
        for high in range(2):
            rows = slice(high * part, (high + 1) * part)
            for s in range(2):
                columns = slice(s * piece, (s + 1) * piece)
                second[rows, columns] = product(whole, weight, block_at(2 * high + low, part), 2 * s + 1)

    def first_body(own, far, near, near_far, weight, *refs):
        whole, first, second = refs[len(after) :]
        me = lax.axis_index("ctx")
        place = lax.axis_index("fsdp")
        for j in range(groups):
            for mask, value in ((0, own), (2, far), (1, near), (3, near_far)):
                whole[j, :, block_at(me ^ mask, width)] = value[j]
        pieces(whole, weight, 1 - (place & 1), 1 - ((place >> 1) & 1), first, second)

    def second_body(whole, weight, first, second):
        place = lax.axis_index("fsdp")
        pieces(whole, weight, place & 1, (place >> 1) & 1, first, second)

    parts = (jax.ShapeDtypeStruct((length, piece), BF16), jax.ShapeDtypeStruct((2 * part, 2 * piece), BF16))
    whole, *gives = call(
        first_body,
        (jax.ShapeDtypeStruct((groups, length, channels), BF16), *parts),
        in_specs=[VMEM] * 5 + [HBM] * len(after),
        us=0.6 * groups,
    )(*gathered, weight, *after)
    keeps = call(second_body, parts, us=0.4 * groups)(whole, weight)
    return whole, keeps, gives


def exchange(gives):
    return flipped(gives[0], "fsdp", 1), flipped(gives[1], "fsdp", 2)


def block_sums(keeps, givens):
    length, piece = keeps[0].shape
    part = length // 4
    both = lambda keep, given, rows, columns: keep[rows, columns].astype(F32) + given[rows, columns].astype(F32)

    def second_body(keep_x, given_x, keep_z, given_z, give_z, give_x, next_z, next_x):
        place = lax.axis_index("fsdp")
        side, low = place & 1, (place >> 1) & 1
        for high in range(2):
            rows = slice(high * part, (high + 1) * part)
            take = lambda bit: both(keep_x, given_x, block_at(2 * high + bit, part), slice(None))
            give_z[rows, :] = take(1 - low).astype(BF16)
            next_z[rows, :] = take(low)
        take = lambda bit: both(keep_z, given_z, slice(None), block_at(bit, piece))
        give_x[...] = take(1 - side).astype(BF16)
        next_x[...] = take(side)

    square = lambda kind: jax.ShapeDtypeStruct((2 * part, piece), kind)
    give_z, give_x, next_z, next_x = call(second_body, (square(BF16), square(BF16), square(F32), square(F32)))(
        keeps[0], givens[0], keeps[1], givens[1]
    )

    def third_body(keep_z, given_z, keep_x, given_x, give, keep):
        high = lax.axis_index("fsdp") >> 2
        for bit, out in ((1 - high, give), (high, keep)):
            at = block_at(bit, part)
            for half, (mine, other) in enumerate(((keep_z, given_z), (keep_x, given_x))):
                columns = slice(half * piece, (half + 1) * piece)
                out[:, columns] = both(mine, other, at, slice(None)).astype(out.dtype)

    block = lambda kind: jax.ShapeDtypeStruct((part, 2 * piece), kind)
    give, keep = call(third_body, (block(BF16), block(F32)))(
        next_z, flipped(give_z, "fsdp", 2), next_x, flipped(give_x, "fsdp", 1)
    )

    def last_body(keep, given, out):
        out[...] = (keep[...] + given[...].astype(F32)).astype(BF16)

    return to_placement(call(last_body, block(BF16))(keep, flipped(give, "fsdp", 4)))


def turned(pieces):
    part, depth = pieces[0].shape

    def body(a, b, c, d, out):
        me = lax.axis_index("ctx")
        side = lax.axis_index("fsdp") & 1
        for mask, piece in ((0, a), (1, b), (2 ^ side, c), (3 ^ side, d)):
            out[:, block_at(me ^ mask, part)] = piece[...].T

    return call(body, jax.ShapeDtypeStruct((depth, 4 * part), pieces[0].dtype), us=1.0)(*pieces)


def weight_gradient(rows, values):
    depth, length = rows.shape
    groups, _, channels = values.shape
    tile = depth // 2

    def body(rows, values, out):
        out[0] = dot(rows[...], values[0], (1, 0))

    return pl.pallas_call(
        body,
        out_shape=jax.ShapeDtypeStruct((groups, depth, channels), F32),
        grid=(groups, depth // tile),
        in_specs=[
            pl.BlockSpec((tile, length), lambda j, i: (i, 0)),
            pl.BlockSpec((1, length, channels), lambda j, i: (j, 0, 0)),
        ],
        out_specs=pl.BlockSpec((1, tile, channels), lambda j, i: (j, i, 0)),
        compiler_params=pltpu.CompilerParams(vmem_limit_bytes=VMEM_LIMIT),
        cost_estimate=cost(1.5 * groups),
    )(rows, values)


def four_by_eight(tokens, weights, tables, out_weight, grad_mixed):
    length, width = 4 * tokens.shape[0], weights.shape[2] // 4
    own, near, far = column_blocks(tokens)
    here = (own, flipped(near, "ctx", 1))
    far = fetched(far)
    there = (far, flipped(far, "fsdp", 1))
    feats_here = channel_sums(here, 0, weights)
    grad_own, grad_near, grad_far = column_blocks(grad_mixed)
    grad_here = (grad_own, flipped(grad_near, "ctx", 1))
    grad_far = fetched(later(grad_far, feats_here[2]))
    grad_there = (grad_far, flipped(grad_far, "fsdp", 1))
    feats_there = channel_sums(there, 1, weights)
    grads_here = channel_sums(grad_here, 0, out_weight[None])
    grads_there = channel_sums(grad_there, 1, out_weight[None])
    *saved, gated = filter_forward(by_token(feats_here, feats_there), sum_of_three, tables, length, width)
    all_gated = all_channels(gated[None])
    whole_gated, keeps, gives = output_pieces(all_gated, out_weight[None])
    mixed = block_sums(keeps, exchange(gives))
    grads = filter_backward(by_token(grads_here, grads_there), sum_of_three, tables, saved, length, width)
    whole_grads, keeps, gives = output_pieces(all_channels(grads, all_gated[1]), weights)
    grad_tokens = block_sums(keeps, exchange(gives))
    grad_in = weight_gradient(turned(here + there), whole_grads)
    grad_out = weight_gradient(turned(grad_here + grad_there), whole_gated)[0]
    return mixed, grad_tokens, grad_in, grad_out


def any_mesh(tokens, weights, tables, out_weight, grad_mixed):
    count = lax.axis_size("ctx")
    columns = lambda rows: lax.all_to_all(rows, "ctx", split_axis=1, concat_axis=0, tiled=True)
    whole_tokens, whole_cotangents = columns(tokens), columns(grad_mixed)
    length, width = whole_tokens.shape[0], weights.shape[2] // count

    def channel_sums(rows, weight):
        partial = jnp.einsum("td,jdc->jtc", rows, weight, preferred_element_type=F32)
        return lax.psum_scatter(partial.astype(BF16), "ctx", scatter_dimension=2, tiled=True)

    def block_sums(values, weight):
        partial = jnp.einsum("jtc,jdc->td", values, weight, preferred_element_type=F32)
        ratio = lax.axis_size("fsdp") // count
        pieces = partial.astype(BF16).reshape(count, length // count, ratio, -1).transpose(0, 2, 1, 3)
        pieces = pieces.reshape(count * ratio, length // count, -1)
        return to_placement(lax.psum_scatter(pieces, "fsdp", scatter_dimension=0, tiled=True)[0])

    feats = channel_sums(whole_tokens, weights)
    grad_gated = channel_sums(whole_cotangents, out_weight[None])
    *saved, gated = filter_forward((feats,), plain, tables, length, width)
    grads = filter_backward((grad_gated,), plain, tables, saved, length, width)
    whole_gated = lax.all_gather(gated, "ctx", axis=1, tiled=True)
    whole_grads = lax.all_gather(grads, "ctx", axis=2, tiled=True)
    mixed = block_sums(whole_gated[None], out_weight[None])
    grad_tokens = block_sums(whole_grads, weights)
    grad_in = jnp.einsum("td,jtc->jdc", whole_tokens, whole_grads, preferred_element_type=F32)
    grad_out = jnp.einsum("td,tc->dc", whole_cotangents, whole_gated, preferred_element_type=F32)
    return mixed, grad_tokens, grad_in, grad_out


def per_device(tokens, in_weight, conv_taps, decay_rate, residue, skip_gain, out_weight, grad_mixed):
    count, blocks = lax.axis_size("ctx"), lax.axis_size("fsdp")
    weights = in_weight.transpose(1, 0, 2)
    length = count * tokens.shape[0]
    width = weights.shape[2] // count
    mine = lambda table: lax.dynamic_slice_in_dim(table, lax.axis_index("ctx") * width, width, table.ndim - 1)
    rate = mine(decay_rate)
    gain = mine(residue) * jnp.sqrt(-jnp.expm1(-2.0 * rate))
    tables = (mine(conv_taps.transpose(1, 0, 2)), jnp.exp(-rate), jnp.exp(-rate * (length // CHUNKS)), gain, mine(skip_gain[None]))
    tuned = count == 4 and blocks == 8 and width % LANES == 0 and tokens.shape[0] % LANES == 0
    plan = four_by_eight if tuned else any_mesh
    mixed, grad_tokens, grad_in, grad_out = plan(tokens, weights, tables, out_weight, grad_mixed)
    return mixed, grad_tokens, grad_in.transpose(1, 0, 2), grad_out


def solution(mesh):
    return jax.shard_map(
        per_device,
        mesh=mesh,
        in_specs=(
            P("ctx", None),
            P("ctx", None, "fsdp"),
            P(None, None, "fsdp"),
            P(None, "fsdp"),
            P(None, "fsdp"),
            P("fsdp"),
            P("ctx", "fsdp"),
            P("ctx", None),
        ),
        out_specs=(P("ctx", "fsdp"), P("ctx", "fsdp"), P("ctx", None, "fsdp"), P("ctx", "fsdp")),
        check_vma=False,
    )
```

```python
import functools

import jax
import jax.numpy as jnp
from jax import lax
from jax.experimental import pallas as pl
from jax.experimental.pallas import tpu as pltpu
from jax.sharding import PartitionSpec as P

BF16 = jnp.bfloat16
F32 = jnp.float32
LANES = 128
CHUNKS = 8
MARGIN = 8
VMEM_LIMIT = 16 * 1024 * 1024
SMALL_LIMIT = 4 * 1024 * 1024
FLOPS_PER_US = 1_150_000_000


VMEM = pl.BlockSpec(memory_space=pltpu.VMEM)
HBM = pl.BlockSpec(memory_space=pl.ANY)


def cost(us):
    return pl.CostEstimate(flops=int(us * FLOPS_PER_US), bytes_accessed=0, transcendentals=0)


def call(body, outs, scratch=(), in_specs=None, us=0.5):
    return pl.pallas_call(
        body,
        out_shape=outs,
        **({} if in_specs is None else {"in_specs": in_specs}),
        scratch_shapes=list(scratch),
        compiler_params=pltpu.CompilerParams(vmem_limit_bytes=VMEM_LIMIT),
        cost_estimate=cost(us),
    )


def flipped(value, axis, mask):
    count = lax.axis_size(axis)
    return lax.ppermute(value, axis, [(source, source ^ mask) for source in range(count)])


def block_at(index, size):
    return pl.ds(pl.multiple_of(index * size, size), size)


def to_placement(value):
    count = lax.axis_size("ctx")
    ratio = lax.axis_size("fsdp") // count
    pairs = []
    for f in range(ratio * count):
        for k in range(count):
            target = (k * ratio + f % ratio, f // ratio)
            pairs.append((f * count + k, target[0] * count + target[1]))
    return lax.ppermute(value, ("fsdp", "ctx"), pairs)


def dot(left, right, contract):
    return lax.dot_general(left, right, ((contract[:1], contract[1:]), ((), ())), preferred_element_type=F32)


def shifted(value, steps, backward):
    rows = lax.broadcasted_iota(jnp.int32, value.shape, 0)
    if backward:
        return jnp.where(rows < CHUNKS - steps, pltpu.roll(value, CHUNKS - steps, 0), 0.0)
    return jnp.where(rows >= steps, pltpu.roll(value, steps, 0), 0.0)


def modal_scan(source, target, decay, spread, gain, backward):
    poles, width = decay.shape
    steps = source.shape[0] // CHUNKS
    wide = lambda table, n: jnp.broadcast_to(table[n : n + 1, :], (CHUNKS, width))
    decays = [wide(decay, n) for n in range(poles)]

    def rows(i):
        return pl.ds(steps - 1 - i if backward else i, CHUNKS, stride=steps)

    def gather_up(i, states):
        entry = source[rows(i), :]
        return tuple(d * s + entry for d, s in zip(decays, states))

    zero = jnp.zeros((CHUNKS, width), F32)
    ends = lax.fori_loop(0, steps, gather_up, (zero,) * poles, unroll=4)
    states = []
    for n in range(poles):
        factor = wide(spread, n)
        state = shifted(ends[n], 1, backward)
        reach = 1
        while reach < CHUNKS:
            state = state + factor * shifted(state, reach, backward)
            factor = factor * factor
            reach *= 2
        states.append(state)
    gains = [wide(gain, n) for n in range(poles)]

    def advance(i, states):
        entry = source[rows(i), :]
        states = tuple(d * s + entry for d, s in zip(decays, states))
        terms = [g * s for g, s in zip(gains, states)]
        while len(terms) > 1:
            terms = [a + b for a, b in zip(terms[::2], terms[1::2])]
        target[rows(i), :] = terms[0]
        return states

    lax.fori_loop(0, steps, advance, tuple(states), unroll=2)


def row_blocks(length):
    size = 64 if length % 64 == 0 else length
    return [(start, size) for start in range(0, length, size)]


def forward_body(parts, kinds, taps, decay, spread, gain, skip, query, key, value, long_out, gated, feats, signal, summed):
    length, width = query.shape
    blocks = row_blocks(length)
    for j in range(3):
        feats[j, :MARGIN, :] = jnp.zeros((MARGIN, width), F32)
        for start, size in blocks:
            row, total = kinds(parts, j, start, size)
            feats[j, pl.ds(MARGIN + row, size), :] = total.astype(BF16).astype(F32)
    for start, size in blocks:
        mixed = []
        for j in range(3):
            total = taps[j, 0:1, :] * feats[j, MARGIN + start : MARGIN + start + size, :]
            for lag in range(1, taps.shape[1]):
                first = MARGIN + start - lag
                total = total + taps[j, lag : lag + 1, :] * feats[j, first : first + size, :]
            mixed.append(total)
        at = slice(start, start + size)
        query[at, :], key[at, :], value[at, :] = mixed
        signal[at, :] = mixed[1] * mixed[2]
    modal_scan(signal, summed, decay[...], spread[...], gain[...], False)
    for start, size in blocks:
        at = slice(start, start + size)
        result = summed[at, :] + skip[...] * signal[at, :]
        long_out[at, :] = result
        gated[at, :] = (query[at, :] * result).astype(BF16)


def backward_body(parts, kinds, taps, decay, spread, gain, skip, query, key, value, long_out, grads, mixin, grad_long, summed):
    length, width = query.shape
    blocks = row_blocks(length)
    for start, size in blocks:
        row, grad_gated = kinds(parts, 0, start, size)
        at = pl.ds(row, size)
        mixin[0, at, :] = grad_gated * long_out[at, :]
        grad_long[at, :] = grad_gated * query[at, :]
    modal_scan(grad_long, summed, decay[...], spread[...], gain[...], True)
    for start, size in blocks:
        at = slice(start, start + size)
        grad_signal = summed[at, :] + skip[...] * grad_long[at, :]
        mixin[1, at, :] = grad_signal * value[at, :]
        mixin[2, at, :] = grad_signal * key[at, :]
    for j in range(3):
        mixin[j, length : length + MARGIN, :] = jnp.zeros((MARGIN, width), F32)
        for start, size in blocks:
            total = taps[j, 0:1, :] * mixin[j, start : start + size, :]
            for lag in range(1, taps.shape[1]):
                total = total + taps[j, lag : lag + 1, :] * mixin[j, start + lag : start + lag + size, :]
            grads[j, start : start + size, :] = total.astype(BF16)


def sum_of_three(parts, j, start, size):
    half = parts[0].shape[1]
    other, local = divmod(start, half)
    own, near, far = parts[3 * other : 3 * other + 3]
    at = slice(local, local + size)
    total = own[j, at, :] + near[j, at, :].astype(F32) + far[j, at, :].astype(F32)
    return pl.multiple_of(((lax.axis_index("ctx") >> 1) ^ other) * half + local, MARGIN), total


def plain(parts, j, start, size):
    return start, parts[0][j, start : start + size, :].astype(F32)


def filter_forward(parts, kinds, tables, length, width):
    count = len(parts)

    def body(*refs):
        forward_body(refs[:count], kinds, *refs[count:])

    wide = jax.ShapeDtypeStruct((length, width), F32)
    return call(
        body,
        (wide, wide, wide, wide, jax.ShapeDtypeStruct((length, width), BF16)),
        [
            pltpu.VMEM((3, MARGIN + length, width), F32),
            pltpu.VMEM((length, width), F32),
            pltpu.VMEM((length, width), F32),
        ],
        us=3.2,
    )(*parts, *tables)


def filter_backward(parts, kinds, tables, saved, length, width, after=()):
    count = len(parts)
    inputs = count + len(tables) + len(saved)

    def body(*refs):
        backward_body(refs[:count], kinds, *refs[count:inputs], *refs[inputs + len(after) :])

    return call(
        body,
        jax.ShapeDtypeStruct((3, length, width), BF16),
        [
            pltpu.VMEM((3, length + MARGIN, width), F32),
            pltpu.VMEM((length, width), F32),
            pltpu.VMEM((length, width), F32),
        ],
        in_specs=[VMEM] * inputs + [HBM] * len(after),
        us=2.1,
    )(*parts, *tables, *saved, *after)


def later(value, *after):
    def body(*refs):
        pass

    return pl.pallas_call(
        body,
        out_shape=jax.ShapeDtypeStruct(value.shape, value.dtype),
        in_specs=[HBM] * (1 + len(after)),
        out_specs=HBM,
        input_output_aliases={0: 0},
        compiler_params=pltpu.CompilerParams(vmem_limit_bytes=SMALL_LIMIT),
        cost_estimate=cost(0.05),
    )(value, *after)


def column_blocks(rows):
    length, width = rows.shape[0], rows.shape[1] // 4

    def body(rows, own, near, far, arrived):
        me = lax.axis_index("ctx")
        side = lax.axis_index("fsdp") & 1
        copies = []
        for n, (mask, out) in enumerate(((2 ^ side, far), (1, near), (0, own))):
            copies.append(pltpu.make_async_copy(rows.at[:, block_at(me ^ mask, width)], out, arrived.at[n]))
            copies[-1].start()
        for copy in copies:
            copy.wait()

    block = jax.ShapeDtypeStruct((length, width), rows.dtype)
    return call(body, (block,) * 3, [pltpu.SemaphoreType.DMA((3,))], in_specs=[HBM], us=0.7)(rows)


def fetched(block):
    pairs = [(4 * f + k, 4 * f + (k ^ 2 ^ (f & 1))) for f in range(8) for k in range(4)]
    return lax.ppermute(block, ("fsdp", "ctx"), pairs)


def project(pieces, other, weight):
    groups, depth, channels = weight.shape
    part = pieces[0].shape[0]
    length = 2 * part
    width = channels // 4

    def body(first, second, weight, own, far, give, give_far, held, product):
        me = lax.axis_index("ctx")
        core = (me ^ lax.axis_index("fsdp")) & 1 if other else me & 1
        held[block_at(core, part), :] = first[...]
        held[block_at(1 - core, part), :] = second[...]
        for j in range(groups):
            product[...] = dot(held[...], weight[j], (1, 0))
            own[j] = product[:, block_at(me, width)]
            far[j] = product[:, block_at(me ^ 2, width)].astype(BF16)
            give[j] = product[:, block_at(me ^ 1, width)].astype(BF16)
            give_far[j] = product[:, block_at(me ^ 3, width)].astype(BF16)

    sums = jax.ShapeDtypeStruct((groups, length, width), BF16)
    return call(
        body,
        (jax.ShapeDtypeStruct((groups, length, width), F32), sums, sums, sums),
        [pltpu.VMEM((length, depth), BF16), pltpu.VMEM((length, channels), F32)],
        us=0.7 * groups,
    )(*pieces, weight)


def add_far(left, right):
    def body(left, right, out):
        out[...] = (left[...].astype(F32) + right[...].astype(F32)).astype(BF16)

    return call(body, jax.ShapeDtypeStruct(left.shape, BF16))(left, right)


def channel_sums(pieces, other, weight):
    own, far, give, give_far = project(pieces, other, weight)
    passed = add_far(far, flipped(give_far, "ctx", 1))
    return own, flipped(give, "ctx", 1), flipped(passed, "ctx", 2)


def by_token(here, there):
    return here[0], here[1], there[2], there[0], there[1], here[2]


def all_channels(value, far):
    return value, far, flipped(value, "ctx", 1), flipped(far, "ctx", 1)


def output_pieces(gathered, weight, after=()):
    groups, length, width = gathered[0].shape
    piece = weight.shape[1] // 4
    part = length // 4
    channels = 4 * width

    def product(whole, weight, at, index):
        total = None
        for j in range(groups):
            term = dot(whole[j, at, :], weight[j, block_at(index, piece), :], (1, 1))
            total = term if total is None else total + term
        return total.astype(BF16)

    def pieces(whole, weight, side, low, first, second):
        first[...] = product(whole, weight, slice(None), 2 * side)
        for high in range(2):
            rows = slice(high * part, (high + 1) * part)
            for s in range(2):
                columns = slice(s * piece, (s + 1) * piece)
                second[rows, columns] = product(whole, weight, block_at(2 * high + low, part), 2 * s + 1)

    def first_body(own, far, near, near_far, weight, *refs):
        whole, first, second = refs[len(after) :]
        me = lax.axis_index("ctx")
        place = lax.axis_index("fsdp")
        for j in range(groups):
            for mask, value in ((0, own), (2, far), (1, near), (3, near_far)):
                whole[j, :, block_at(me ^ mask, width)] = value[j]
        pieces(whole, weight, 1 - (place & 1), 1 - ((place >> 1) & 1), first, second)

    def second_body(whole, weight, first, second):
        place = lax.axis_index("fsdp")
        pieces(whole, weight, place & 1, (place >> 1) & 1, first, second)

    parts = (jax.ShapeDtypeStruct((length, piece), BF16), jax.ShapeDtypeStruct((2 * part, 2 * piece), BF16))
    whole, *gives = call(
        first_body,
        (jax.ShapeDtypeStruct((groups, length, channels), BF16), *parts),
        in_specs=[VMEM] * 5 + [HBM] * len(after),
        us=0.6 * groups,
    )(*gathered, weight, *after)
    keeps = call(second_body, parts, us=0.4 * groups)(whole, weight)
    return whole, keeps, gives


def exchange(gives):
    return flipped(gives[0], "fsdp", 1), flipped(gives[1], "fsdp", 2)


def block_sums(keeps, givens):
    length, piece = keeps[0].shape
    part = length // 4
    both = lambda keep, given, rows, columns: keep[rows, columns].astype(F32) + given[rows, columns].astype(F32)

    def second_body(keep_x, given_x, keep_z, given_z, give_z, give_x, next_z, next_x):
        place = lax.axis_index("fsdp")
        side, low = place & 1, (place >> 1) & 1
        for high in range(2):
            rows = slice(high * part, (high + 1) * part)
            take = lambda bit: both(keep_x, given_x, block_at(2 * high + bit, part), slice(None))
            give_z[rows, :] = take(1 - low).astype(BF16)
            next_z[rows, :] = take(low)
        take = lambda bit: both(keep_z, given_z, slice(None), block_at(bit, piece))
        give_x[...] = take(1 - side).astype(BF16)
        next_x[...] = take(side)

    square = lambda kind: jax.ShapeDtypeStruct((2 * part, piece), kind)
    give_z, give_x, next_z, next_x = call(second_body, (square(BF16), square(BF16), square(F32), square(F32)))(
        keeps[0], givens[0], keeps[1], givens[1]
    )

    def third_body(keep_z, given_z, keep_x, given_x, give, keep):
        high = lax.axis_index("fsdp") >> 2
        for bit, out in ((1 - high, give), (high, keep)):
            at = block_at(bit, part)
            for half, (mine, other) in enumerate(((keep_z, given_z), (keep_x, given_x))):
                columns = slice(half * piece, (half + 1) * piece)
                out[:, columns] = both(mine, other, at, slice(None)).astype(out.dtype)

    block = lambda kind: jax.ShapeDtypeStruct((part, 2 * piece), kind)
    give, keep = call(third_body, (block(BF16), block(F32)))(
        next_z, flipped(give_z, "fsdp", 2), next_x, flipped(give_x, "fsdp", 1)
    )

    def last_body(keep, given, out):
        out[...] = (keep[...] + given[...].astype(F32)).astype(BF16)

    return to_placement(call(last_body, block(BF16))(keep, flipped(give, "fsdp", 4)))


def turned(pieces):
    part, depth = pieces[0].shape

    def body(a, b, c, d, out):
        me = lax.axis_index("ctx")
        side = lax.axis_index("fsdp") & 1
        for mask, piece in ((0, a), (1, b), (2 ^ side, c), (3 ^ side, d)):
            out[:, block_at(me ^ mask, part)] = piece[...].T

    return call(body, jax.ShapeDtypeStruct((depth, 4 * part), pieces[0].dtype), us=1.0)(*pieces)


def weight_gradient(rows, values):
    depth, length = rows.shape
    groups, _, channels = values.shape
    tile = depth // 2

    def body(rows, values, out, mark):
        out[0] = dot(rows[...], values[0], (1, 0))
        mark[...] = jnp.zeros_like(mark)

    return pl.pallas_call(
        body,
        out_shape=(jax.ShapeDtypeStruct((groups, depth, channels), F32), jax.ShapeDtypeStruct((8, LANES), F32)),
        grid=(groups, depth // tile),
        in_specs=[
            pl.BlockSpec((tile, length), lambda j, i: (i, 0)),
            pl.BlockSpec((1, length, channels), lambda j, i: (j, 0, 0)),
        ],
        out_specs=(pl.BlockSpec((1, tile, channels), lambda j, i: (j, i, 0)), pl.BlockSpec((8, LANES), lambda j, i: (0, 0))),
        compiler_params=pltpu.CompilerParams(vmem_limit_bytes=VMEM_LIMIT),
        cost_estimate=cost(1.5 * groups),
    )(rows, values)


def four_by_eight(tokens, weights, tables, out_weight, grad_mixed):
    length, width = 4 * tokens.shape[0], weights.shape[2] // 4
    own, near, far = column_blocks(tokens)
    here = (own, flipped(near, "ctx", 1))
    far = fetched(far)
    there = (far, flipped(far, "fsdp", 1))
    feats_here = channel_sums(here, 0, weights)
    grad_own, grad_near, grad_far = column_blocks(grad_mixed)
    grad_here = (grad_own, flipped(grad_near, "ctx", 1))
    grad_far = fetched(later(grad_far, feats_here[2]))
    grad_there = (grad_far, flipped(grad_far, "fsdp", 1))
    feats_there = channel_sums(there, 1, weights)
    grads_here = channel_sums(grad_here, 0, out_weight[None])
    grads_there = channel_sums(grad_there, 1, out_weight[None])
    *saved, gated = filter_forward(by_token(feats_here, feats_there), sum_of_three, tables, length, width)
    gated = gated[None]
    gated_far = flipped(gated, "ctx", 2)
    all_gated = all_channels(gated, gated_far)
    whole_gated, keeps, gives = output_pieces(all_gated, out_weight[None])
    givens = exchange(gives)
    mixed = block_sums(keeps, givens)
    grads = filter_backward(by_token(grads_here, grads_there), sum_of_three, tables, saved, length, width)
    grads = later(grads, gated_far)
    grad_out, mark = weight_gradient(turned(grad_here + grad_there), whole_gated)
    token_rows = turned(here + there)
    grads_far = later(flipped(grads, "ctx", 2), *givens, keeps[0], token_rows, mark)
    whole_grads, keeps, gives = output_pieces(all_channels(grads, grads_far), weights)
    grad_tokens = block_sums(keeps, exchange(gives))
    grad_in, _ = weight_gradient(token_rows, whole_grads)
    return mixed, grad_tokens, grad_in, grad_out[0]


def any_mesh(tokens, weights, tables, out_weight, grad_mixed):
    count = lax.axis_size("ctx")
    columns = lambda rows: lax.all_to_all(rows, "ctx", split_axis=1, concat_axis=0, tiled=True)
    whole_tokens, whole_cotangents = columns(tokens), columns(grad_mixed)
    length, width = whole_tokens.shape[0], weights.shape[2] // count

    def channel_sums(rows, weight):
        partial = jnp.einsum("td,jdc->jtc", rows, weight, preferred_element_type=F32)
        return lax.psum_scatter(partial.astype(BF16), "ctx", scatter_dimension=2, tiled=True)

    def block_sums(values, weight):
        partial = jnp.einsum("jtc,jdc->td", values, weight, preferred_element_type=F32)
        ratio = lax.axis_size("fsdp") // count
        pieces = partial.astype(BF16).reshape(count, length // count, ratio, -1).transpose(0, 2, 1, 3)
        pieces = pieces.reshape(count * ratio, length // count, -1)
        return to_placement(lax.psum_scatter(pieces, "fsdp", scatter_dimension=0, tiled=True)[0])

    feats = channel_sums(whole_tokens, weights)
    grad_gated = channel_sums(whole_cotangents, out_weight[None])
    *saved, gated = filter_forward((feats,), plain, tables, length, width)
    grads = filter_backward((grad_gated,), plain, tables, saved, length, width)
    whole_gated = lax.all_gather(gated, "ctx", axis=1, tiled=True)
    whole_grads = lax.all_gather(grads, "ctx", axis=2, tiled=True)
    mixed = block_sums(whole_gated[None], out_weight[None])
    grad_tokens = block_sums(whole_grads, weights)
    grad_in = jnp.einsum("td,jtc->jdc", whole_tokens, whole_grads, preferred_element_type=F32)
    grad_out = jnp.einsum("td,tc->dc", whole_cotangents, whole_gated, preferred_element_type=F32)
    return mixed, grad_tokens, grad_in, grad_out


def per_device(tokens, in_weight, conv_taps, decay_rate, residue, skip_gain, out_weight, grad_mixed):
    count, blocks = lax.axis_size("ctx"), lax.axis_size("fsdp")
    weights = in_weight.transpose(1, 0, 2)
    length = count * tokens.shape[0]
    width = weights.shape[2] // count
    mine = lambda table: lax.dynamic_slice_in_dim(table, lax.axis_index("ctx") * width, width, table.ndim - 1)
    rate = mine(decay_rate)
    gain = mine(residue) * jnp.sqrt(-jnp.expm1(-2.0 * rate))
    tables = (mine(conv_taps.transpose(1, 0, 2)), jnp.exp(-rate), jnp.exp(-rate * (length // CHUNKS)), gain, mine(skip_gain[None]))
    tuned = count == 4 and blocks == 8 and width % LANES == 0 and tokens.shape[0] % LANES == 0
    plan = four_by_eight if tuned else any_mesh
    mixed, grad_tokens, grad_in, grad_out = plan(tokens, weights, tables, out_weight, grad_mixed)
    return mixed, grad_tokens, grad_in.transpose(1, 0, 2), grad_out


def solution(mesh):
    return jax.shard_map(
        per_device,
        mesh=mesh,
        in_specs=(
            P("ctx", None),
            P("ctx", None, "fsdp"),
            P(None, None, "fsdp"),
            P(None, "fsdp"),
            P(None, "fsdp"),
            P("fsdp"),
            P("ctx", "fsdp"),
            P("ctx", None),
        ),
        out_specs=(P("ctx", "fsdp"), P("ctx", "fsdp"), P("ctx", None, "fsdp"), P("ctx", "fsdp")),
        check_vma=False,
    )
```

```python
import functools

import jax
import jax.numpy as jnp
from jax import lax
from jax.experimental import pallas as pl
from jax.experimental.pallas import tpu as pltpu
from jax.sharding import PartitionSpec as P

BF16 = jnp.bfloat16
F32 = jnp.float32
LANES = 128
CHUNKS = 8
MARGIN = 8
VMEM_LIMIT = 16 * 1024 * 1024
SMALL_LIMIT = 4 * 1024 * 1024
FLOPS_PER_US = 1_150_000_000


VMEM = pl.BlockSpec(memory_space=pltpu.VMEM)
HBM = pl.BlockSpec(memory_space=pl.ANY)


def cost(us):
    return pl.CostEstimate(flops=int(us * FLOPS_PER_US), bytes_accessed=0, transcendentals=0)


def call(body, outs, scratch=(), in_specs=None, us=0.5):
    return pl.pallas_call(
        body,
        out_shape=outs,
        **({} if in_specs is None else {"in_specs": in_specs}),
        scratch_shapes=list(scratch),
        compiler_params=pltpu.CompilerParams(vmem_limit_bytes=VMEM_LIMIT),
        cost_estimate=cost(us),
    )


def flipped(value, axis, mask):
    count = lax.axis_size(axis)
    return lax.ppermute(value, axis, [(source, source ^ mask) for source in range(count)])


def block_at(index, size):
    return pl.ds(pl.multiple_of(index * size, size), size)


def to_placement(value):
    count = lax.axis_size("ctx")
    ratio = lax.axis_size("fsdp") // count
    pairs = []
    for f in range(ratio * count):
        for k in range(count):
            target = (k * ratio + f % ratio, f // ratio)
            pairs.append((f * count + k, target[0] * count + target[1]))
    return lax.ppermute(value, ("fsdp", "ctx"), pairs)


def dot(left, right, contract):
    return lax.dot_general(left, right, ((contract[:1], contract[1:]), ((), ())), preferred_element_type=F32)


def shifted(value, steps, backward):
    rows = lax.broadcasted_iota(jnp.int32, value.shape, 0)
    if backward:
        return jnp.where(rows < CHUNKS - steps, pltpu.roll(value, CHUNKS - steps, 0), 0.0)
    return jnp.where(rows >= steps, pltpu.roll(value, steps, 0), 0.0)


def modal_scan(source, target, decay, spread, gain, backward):
    poles, width = decay.shape
    steps = source.shape[0] // CHUNKS
    wide = lambda table, n: jnp.broadcast_to(table[n : n + 1, :], (CHUNKS, width))
    decays = [wide(decay, n) for n in range(poles)]

    def rows(i):
        return pl.ds(steps - 1 - i if backward else i, CHUNKS, stride=steps)

    def gather_up(i, states):
        entry = source[rows(i), :]
        return tuple(d * s + entry for d, s in zip(decays, states))

    zero = jnp.zeros((CHUNKS, width), F32)
    ends = lax.fori_loop(0, steps, gather_up, (zero,) * poles, unroll=4)
    states = []
    for n in range(poles):
        factor = wide(spread, n)
        state = shifted(ends[n], 1, backward)
        reach = 1
        while reach < CHUNKS:
            state = state + factor * shifted(state, reach, backward)
            factor = factor * factor
            reach *= 2
        states.append(state)
    gains = [wide(gain, n) for n in range(poles)]

    def advance(i, states):
        entry = source[rows(i), :]
        states = tuple(d * s + entry for d, s in zip(decays, states))
        terms = [g * s for g, s in zip(gains, states)]
        while len(terms) > 1:
            terms = [a + b for a, b in zip(terms[::2], terms[1::2])]
        target[rows(i), :] = terms[0]
        return states

    lax.fori_loop(0, steps, advance, tuple(states), unroll=2)


def row_blocks(length):
    size = 64 if length % 64 == 0 else length
    return [(start, size) for start in range(0, length, size)]


def forward_body(parts, kinds, taps, decay, spread, gain, skip, query, key, value, long_out, gated, feats, signal, summed):
    length, width = query.shape
    blocks = row_blocks(length)
    for j in range(3):
        feats[j, :MARGIN, :] = jnp.zeros((MARGIN, width), F32)
        for start, size in blocks:
            row, total = kinds(parts, j, start, size)
            feats[j, pl.ds(MARGIN + row, size), :] = total.astype(BF16).astype(F32)
    for start, size in blocks:
        mixed = []
        for j in range(3):
            total = taps[j, 0:1, :] * feats[j, MARGIN + start : MARGIN + start + size, :]
            for lag in range(1, taps.shape[1]):
                first = MARGIN + start - lag
                total = total + taps[j, lag : lag + 1, :] * feats[j, first : first + size, :]
            mixed.append(total)
        at = slice(start, start + size)
        query[at, :], key[at, :], value[at, :] = mixed
        signal[at, :] = mixed[1] * mixed[2]
    modal_scan(signal, summed, decay[...], spread[...], gain[...], False)
    for start, size in blocks:
        at = slice(start, start + size)
        result = summed[at, :] + skip[...] * signal[at, :]
        long_out[at, :] = result
        gated[at, :] = (query[at, :] * result).astype(BF16)


def backward_body(parts, kinds, taps, decay, spread, gain, skip, query, key, value, long_out, grads, mixin, grad_long, summed):
    length, width = query.shape
    blocks = row_blocks(length)
    for start, size in blocks:
        row, grad_gated = kinds(parts, 0, start, size)
        at = pl.ds(row, size)
        mixin[0, at, :] = grad_gated * long_out[at, :]
        grad_long[at, :] = grad_gated * query[at, :]
    modal_scan(grad_long, summed, decay[...], spread[...], gain[...], True)
    for start, size in blocks:
        at = slice(start, start + size)
        grad_signal = summed[at, :] + skip[...] * grad_long[at, :]
        mixin[1, at, :] = grad_signal * value[at, :]
        mixin[2, at, :] = grad_signal * key[at, :]
    for j in range(3):
        mixin[j, length : length + MARGIN, :] = jnp.zeros((MARGIN, width), F32)
        for start, size in blocks:
            total = taps[j, 0:1, :] * mixin[j, start : start + size, :]
            for lag in range(1, taps.shape[1]):
                total = total + taps[j, lag : lag + 1, :] * mixin[j, start + lag : start + lag + size, :]
            grads[j, start : start + size, :] = total.astype(BF16)


def sum_of_three(parts, j, start, size):
    half = parts[0].shape[1]
    other, local = divmod(start, half)
    own, near, far = parts[3 * other : 3 * other + 3]
    at = slice(local, local + size)
    total = own[j, at, :] + near[j, at, :].astype(F32) + far[j, at, :].astype(F32)
    return pl.multiple_of(((lax.axis_index("ctx") >> 1) ^ other) * half + local, MARGIN), total


def plain(parts, j, start, size):
    return start, parts[0][j, start : start + size, :].astype(F32)


def filter_forward(parts, kinds, tables, length, width):
    count = len(parts)

    def body(*refs):
        forward_body(refs[:count], kinds, *refs[count:])

    wide = jax.ShapeDtypeStruct((length, width), F32)
    return call(
        body,
        (wide, wide, wide, wide, jax.ShapeDtypeStruct((length, width), BF16)),
        [
            pltpu.VMEM((3, MARGIN + length, width), F32),
            pltpu.VMEM((length, width), F32),
            pltpu.VMEM((length, width), F32),
        ],
        us=3.2,
    )(*parts, *tables)


def filter_backward(parts, kinds, tables, saved, length, width, after=()):
    count = len(parts)
    inputs = count + len(tables) + len(saved)

    def body(*refs):
        backward_body(refs[:count], kinds, *refs[count:inputs], *refs[inputs + len(after) :])

    return call(
        body,
        jax.ShapeDtypeStruct((3, length, width), BF16),
        [
            pltpu.VMEM((3, length + MARGIN, width), F32),
            pltpu.VMEM((length, width), F32),
            pltpu.VMEM((length, width), F32),
        ],
        in_specs=[VMEM] * inputs + [HBM] * len(after),
        us=2.1,
    )(*parts, *tables, *saved, *after)


def later(value, *after):
    def body(*refs):
        pass

    return pl.pallas_call(
        body,
        out_shape=jax.ShapeDtypeStruct(value.shape, value.dtype),
        in_specs=[HBM] * (1 + len(after)),
        out_specs=HBM,
        input_output_aliases={0: 0},
        compiler_params=pltpu.CompilerParams(vmem_limit_bytes=SMALL_LIMIT),
        cost_estimate=cost(0.05),
    )(value, *after)


def settled(value):
    def body(value, out):
        out[...] = value[...]

    return call(body, jax.ShapeDtypeStruct(value.shape, value.dtype), us=0.3)(value)


def loaded(values, after):
    count = len(values)

    def body(*refs):
        sources, outs, arrived = refs[:count], refs[count + 1 : 2 * count + 1], refs[-1]
        copies = [pltpu.make_async_copy(a, b, arrived.at[n]) for n, (a, b) in enumerate(zip(sources, outs))]
        for copy in copies:
            copy.start()
        for copy in copies:
            copy.wait()

    return pl.pallas_call(
        body,
        out_shape=tuple(pltpu.VMEM(value.shape, value.dtype) for value in values),
        in_specs=[HBM] * (count + 1),
        out_specs=(VMEM,) * count,
        scratch_shapes=[pltpu.SemaphoreType.DMA((count,))],
        compiler_params=pltpu.CompilerParams(vmem_limit_bytes=VMEM_LIMIT),
        cost_estimate=cost(1.3),
    )(*[pltpu.with_memory_space_constraint(value, pltpu.HBM) for value in values], after)


def column_blocks(rows):
    length, width = rows.shape[0], rows.shape[1] // 4

    def body(rows, own, near, far, arrived):
        me = lax.axis_index("ctx")
        side = lax.axis_index("fsdp") & 1
        copies = []
        for n, (mask, out) in enumerate(((2 ^ side, far), (1, near), (0, own))):
            copies.append(pltpu.make_async_copy(rows.at[:, block_at(me ^ mask, width)], out, arrived.at[n]))
            copies[-1].start()
        for copy in copies:
            copy.wait()

    block = jax.ShapeDtypeStruct((length, width), rows.dtype)
    return call(body, (block,) * 3, [pltpu.SemaphoreType.DMA((3,))], in_specs=[HBM], us=0.7)(
        pltpu.with_memory_space_constraint(rows, pltpu.HBM)
    )


def fetched(block):
    pairs = [(4 * f + k, 4 * f + (k ^ 2 ^ (f & 1))) for f in range(8) for k in range(4)]
    return lax.ppermute(block, ("fsdp", "ctx"), pairs)


def project(pieces, other, weight):
    groups, depth, channels = weight.shape
    part = pieces[0].shape[0]
    length = 2 * part
    width = channels // 4

    def body(first, second, weight, own, far, give, give_far, held, product):
        me = lax.axis_index("ctx")
        core = (me ^ lax.axis_index("fsdp")) & 1 if other else me & 1
        held[block_at(core, part), :] = first[...]
        held[block_at(1 - core, part), :] = second[...]
        for j in range(groups):
            product[...] = dot(held[...], weight[j], (1, 0))
            own[j] = product[:, block_at(me, width)]
            far[j] = product[:, block_at(me ^ 2, width)].astype(BF16)
            give[j] = product[:, block_at(me ^ 1, width)].astype(BF16)
            give_far[j] = product[:, block_at(me ^ 3, width)].astype(BF16)

    sums = jax.ShapeDtypeStruct((groups, length, width), BF16)
    return call(
        body,
        (jax.ShapeDtypeStruct((groups, length, width), F32), sums, sums, sums),
        [pltpu.VMEM((length, depth), BF16), pltpu.VMEM((length, channels), F32)],
        us=0.7 * groups,
    )(*pieces, weight)


def add_far(left, right):
    def body(left, right, out):
        out[...] = (left[...].astype(F32) + right[...].astype(F32)).astype(BF16)

    return call(body, jax.ShapeDtypeStruct(left.shape, BF16))(left, right)


def channel_sums(pieces, other, weight):
    own, far, give, give_far = project(pieces, other, weight)
    passed = add_far(far, flipped(give_far, "ctx", 1))
    return (own, flipped(give, "ctx", 1), flipped(passed, "ctx", 2)), passed


def by_token(here, there):
    return here[0], here[1], there[2], there[0], there[1], here[2]


def all_channels(value, far):
    return value, far, flipped(value, "ctx", 1), flipped(far, "ctx", 1)


def output_pieces(gathered, weight, after=()):
    groups, length, width = gathered[0].shape
    piece = weight.shape[1] // 4
    part = length // 4
    channels = 4 * width

    def product(whole, weight, at, index):
        total = None
        for j in range(groups):
            term = dot(whole[j, at, :], weight[j, block_at(index, piece), :], (1, 1))
            total = term if total is None else total + term
        return total.astype(BF16)

    def pieces(whole, weight, side, low, first, second):
        first[...] = product(whole, weight, slice(None), 2 * side)
        for high in range(2):
            rows = slice(high * part, (high + 1) * part)
            for s in range(2):
                columns = slice(s * piece, (s + 1) * piece)
                second[rows, columns] = product(whole, weight, block_at(2 * high + low, part), 2 * s + 1)

    def first_body(own, far, near, near_far, weight, *refs):
        whole, first, second = refs[len(after) :]
        me = lax.axis_index("ctx")
        place = lax.axis_index("fsdp")
        for j in range(groups):
            for mask, value in ((0, own), (2, far), (1, near), (3, near_far)):
                whole[j, :, block_at(me ^ mask, width)] = value[j]
        pieces(whole, weight, 1 - (place & 1), 1 - ((place >> 1) & 1), first, second)

    def second_body(whole, weight, first, second):
        place = lax.axis_index("fsdp")
        pieces(whole, weight, place & 1, (place >> 1) & 1, first, second)

    parts = (jax.ShapeDtypeStruct((length, piece), BF16), jax.ShapeDtypeStruct((2 * part, 2 * piece), BF16))
    whole, *gives = call(
        first_body,
        (jax.ShapeDtypeStruct((groups, length, channels), BF16), *parts),
        in_specs=[VMEM] * 5 + [HBM] * len(after),
        us=0.6 * groups,
    )(*gathered, weight, *after)
    keeps = call(second_body, parts, us=0.4 * groups)(whole, weight)
    return whole, keeps, gives


def exchange(gives):
    return flipped(gives[0], "fsdp", 1), flipped(gives[1], "fsdp", 2)


def block_sums(keeps, givens, after=()):
    length, piece = keeps[0].shape
    part = length // 4
    both = lambda keep, given, rows, columns: keep[rows, columns].astype(F32) + given[rows, columns].astype(F32)

    def second_body(keep_x, given_x, keep_z, given_z, *refs):
        give_z, give_x, next_z, next_x = refs[len(after) :]
        place = lax.axis_index("fsdp")
        side, low = place & 1, (place >> 1) & 1
        for high in range(2):
            rows = slice(high * part, (high + 1) * part)
            take = lambda bit: both(keep_x, given_x, block_at(2 * high + bit, part), slice(None))
            give_z[rows, :] = take(1 - low).astype(BF16)
            next_z[rows, :] = take(low)
        take = lambda bit: both(keep_z, given_z, slice(None), block_at(bit, piece))
        give_x[...] = take(1 - side).astype(BF16)
        next_x[...] = take(side)

    square = lambda kind: jax.ShapeDtypeStruct((2 * part, piece), kind)
    give_z, give_x, next_z, next_x = call(
        second_body,
        (square(BF16), square(BF16), square(F32), square(F32)),
        in_specs=[VMEM] * 4 + [HBM] * len(after),
    )(keeps[0], givens[0], keeps[1], givens[1], *after)

    def third_body(keep_z, given_z, keep_x, given_x, give, keep):
        high = lax.axis_index("fsdp") >> 2
        for bit, out in ((1 - high, give), (high, keep)):
            at = block_at(bit, part)
            for half, (mine, other) in enumerate(((keep_z, given_z), (keep_x, given_x))):
                columns = slice(half * piece, (half + 1) * piece)
                out[:, columns] = both(mine, other, at, slice(None)).astype(out.dtype)

    block = lambda kind: jax.ShapeDtypeStruct((part, 2 * piece), kind)
    give, keep = call(third_body, (block(BF16), block(F32)))(
        next_z, flipped(give_z, "fsdp", 2), next_x, flipped(give_x, "fsdp", 1)
    )

    def last_body(keep, given, out):
        out[...] = (keep[...] + given[...].astype(F32)).astype(BF16)

    return call(last_body, block(BF16))(keep, flipped(give, "fsdp", 4)), give


def turned(pieces):
    part, depth = pieces[0].shape

    def body(a, b, c, d, out):
        me = lax.axis_index("ctx")
        side = lax.axis_index("fsdp") & 1
        for mask, piece in ((0, a), (1, b), (2 ^ side, c), (3 ^ side, d)):
            out[:, block_at(me ^ mask, part)] = piece[...].T

    return call(body, jax.ShapeDtypeStruct((depth, 4 * part), pieces[0].dtype), us=1.0)(*pieces)


def weight_gradient(rows, values, after=()):
    depth, length = rows.shape
    groups, _, channels = values.shape
    tile = depth // 2

    def body(rows, values, *refs):
        out, mark = refs[len(after) :]
        out[0] = dot(rows[...], values[0], (1, 0))
        mark[...] = jnp.zeros_like(mark)

    return pl.pallas_call(
        body,
        out_shape=(jax.ShapeDtypeStruct((groups, depth, channels), F32), jax.ShapeDtypeStruct((8, LANES), F32)),
        grid=(groups, depth // tile),
        in_specs=[
            pl.BlockSpec((tile, length), lambda j, i: (i, 0)),
            pl.BlockSpec((1, length, channels), lambda j, i: (j, 0, 0)),
        ]
        + [HBM] * len(after),
        out_specs=(pl.BlockSpec((1, tile, channels), lambda j, i: (j, i, 0)), pl.BlockSpec((8, LANES), lambda j, i: (0, 0))),
        compiler_params=pltpu.CompilerParams(vmem_limit_bytes=VMEM_LIMIT),
        cost_estimate=cost(1.5 * groups),
    )(rows, values, *after)


def four_by_eight(tokens, weights, tables, out_weight, grad_mixed):
    length, width = 4 * tokens.shape[0], weights.shape[2] // 4
    own, near, far = column_blocks(tokens)
    weights, out_weight = loaded((weights, out_weight), near)
    here = (own, flipped(near, "ctx", 1))
    feats_here, passed = channel_sums(here, 0, weights)
    far = later(fetched(far), passed)
    there = (far, flipped(far, "fsdp", 1))
    grad_own, grad_near, grad_far = column_blocks(grad_mixed)
    grad_here = (grad_own, flipped(grad_near, "ctx", 1))
    grad_far = fetched(later(grad_far, far))
    grad_there = (grad_far, flipped(grad_far, "fsdp", 1))
    feats_there, _ = channel_sums(there, 1, weights)
    grads_here, _ = channel_sums(grad_here, 0, out_weight[None])
    grads_there, _ = channel_sums(grad_there, 1, out_weight[None])
    *saved, gated = filter_forward(by_token(feats_here, feats_there), sum_of_three, tables, length, width)
    gated = gated[None]
    gated_far = flipped(gated, "ctx", 2)
    all_gated = all_channels(gated, gated_far)
    whole_gated, keeps, gives = output_pieces(all_gated, out_weight[None])
    givens = exchange(gives)
    mixed, mixed_last = block_sums(keeps, givens)
    grads = filter_backward(by_token(grads_here, grads_there), sum_of_three, tables, saved, length, width)
    grads = later(grads, gated_far)
    grad_out, mark = weight_gradient(turned(grad_here + grad_there), whole_gated)
    token_rows = turned(here + there)
    grads_far = later(flipped(grads, "ctx", 2), *givens, keeps[0], token_rows, mark)
    whole_grads, keeps, gives = output_pieces(all_channels(grads, grads_far), weights)
    grad_in, mark = weight_gradient(token_rows, whole_grads, (mixed_last,))
    grad_tokens, last = block_sums(keeps, exchange(gives), (mark,))
    mixed = settled(to_placement(later(mixed, last)))
    grad_tokens = settled(to_placement(grad_tokens))
    return mixed, grad_tokens, grad_in, grad_out[0]


def any_mesh(tokens, weights, tables, out_weight, grad_mixed):
    count = lax.axis_size("ctx")
    columns = lambda rows: lax.all_to_all(rows, "ctx", split_axis=1, concat_axis=0, tiled=True)
    whole_tokens, whole_cotangents = columns(tokens), columns(grad_mixed)
    length, width = whole_tokens.shape[0], weights.shape[2] // count

    def channel_sums(rows, weight):
        partial = jnp.einsum("td,jdc->jtc", rows, weight, preferred_element_type=F32)
        return lax.psum_scatter(partial.astype(BF16), "ctx", scatter_dimension=2, tiled=True)

    def block_sums(values, weight):
        partial = jnp.einsum("jtc,jdc->td", values, weight, preferred_element_type=F32)
        ratio = lax.axis_size("fsdp") // count
        pieces = partial.astype(BF16).reshape(count, length // count, ratio, -1).transpose(0, 2, 1, 3)
        pieces = pieces.reshape(count * ratio, length // count, -1)
        return to_placement(lax.psum_scatter(pieces, "fsdp", scatter_dimension=0, tiled=True)[0])

    feats = channel_sums(whole_tokens, weights)
    grad_gated = channel_sums(whole_cotangents, out_weight[None])
    *saved, gated = filter_forward((feats,), plain, tables, length, width)
    grads = filter_backward((grad_gated,), plain, tables, saved, length, width)
    whole_gated = lax.all_gather(gated, "ctx", axis=1, tiled=True)
    whole_grads = lax.all_gather(grads, "ctx", axis=2, tiled=True)
    mixed = block_sums(whole_gated[None], out_weight[None])
    grad_tokens = block_sums(whole_grads, weights)
    grad_in = jnp.einsum("td,jtc->jdc", whole_tokens, whole_grads, preferred_element_type=F32)
    grad_out = jnp.einsum("td,tc->dc", whole_cotangents, whole_gated, preferred_element_type=F32)
    return mixed, grad_tokens, grad_in, grad_out


def per_device(tokens, in_weight, conv_taps, decay_rate, residue, skip_gain, out_weight, grad_mixed):
    count, blocks = lax.axis_size("ctx"), lax.axis_size("fsdp")
    weights = in_weight.transpose(1, 0, 2)
    length = count * tokens.shape[0]
    width = weights.shape[2] // count
    mine = lambda table: lax.dynamic_slice_in_dim(table, lax.axis_index("ctx") * width, width, table.ndim - 1)
    rate = mine(decay_rate)
    gain = mine(residue) * jnp.sqrt(-jnp.expm1(-2.0 * rate))
    tables = (mine(conv_taps.transpose(1, 0, 2)), jnp.exp(-rate), jnp.exp(-rate * (length // CHUNKS)), gain, mine(skip_gain[None]))
    tuned = count == 4 and blocks == 8 and width % LANES == 0 and tokens.shape[0] % LANES == 0
    plan = four_by_eight if tuned else any_mesh
    mixed, grad_tokens, grad_in, grad_out = plan(tokens, weights, tables, out_weight, grad_mixed)
    return mixed, grad_tokens, grad_in.transpose(1, 0, 2), grad_out


def solution(mesh):
    return jax.shard_map(
        per_device,
        mesh=mesh,
        in_specs=(
            P("ctx", None),
            P("ctx", None, "fsdp"),
            P(None, None, "fsdp"),
            P(None, "fsdp"),
            P(None, "fsdp"),
            P("fsdp"),
            P("ctx", "fsdp"),
            P("ctx", None),
        ),
        out_specs=(P("ctx", "fsdp"), P("ctx", "fsdp"), P("ctx", None, "fsdp"), P("ctx", "fsdp")),
        check_vma=False,
    )
```

```python
import functools

import jax
import jax.numpy as jnp
from jax import lax
from jax.experimental import pallas as pl
from jax.experimental.pallas import tpu as pltpu
from jax.sharding import PartitionSpec as P

BF16 = jnp.bfloat16
F32 = jnp.float32
LANES = 128
CHUNKS = 8
MARGIN = 8
VMEM_LIMIT = 12 * 1024 * 1024
SMALL_LIMIT = 4 * 1024 * 1024
FLOPS_PER_US = 1_150_000_000


VMEM = pl.BlockSpec(memory_space=pltpu.VMEM)
HBM = pl.BlockSpec(memory_space=pl.ANY)


def cost(us):
    return pl.CostEstimate(flops=int(us * FLOPS_PER_US), bytes_accessed=0, transcendentals=0)


def call(body, outs, scratch=(), in_specs=None, us=0.5, limit=VMEM_LIMIT):
    return pl.pallas_call(
        body,
        out_shape=outs,
        **({} if in_specs is None else {"in_specs": in_specs}),
        scratch_shapes=list(scratch),
        compiler_params=pltpu.CompilerParams(vmem_limit_bytes=limit),
        cost_estimate=cost(us),
    )


def flipped(value, axis, mask):
    count = lax.axis_size(axis)
    return lax.ppermute(value, axis, [(source, source ^ mask) for source in range(count)])


def block_at(index, size):
    return pl.ds(pl.multiple_of(index * size, size), size)


def to_placement(value):
    count = lax.axis_size("ctx")
    ratio = lax.axis_size("fsdp") // count
    pairs = []
    for f in range(ratio * count):
        for k in range(count):
            target = (k * ratio + f % ratio, f // ratio)
            pairs.append((f * count + k, target[0] * count + target[1]))
    return lax.ppermute(value, ("fsdp", "ctx"), pairs)


def dot(left, right, contract):
    return lax.dot_general(left, right, ((contract[:1], contract[1:]), ((), ())), preferred_element_type=F32)


def shifted(value, steps, backward):
    rows = lax.broadcasted_iota(jnp.int32, value.shape, 0)
    if backward:
        return jnp.where(rows < CHUNKS - steps, pltpu.roll(value, CHUNKS - steps, 0), 0.0)
    return jnp.where(rows >= steps, pltpu.roll(value, steps, 0), 0.0)


def modal_scan(source, target, decay, spread, gain, backward):
    poles, width = decay.shape
    steps = source.shape[0] // CHUNKS
    wide = lambda table, n: jnp.broadcast_to(table[n : n + 1, :], (CHUNKS, width))
    decays = [wide(decay, n) for n in range(poles)]

    def rows(i):
        return pl.ds(steps - 1 - i if backward else i, CHUNKS, stride=steps)

    def gather_up(i, states):
        entry = source[rows(i), :]
        return tuple(d * s + entry for d, s in zip(decays, states))

    zero = jnp.zeros((CHUNKS, width), F32)
    ends = lax.fori_loop(0, steps, gather_up, (zero,) * poles, unroll=4)
    states = []
    for n in range(poles):
        factor = wide(spread, n)
        state = shifted(ends[n], 1, backward)
        reach = 1
        while reach < CHUNKS:
            state = state + factor * shifted(state, reach, backward)
            factor = factor * factor
            reach *= 2
        states.append(state)
    gains = [wide(gain, n) for n in range(poles)]

    def advance(i, states):
        entry = source[rows(i), :]
        states = tuple(d * s + entry for d, s in zip(decays, states))
        terms = [g * s for g, s in zip(gains, states)]
        while len(terms) > 1:
            terms = [a + b for a, b in zip(terms[::2], terms[1::2])]
        target[rows(i), :] = terms[0]
        return states

    lax.fori_loop(0, steps, advance, tuple(states), unroll=2)


def row_blocks(length):
    size = 64 if length % 64 == 0 else length
    return [(start, size) for start in range(0, length, size)]


def forward_body(parts, kinds, taps, decay, spread, gain, skip, query, key, value, long_out, gated, feats, signal, summed):
    length, width = query.shape
    blocks = row_blocks(length)
    for j in range(3):
        feats[j, :MARGIN, :] = jnp.zeros((MARGIN, width), F32)
        for start, size in blocks:
            row, total = kinds(parts, j, start, size)
            feats[j, pl.ds(MARGIN + row, size), :] = total.astype(BF16).astype(F32)
    for start, size in blocks:
        mixed = []
        for j in range(3):
            total = taps[j, 0:1, :] * feats[j, MARGIN + start : MARGIN + start + size, :]
            for lag in range(1, taps.shape[1]):
                first = MARGIN + start - lag
                total = total + taps[j, lag : lag + 1, :] * feats[j, first : first + size, :]
            mixed.append(total)
        at = slice(start, start + size)
        query[at, :], key[at, :], value[at, :] = mixed
        signal[at, :] = mixed[1] * mixed[2]
    modal_scan(signal, summed, decay[...], spread[...], gain[...], False)
    for start, size in blocks:
        at = slice(start, start + size)
        result = summed[at, :] + skip[...] * signal[at, :]
        long_out[at, :] = result
        gated[at, :] = (query[at, :] * result).astype(BF16)


def backward_body(parts, kinds, taps, decay, spread, gain, skip, query, key, value, long_out, grads, mixin, grad_long, summed):
    length, width = query.shape
    blocks = row_blocks(length)
    for start, size in blocks:
        row, grad_gated = kinds(parts, 0, start, size)
        at = pl.ds(row, size)
        mixin[0, at, :] = grad_gated * long_out[at, :]
        grad_long[at, :] = grad_gated * query[at, :]
    modal_scan(grad_long, summed, decay[...], spread[...], gain[...], True)
    for start, size in blocks:
        at = slice(start, start + size)
        grad_signal = summed[at, :] + skip[...] * grad_long[at, :]
        mixin[1, at, :] = grad_signal * value[at, :]
        mixin[2, at, :] = grad_signal * key[at, :]
    for j in range(3):
        mixin[j, length : length + MARGIN, :] = jnp.zeros((MARGIN, width), F32)
        for start, size in blocks:
            total = taps[j, 0:1, :] * mixin[j, start : start + size, :]
            for lag in range(1, taps.shape[1]):
                total = total + taps[j, lag : lag + 1, :] * mixin[j, start + lag : start + lag + size, :]
            grads[j, start : start + size, :] = total.astype(BF16)


def sum_of_three(parts, j, start, size):
    half = parts[0].shape[1]
    other, local = divmod(start, half)
    own, near, far = parts[3 * other : 3 * other + 3]
    at = slice(local, local + size)
    total = own[j, at, :] + near[j, at, :].astype(F32) + far[j, at, :].astype(F32)
    return pl.multiple_of(((lax.axis_index("ctx") >> 1) ^ other) * half + local, MARGIN), total


def plain(parts, j, start, size):
    return start, parts[0][j, start : start + size, :].astype(F32)


def filter_forward(parts, kinds, tables, length, width):
    count = len(parts)

    def body(*refs):
        forward_body(refs[:count], kinds, *refs[count:])

    wide = jax.ShapeDtypeStruct((length, width), F32)
    return call(
        body,
        (wide, wide, wide, wide, jax.ShapeDtypeStruct((length, width), BF16)),
        [
            pltpu.VMEM((3, MARGIN + length, width), F32),
            pltpu.VMEM((length, width), F32),
            pltpu.VMEM((length, width), F32),
        ],
        us=3.2,
    )(*parts, *tables)


def filter_backward(parts, kinds, tables, saved, length, width, after=()):
    count = len(parts)
    inputs = count + len(tables) + len(saved)

    def body(*refs):
        backward_body(refs[:count], kinds, *refs[count:inputs], *refs[inputs + len(after) :])

    return call(
        body,
        jax.ShapeDtypeStruct((3, length, width), BF16),
        [
            pltpu.VMEM((3, length + MARGIN, width), F32),
            pltpu.VMEM((length, width), F32),
            pltpu.VMEM((length, width), F32),
        ],
        in_specs=[VMEM] * inputs + [HBM] * len(after),
        us=2.1,
    )(*parts, *tables, *saved, *after)


def later(value, *after):
    def body(*refs):
        pass

    return pl.pallas_call(
        body,
        out_shape=jax.ShapeDtypeStruct(value.shape, value.dtype),
        in_specs=[HBM] * (1 + len(after)),
        out_specs=HBM,
        input_output_aliases={0: 0},
        compiler_params=pltpu.CompilerParams(vmem_limit_bytes=SMALL_LIMIT),
        cost_estimate=cost(0.05),
    )(value, *after)


def loaded(values, after):
    count = len(values)

    def body(*refs):
        sources, outs, arrived = refs[:count], refs[count + 1 : 2 * count + 1], refs[-1]
        copies = [pltpu.make_async_copy(a, b, arrived.at[n]) for n, (a, b) in enumerate(zip(sources, outs))]
        for copy in copies:
            copy.start()
        for copy in copies:
            copy.wait()

    return pl.pallas_call(
        body,
        out_shape=tuple(pltpu.VMEM(value.shape, value.dtype) for value in values),
        in_specs=[HBM] * (count + 1),
        out_specs=(VMEM,) * count,
        scratch_shapes=[pltpu.SemaphoreType.DMA((count,))],
        compiler_params=pltpu.CompilerParams(vmem_limit_bytes=SMALL_LIMIT),
        cost_estimate=cost(1.3),
    )(*[pltpu.with_memory_space_constraint(value, pltpu.HBM) for value in values], after)


def column_blocks(rows):
    length, width = rows.shape[0], rows.shape[1] // 4

    def body(rows, own, near, far, arrived):
        me = lax.axis_index("ctx")
        side = lax.axis_index("fsdp") & 1
        copies = []
        for n, (mask, out) in enumerate(((2 ^ side, far), (1, near), (0, own))):
            copies.append(pltpu.make_async_copy(rows.at[:, block_at(me ^ mask, width)], out, arrived.at[n]))
            copies[-1].start()
        for copy in copies:
            copy.wait()

    block = jax.ShapeDtypeStruct((length, width), rows.dtype)
    return call(body, (block,) * 3, [pltpu.SemaphoreType.DMA((3,))], in_specs=[HBM], us=0.7, limit=SMALL_LIMIT)(
        pltpu.with_memory_space_constraint(rows, pltpu.HBM)
    )


def fetched(block):
    pairs = [(4 * f + k, 4 * f + (k ^ 2 ^ (f & 1))) for f in range(8) for k in range(4)]
    return lax.ppermute(block, ("fsdp", "ctx"), pairs)


def project(pieces, other, weight, after=()):
    groups, depth, channels = weight.shape
    part = pieces[0].shape[0]
    length = 2 * part
    width = channels // 4

    def body(first, second, weight, *refs):
        own, far, give, give_far, held, product = refs[len(after) :]
        me = lax.axis_index("ctx")
        core = (me ^ lax.axis_index("fsdp")) & 1 if other else me & 1
        held[block_at(core, part), :] = first[...]
        held[block_at(1 - core, part), :] = second[...]
        for j in range(groups):
            product[...] = dot(held[...], weight[j], (1, 0))
            own[j] = product[:, block_at(me, width)]
            far[j] = product[:, block_at(me ^ 2, width)].astype(BF16)
            give[j] = product[:, block_at(me ^ 1, width)].astype(BF16)
            give_far[j] = product[:, block_at(me ^ 3, width)].astype(BF16)

    sums = jax.ShapeDtypeStruct((groups, length, width), BF16)
    return call(
        body,
        (jax.ShapeDtypeStruct((groups, length, width), F32), sums, sums, sums),
        [pltpu.VMEM((length, depth), BF16), pltpu.VMEM((length, channels), F32)],
        in_specs=[VMEM] * 3 + [HBM] * len(after),
        us=0.45 * groups,
    )(*pieces, weight, *after)


def add_far(left, right):
    def body(left, right, out):
        out[...] = (left[...].astype(F32) + right[...].astype(F32)).astype(BF16)

    return call(body, jax.ShapeDtypeStruct(left.shape, BF16), limit=SMALL_LIMIT)(left, right)


def channel_sums(pieces, other, weight, after=()):
    own, far, give, give_far = project(pieces, other, weight, after)
    passed = add_far(far, flipped(give_far, "ctx", 1))
    return (own, flipped(give, "ctx", 1), flipped(passed, "ctx", 2)), passed


def by_token(here, there):
    return here[0], here[1], there[2], there[0], there[1], here[2]


def all_channels(value, far):
    return value, far, flipped(value, "ctx", 1), flipped(far, "ctx", 1)


def output_pieces(gathered, weight, after=()):
    groups, length, width = gathered[0].shape
    piece = weight.shape[1] // 4
    part = length // 4
    channels = 4 * width

    def product(whole, weight, at, index):
        total = None
        for j in range(groups):
            term = dot(whole[j, at, :], weight[j, block_at(index, piece), :], (1, 1))
            total = term if total is None else total + term
        return total.astype(BF16)

    def pieces(whole, weight, side, low, first, second):
        first[...] = product(whole, weight, slice(None), 2 * side)
        for high in range(2):
            rows = slice(high * part, (high + 1) * part)
            for s in range(2):
                columns = slice(s * piece, (s + 1) * piece)
                second[rows, columns] = product(whole, weight, block_at(2 * high + low, part), 2 * s + 1)

    def first_body(own, far, near, near_far, weight, *refs):
        whole, first, second = refs[len(after) :]
        me = lax.axis_index("ctx")
        place = lax.axis_index("fsdp")
        for j in range(groups):
            for mask, value in ((0, own), (2, far), (1, near), (3, near_far)):
                whole[j, :, block_at(me ^ mask, width)] = value[j]
        pieces(whole, weight, 1 - (place & 1), 1 - ((place >> 1) & 1), first, second)

    def second_body(whole, weight, first, second):
        place = lax.axis_index("fsdp")
        pieces(whole, weight, place & 1, (place >> 1) & 1, first, second)

    parts = (jax.ShapeDtypeStruct((length, piece), BF16), jax.ShapeDtypeStruct((2 * part, 2 * piece), BF16))
    whole, *gives = call(
        first_body,
        (jax.ShapeDtypeStruct((groups, length, channels), BF16), *parts),
        in_specs=[VMEM] * 5 + [HBM] * len(after),
        us=0.6 * groups,
    )(*gathered, weight, *after)
    keeps = call(second_body, parts, us=0.4 * groups)(whole, weight)
    return whole, keeps, gives


def exchange(gives):
    return flipped(gives[0], "fsdp", 1), flipped(gives[1], "fsdp", 2)


def final_pairs(flip):
    pairs = []
    for f in range(8):
        for k in range(4):
            high, low, x, y, core = f >> 2, (f >> 1) & 1, f & 1, k >> 1, k & 1
            pairs.append((4 * f + k, 4 * (4 * (y ^ high ^ flip) + 2 * core + x) + 2 * y + low))
    return pairs


def block_sums(keeps, givens, after=(), after_second=()):
    length, piece = keeps[0].shape
    part = length // 4
    both = lambda keep, given, rows, columns: keep[rows, columns].astype(F32) + given[rows, columns].astype(F32)

    def second_body(keep_x, given_x, keep_z, given_z, *refs):
        give_z, give_x, next_z, next_x = refs[len(after) :]
        place = lax.axis_index("fsdp")
        side, low = place & 1, (place >> 1) & 1
        for high in range(2):
            rows = slice(high * part, (high + 1) * part)
            take = lambda bit: both(keep_x, given_x, block_at(2 * high + bit, part), slice(None))
            give_z[rows, :] = take(1 - low).astype(BF16)
            next_z[rows, :] = take(low)
        take = lambda bit: both(keep_z, given_z, slice(None), block_at(bit, piece))
        give_x[...] = take(1 - side).astype(BF16)
        next_x[...] = take(side)

    square = lambda kind: jax.ShapeDtypeStruct((2 * part, piece), kind)
    give_z, give_x, next_z, next_x = call(
        second_body,
        (square(BF16), square(BF16), square(F32), square(F32)),
        in_specs=[VMEM] * 4 + [HBM] * len(after),
        limit=SMALL_LIMIT,
    )(keeps[0], givens[0], keeps[1], givens[1], *after)

    def third_body(keep_z, given_z, keep_x, given_x, *refs):
        give, keep = refs[len(after_second) :]
        y = lax.axis_index("ctx") >> 1
        for bit, out in ((1 - y, give), (y, keep)):
            at = block_at(bit, part)
            for half, (mine, other) in enumerate(((keep_z, given_z), (keep_x, given_x))):
                columns = slice(half * piece, (half + 1) * piece)
                out[:, columns] = both(mine, other, at, slice(None)).astype(BF16)

    block = jax.ShapeDtypeStruct((part, 2 * piece), BF16)
    give, keep = call(third_body, (block, block), in_specs=[VMEM] * 4 + [HBM] * len(after_second), limit=SMALL_LIMIT)(
        next_z, flipped(give_z, "fsdp", 2), next_x, flipped(give_x, "fsdp", 1), *after_second
    )

    def order_body(keep, given, first, second):
        high = lax.axis_index("fsdp") >> 2
        swap = high == 1
        first[...] = jnp.where(swap, given[...].astype(F32), keep[...].astype(F32)).astype(BF16)
        second[...] = jnp.where(swap, keep[...].astype(F32), given[...].astype(F32)).astype(BF16)

    blocks = call(order_body, (block, block), limit=SMALL_LIMIT)(keep, flipped(give, "ctx", 2))
    arrived = [lax.ppermute(value, ("fsdp", "ctx"), final_pairs(flip)) for flip, value in enumerate(blocks)]

    def last_body(first, second, out):
        out[...] = (first[...].astype(F32) + second[...].astype(F32)).astype(BF16)

    return call(last_body, block, limit=SMALL_LIMIT)(*arrived), give


def turned(pieces):
    part, depth = pieces[0].shape

    def body(a, b, c, d, out):
        me = lax.axis_index("ctx")
        side = lax.axis_index("fsdp") & 1
        for mask, piece in ((0, a), (1, b), (2 ^ side, c), (3 ^ side, d)):
            out[:, block_at(me ^ mask, part)] = piece[...].T

    return call(body, jax.ShapeDtypeStruct((depth, 4 * part), pieces[0].dtype), us=0.4, limit=SMALL_LIMIT)(*pieces)


def weight_gradient(rows, values, after=()):
    depth, length = rows.shape
    groups, _, channels = values.shape
    tile = depth // 2

    def body(rows, values, *refs):
        out, mark = refs[len(after) :]
        out[0] = dot(rows[...], values[0], (1, 0))
        mark[...] = jnp.zeros_like(mark)

    return pl.pallas_call(
        body,
        out_shape=(jax.ShapeDtypeStruct((groups, depth, channels), F32), jax.ShapeDtypeStruct((8, LANES), F32)),
        grid=(groups, depth // tile),
        in_specs=[
            pl.BlockSpec((tile, length), lambda j, i: (i, 0)),
            pl.BlockSpec((1, length, channels), lambda j, i: (j, 0, 0)),
        ]
        + [HBM] * len(after),
        out_specs=(pl.BlockSpec((1, tile, channels), lambda j, i: (j, i, 0)), pl.BlockSpec((8, LANES), lambda j, i: (0, 0))),
        compiler_params=pltpu.CompilerParams(vmem_limit_bytes=VMEM_LIMIT),
        cost_estimate=cost(1.5 * groups),
    )(rows, values, *after)


def four_by_eight(tokens, weights, tables, out_weight, grad_mixed):
    length, width = 4 * tokens.shape[0], weights.shape[2] // 4
    own, near, far = column_blocks(tokens)
    weights, out_weight = loaded((weights, out_weight), near)
    here = (own, flipped(near, "ctx", 1))
    feats_here, passed = channel_sums(here, 0, weights)
    far = later(fetched(far), passed)
    there = (far, flipped(far, "fsdp", 1))
    grad_own, grad_near, grad_far = column_blocks(grad_mixed)
    grad_here = (grad_own, flipped(grad_near, "ctx", 1))
    grad_far = fetched(later(grad_far, feats_here[2]))
    grad_there = (grad_far, flipped(grad_far, "fsdp", 1))
    feats_there, _ = channel_sums(there, 1, weights)
    grads_here, _ = channel_sums(grad_here, 0, out_weight[None])
    *saved, gated = filter_forward(by_token(feats_here, feats_there), sum_of_three, tables, length, width)
    grads_there, _ = channel_sums(grad_there, 1, out_weight[None], (gated,))
    gated = gated[None]
    gated_far = flipped(gated, "ctx", 2)
    all_gated = all_channels(gated, gated_far)
    whole_gated, keeps, gives = output_pieces(all_gated, out_weight[None])
    givens = exchange(gives)
    mixed_halves = keeps, givens
    grads = filter_backward(by_token(grads_here, grads_there), sum_of_three, tables, saved, length, width)
    grads = later(grads, gated_far)
    grad_out, mark = weight_gradient(turned(grad_here + grad_there), whole_gated)
    token_rows = turned(here + there)
    grads_far = later(flipped(grads, "ctx", 2), *givens, keeps[0], token_rows, mark)
    whole_grads, keeps, gives = output_pieces(all_channels(grads, grads_far), weights)
    mixed, mixed_give = block_sums(*mixed_halves, (), gives[:1])
    grad_in, mark = weight_gradient(token_rows, whole_grads, (mixed_give,))
    grad_tokens, _ = block_sums(keeps, exchange(gives), (mark,))
    return mixed, grad_tokens, grad_in, grad_out[0]


def any_mesh(tokens, weights, tables, out_weight, grad_mixed):
    count = lax.axis_size("ctx")
    columns = lambda rows: lax.all_to_all(rows, "ctx", split_axis=1, concat_axis=0, tiled=True)
    whole_tokens, whole_cotangents = columns(tokens), columns(grad_mixed)
    length, width = whole_tokens.shape[0], weights.shape[2] // count

    def channel_sums(rows, weight):
        partial = jnp.einsum("td,jdc->jtc", rows, weight, preferred_element_type=F32)
        return lax.psum_scatter(partial.astype(BF16), "ctx", scatter_dimension=2, tiled=True)

    def block_sums(values, weight):
        partial = jnp.einsum("jtc,jdc->td", values, weight, preferred_element_type=F32)
        ratio = lax.axis_size("fsdp") // count
        pieces = partial.astype(BF16).reshape(count, length // count, ratio, -1).transpose(0, 2, 1, 3)
        pieces = pieces.reshape(count * ratio, length // count, -1)
        return to_placement(lax.psum_scatter(pieces, "fsdp", scatter_dimension=0, tiled=True)[0])

    feats = channel_sums(whole_tokens, weights)
    grad_gated = channel_sums(whole_cotangents, out_weight[None])
    *saved, gated = filter_forward((feats,), plain, tables, length, width)
    grads = filter_backward((grad_gated,), plain, tables, saved, length, width)
    whole_gated = lax.all_gather(gated, "ctx", axis=1, tiled=True)
    whole_grads = lax.all_gather(grads, "ctx", axis=2, tiled=True)
    mixed = block_sums(whole_gated[None], out_weight[None])
    grad_tokens = block_sums(whole_grads, weights)
    grad_in = jnp.einsum("td,jtc->jdc", whole_tokens, whole_grads, preferred_element_type=F32)
    grad_out = jnp.einsum("td,tc->dc", whole_cotangents, whole_gated, preferred_element_type=F32)
    return mixed, grad_tokens, grad_in, grad_out


def per_device(tokens, in_weight, conv_taps, decay_rate, residue, skip_gain, out_weight, grad_mixed):
    count, blocks = lax.axis_size("ctx"), lax.axis_size("fsdp")
    weights = in_weight.transpose(1, 0, 2)
    length = count * tokens.shape[0]
    width = weights.shape[2] // count
    mine = lambda table: lax.dynamic_slice_in_dim(table, lax.axis_index("ctx") * width, width, table.ndim - 1)
    rate = mine(decay_rate)
    gain = mine(residue) * jnp.sqrt(-jnp.expm1(-2.0 * rate))
    tables = (mine(conv_taps.transpose(1, 0, 2)), jnp.exp(-rate), jnp.exp(-rate * (length // CHUNKS)), gain, mine(skip_gain[None]))
    tuned = count == 4 and blocks == 8 and width % LANES == 0 and tokens.shape[0] % LANES == 0
    plan = four_by_eight if tuned else any_mesh
    mixed, grad_tokens, grad_in, grad_out = plan(tokens, weights, tables, out_weight, grad_mixed)
    return mixed, grad_tokens, grad_in.transpose(1, 0, 2), grad_out


def solution(mesh):
    return jax.shard_map(
        per_device,
        mesh=mesh,
        in_specs=(
            P("ctx", None),
            P("ctx", None, "fsdp"),
            P(None, None, "fsdp"),
            P(None, "fsdp"),
            P(None, "fsdp"),
            P("fsdp"),
            P("ctx", "fsdp"),
            P("ctx", None),
        ),
        out_specs=(P("ctx", "fsdp"), P("ctx", "fsdp"), P("ctx", None, "fsdp"), P("ctx", "fsdp")),
        check_vma=False,
    )
```

```python
import functools

import jax
import jax.numpy as jnp
from jax import lax
from jax.experimental import pallas as pl
from jax.experimental.pallas import tpu as pltpu
from jax.sharding import PartitionSpec as P

BF16 = jnp.bfloat16
F32 = jnp.float32
LANES = 128
CHUNKS = 8
MARGIN = 8
VMEM_LIMIT = 12 * 1024 * 1024
SMALL_LIMIT = 4 * 1024 * 1024
FLOPS_PER_US = 1_150_000_000


VMEM = pl.BlockSpec(memory_space=pltpu.VMEM)
HBM = pl.BlockSpec(memory_space=pl.ANY)


def cost(us):
    return pl.CostEstimate(flops=int(us * FLOPS_PER_US), bytes_accessed=0, transcendentals=0)


def call(body, outs, scratch=(), in_specs=None, us=0.5, limit=VMEM_LIMIT):
    return pl.pallas_call(
        body,
        out_shape=outs,
        **({} if in_specs is None else {"in_specs": in_specs}),
        scratch_shapes=list(scratch),
        compiler_params=pltpu.CompilerParams(vmem_limit_bytes=limit),
        cost_estimate=cost(us),
    )


def flipped(value, axis, mask):
    count = lax.axis_size(axis)
    return lax.ppermute(value, axis, [(source, source ^ mask) for source in range(count)])


def block_at(index, size):
    return pl.ds(pl.multiple_of(index * size, size), size)


def to_placement(value):
    count = lax.axis_size("ctx")
    ratio = lax.axis_size("fsdp") // count
    pairs = []
    for f in range(ratio * count):
        for k in range(count):
            target = (k * ratio + f % ratio, f // ratio)
            pairs.append((f * count + k, target[0] * count + target[1]))
    return lax.ppermute(value, ("fsdp", "ctx"), pairs)


def dot(left, right, contract):
    return lax.dot_general(left, right, ((contract[:1], contract[1:]), ((), ())), preferred_element_type=F32)


def shifted(value, steps, backward):
    rows = lax.broadcasted_iota(jnp.int32, value.shape, 0)
    if backward:
        return jnp.where(rows < CHUNKS - steps, pltpu.roll(value, CHUNKS - steps, 0), 0.0)
    return jnp.where(rows >= steps, pltpu.roll(value, steps, 0), 0.0)


def modal_scan(source, target, decay, spread, gain, backward):
    poles, width = decay.shape
    steps = source.shape[0] // CHUNKS
    wide = lambda table, n: jnp.broadcast_to(table[n : n + 1, :], (CHUNKS, width))
    decays = [wide(decay, n) for n in range(poles)]

    def rows(i):
        return pl.ds(steps - 1 - i if backward else i, CHUNKS, stride=steps)

    def gather_up(i, states):
        entry = source[rows(i), :]
        return tuple(d * s + entry for d, s in zip(decays, states))

    zero = jnp.zeros((CHUNKS, width), F32)
    ends = lax.fori_loop(0, steps, gather_up, (zero,) * poles, unroll=4)
    states = []
    for n in range(poles):
        factor = wide(spread, n)
        state = shifted(ends[n], 1, backward)
        reach = 1
        while reach < CHUNKS:
            state = state + factor * shifted(state, reach, backward)
            factor = factor * factor
            reach *= 2
        states.append(state)
    gains = [wide(gain, n) for n in range(poles)]

    def advance(i, states):
        entry = source[rows(i), :]
        states = tuple(d * s + entry for d, s in zip(decays, states))
        terms = [g * s for g, s in zip(gains, states)]
        while len(terms) > 1:
            terms = [a + b for a, b in zip(terms[::2], terms[1::2])]
        target[rows(i), :] = terms[0]
        return states

    lax.fori_loop(0, steps, advance, tuple(states), unroll=2)


def row_blocks(length):
    size = 64 if length % 64 == 0 else length
    return [(start, size) for start in range(0, length, size)]


def forward_body(parts, kinds, taps, decay, spread, gain, skip, query, key, value, long_out, gated, feats, signal, summed):
    length, width = query.shape
    blocks = row_blocks(length)
    for j in range(3):
        feats[j, :MARGIN, :] = jnp.zeros((MARGIN, width), F32)
        for start, size in blocks:
            row, total = kinds(parts, j, start, size)
            feats[j, pl.ds(MARGIN + row, size), :] = total.astype(BF16).astype(F32)
    for start, size in blocks:
        mixed = []
        for j in range(3):
            total = taps[j, 0:1, :] * feats[j, MARGIN + start : MARGIN + start + size, :]
            for lag in range(1, taps.shape[1]):
                first = MARGIN + start - lag
                total = total + taps[j, lag : lag + 1, :] * feats[j, first : first + size, :]
            mixed.append(total)
        at = slice(start, start + size)
        query[at, :], key[at, :], value[at, :] = mixed
        signal[at, :] = mixed[1] * mixed[2]
    modal_scan(signal, summed, decay[...], spread[...], gain[...], False)
    for start, size in blocks:
        at = slice(start, start + size)
        result = summed[at, :] + skip[...] * signal[at, :]
        long_out[at, :] = result
        gated[at, :] = (query[at, :] * result).astype(BF16)


def backward_body(parts, kinds, taps, decay, spread, gain, skip, query, key, value, long_out, grads, mixin, grad_long, summed):
    length, width = query.shape
    blocks = row_blocks(length)
    for start, size in blocks:
        row, grad_gated = kinds(parts, 0, start, size)
        at = pl.ds(row, size)
        mixin[0, at, :] = grad_gated * long_out[at, :]
        grad_long[at, :] = grad_gated * query[at, :]
    modal_scan(grad_long, summed, decay[...], spread[...], gain[...], True)
    for start, size in blocks:
        at = slice(start, start + size)
        grad_signal = summed[at, :] + skip[...] * grad_long[at, :]
        mixin[1, at, :] = grad_signal * value[at, :]
        mixin[2, at, :] = grad_signal * key[at, :]
    for j in range(3):
        mixin[j, length : length + MARGIN, :] = jnp.zeros((MARGIN, width), F32)
        for start, size in blocks:
            total = taps[j, 0:1, :] * mixin[j, start : start + size, :]
            for lag in range(1, taps.shape[1]):
                total = total + taps[j, lag : lag + 1, :] * mixin[j, start + lag : start + lag + size, :]
            grads[j, start : start + size, :] = total.astype(BF16)


def sum_of_three(parts, j, start, size):
    half = parts[0].shape[1]
    other, local = divmod(start, half)
    own, near, far = parts[3 * other : 3 * other + 3]
    at = slice(local, local + size)
    total = own[j, at, :] + near[j, at, :].astype(F32) + far[j, at, :].astype(F32)
    return pl.multiple_of(((lax.axis_index("ctx") >> 1) ^ other) * half + local, MARGIN), total


def plain(parts, j, start, size):
    return start, parts[0][j, start : start + size, :].astype(F32)


def filter_forward(parts, kinds, tables, length, width, after=()):
    count = len(parts)
    inputs = count + len(tables)

    def body(*refs):
        forward_body(refs[:count], kinds, *refs[count:inputs], *refs[inputs + len(after) :])

    wide = jax.ShapeDtypeStruct((length, width), F32)
    return call(
        body,
        (wide, wide, wide, wide, jax.ShapeDtypeStruct((length, width), BF16)),
        [
            pltpu.VMEM((3, MARGIN + length, width), F32),
            pltpu.VMEM((length, width), F32),
            pltpu.VMEM((length, width), F32),
        ],
        in_specs=[VMEM] * inputs + [HBM] * len(after),
        us=2.1,
    )(*parts, *tables, *after)


def filter_backward(parts, kinds, tables, saved, length, width, after=()):
    count = len(parts)
    inputs = count + len(tables) + len(saved)

    def body(*refs):
        backward_body(refs[:count], kinds, *refs[count:inputs], *refs[inputs + len(after) :])

    return call(
        body,
        jax.ShapeDtypeStruct((3, length, width), BF16),
        [
            pltpu.VMEM((3, length + MARGIN, width), F32),
            pltpu.VMEM((length, width), F32),
            pltpu.VMEM((length, width), F32),
        ],
        in_specs=[VMEM] * inputs + [HBM] * len(after),
        us=2.1,
    )(*parts, *tables, *saved, *after)


def later(value, *after):
    def body(*refs):
        pass

    return pl.pallas_call(
        body,
        out_shape=jax.ShapeDtypeStruct(value.shape, value.dtype),
        in_specs=[HBM] * (1 + len(after)),
        out_specs=HBM,
        input_output_aliases={0: 0},
        compiler_params=pltpu.CompilerParams(vmem_limit_bytes=SMALL_LIMIT),
        cost_estimate=cost(0.05),
    )(value, *after)


def loaded(values, after):
    count = len(values)

    def body(*refs):
        sources, outs, arrived = refs[:count], refs[count + 1 : 2 * count + 1], refs[-1]
        copies = [pltpu.make_async_copy(a, b, arrived.at[n]) for n, (a, b) in enumerate(zip(sources, outs))]
        for copy in copies:
            copy.start()
        for copy in copies:
            copy.wait()

    return pl.pallas_call(
        body,
        out_shape=tuple(pltpu.VMEM(value.shape, value.dtype) for value in values),
        in_specs=[HBM] * (count + 1),
        out_specs=(VMEM,) * count,
        scratch_shapes=[pltpu.SemaphoreType.DMA((count,))],
        compiler_params=pltpu.CompilerParams(vmem_limit_bytes=SMALL_LIMIT),
        cost_estimate=cost(1.3),
    )(*[pltpu.with_memory_space_constraint(value, pltpu.HBM) for value in values], after)


def column_blocks(rows):
    length, width = rows.shape[0], rows.shape[1] // 4

    def body(rows, own, near, far, arrived):
        me = lax.axis_index("ctx")
        side = lax.axis_index("fsdp") & 1
        copies = []
        for n, (mask, out) in enumerate(((2 ^ side, far), (1, near), (0, own))):
            copies.append(pltpu.make_async_copy(rows.at[:, block_at(me ^ mask, width)], out, arrived.at[n]))
            copies[-1].start()
        for copy in copies:
            copy.wait()

    block = jax.ShapeDtypeStruct((length, width), rows.dtype)
    return call(body, (block,) * 3, [pltpu.SemaphoreType.DMA((3,))], in_specs=[HBM], us=0.7, limit=SMALL_LIMIT)(
        pltpu.with_memory_space_constraint(rows, pltpu.HBM)
    )


def fetched(block):
    pairs = [(4 * f + k, 4 * f + (k ^ 2 ^ (f & 1))) for f in range(8) for k in range(4)]
    return lax.ppermute(block, ("fsdp", "ctx"), pairs)


def project(pieces, other, weight, after=()):
    groups, depth, channels = weight.shape
    part = pieces[0].shape[0]
    length = 2 * part
    width = channels // 4

    def body(first, second, weight, *refs):
        own, far, give, give_far, held, product = refs[len(after) :]
        me = lax.axis_index("ctx")
        core = (me ^ lax.axis_index("fsdp")) & 1 if other else me & 1
        held[block_at(core, part), :] = first[...]
        held[block_at(1 - core, part), :] = second[...]
        for j in range(groups):
            product[...] = dot(held[...], weight[j], (1, 0))
            own[j] = product[:, block_at(me, width)]
            far[j] = product[:, block_at(me ^ 2, width)].astype(BF16)
            give[j] = product[:, block_at(me ^ 1, width)].astype(BF16)
            give_far[j] = product[:, block_at(me ^ 3, width)].astype(BF16)

    sums = jax.ShapeDtypeStruct((groups, length, width), BF16)
    return call(
        body,
        (jax.ShapeDtypeStruct((groups, length, width), F32), sums, sums, sums),
        [pltpu.VMEM((length, depth), BF16), pltpu.VMEM((length, channels), F32)],
        in_specs=[VMEM] * 3 + [HBM] * len(after),
        us=0.45 * groups,
    )(*pieces, weight, *after)


def add_far(left, right):
    def body(left, right, out):
        out[...] = (left[...].astype(F32) + right[...].astype(F32)).astype(BF16)

    return call(body, jax.ShapeDtypeStruct(left.shape, BF16), limit=SMALL_LIMIT)(left, right)


def channel_sums(pieces, other, weight, after=()):
    own, far, give, give_far = project(pieces, other, weight, after)
    passed = add_far(far, flipped(give_far, "ctx", 1))
    return (own, flipped(give, "ctx", 1), flipped(passed, "ctx", 2)), passed


def by_token(here, there):
    return here[0], here[1], there[2], there[0], there[1], here[2]


def all_channels(value, far):
    return value, far, flipped(value, "ctx", 1), flipped(far, "ctx", 1)


def output_pieces(gathered, weight, after=()):
    groups, length, width = gathered[0].shape
    piece = weight.shape[1] // 4
    part = length // 4
    channels = 4 * width

    def product(whole, weight, at, index):
        total = None
        for j in range(groups):
            term = dot(whole[j, at, :], weight[j, block_at(index, piece), :], (1, 1))
            total = term if total is None else total + term
        return total.astype(BF16)

    def pieces(whole, weight, side, low, first, second):
        first[...] = product(whole, weight, slice(None), 2 * side)
        for high in range(2):
            rows = slice(high * part, (high + 1) * part)
            for s in range(2):
                columns = slice(s * piece, (s + 1) * piece)
                second[rows, columns] = product(whole, weight, block_at(2 * high + low, part), 2 * s + 1)

    def first_body(own, far, near, near_far, weight, *refs):
        whole, first, second = refs[len(after) :]
        me = lax.axis_index("ctx")
        place = lax.axis_index("fsdp")
        for j in range(groups):
            for mask, value in ((0, own), (2, far), (1, near), (3, near_far)):
                whole[j, :, block_at(me ^ mask, width)] = value[j]
        pieces(whole, weight, 1 - (place & 1), 1 - ((place >> 1) & 1), first, second)

    def second_body(whole, weight, first, second):
        place = lax.axis_index("fsdp")
        pieces(whole, weight, place & 1, (place >> 1) & 1, first, second)

    parts = (jax.ShapeDtypeStruct((length, piece), BF16), jax.ShapeDtypeStruct((2 * part, 2 * piece), BF16))
    whole, *gives = call(
        first_body,
        (jax.ShapeDtypeStruct((groups, length, channels), BF16), *parts),
        in_specs=[VMEM] * 5 + [HBM] * len(after),
        us=0.6 * groups,
    )(*gathered, weight, *after)
    keeps = call(second_body, parts, us=0.4 * groups)(whole, weight)
    return whole, keeps, gives


def exchange(gives):
    return flipped(gives[0], "fsdp", 1), flipped(gives[1], "fsdp", 2)


def final_pairs(flip):
    pairs = []
    for f in range(8):
        for k in range(4):
            high, low, x, y, core = f >> 2, (f >> 1) & 1, f & 1, k >> 1, k & 1
            pairs.append((4 * f + k, 4 * (4 * (y ^ high ^ flip) + 2 * core + x) + 2 * y + low))
    return pairs


def block_sums(keeps, givens, after=(), after_second=()):
    length, piece = keeps[0].shape
    part = length // 4
    both = lambda keep, given, rows, columns: keep[rows, columns].astype(F32) + given[rows, columns].astype(F32)

    def second_body(keep_x, given_x, keep_z, given_z, *refs):
        give_z, give_x, next_z, next_x = refs[len(after) :]
        place = lax.axis_index("fsdp")
        side, low = place & 1, (place >> 1) & 1
        for high in range(2):
            rows = slice(high * part, (high + 1) * part)
            take = lambda bit: both(keep_x, given_x, block_at(2 * high + bit, part), slice(None))
            give_z[rows, :] = take(1 - low).astype(BF16)
            next_z[rows, :] = take(low)
        take = lambda bit: both(keep_z, given_z, slice(None), block_at(bit, piece))
        give_x[...] = take(1 - side).astype(BF16)
        next_x[...] = take(side)

    square = lambda kind: jax.ShapeDtypeStruct((2 * part, piece), kind)
    give_z, give_x, next_z, next_x = call(
        second_body,
        (square(BF16), square(BF16), square(F32), square(F32)),
        in_specs=[VMEM] * 4 + [HBM] * len(after),
        limit=SMALL_LIMIT,
    )(keeps[0], givens[0], keeps[1], givens[1], *after)

    def third_body(keep_z, given_z, keep_x, given_x, *refs):
        give, keep = refs[len(after_second) :]
        y = lax.axis_index("ctx") >> 1
        for bit, out in ((1 - y, give), (y, keep)):
            at = block_at(bit, part)
            for half, (mine, other) in enumerate(((keep_z, given_z), (keep_x, given_x))):
                columns = slice(half * piece, (half + 1) * piece)
                out[:, columns] = both(mine, other, at, slice(None)).astype(BF16)

    block = jax.ShapeDtypeStruct((part, 2 * piece), BF16)
    give, keep = call(third_body, (block, block), in_specs=[VMEM] * 4 + [HBM] * len(after_second), limit=SMALL_LIMIT)(
        next_z, flipped(give_z, "fsdp", 2), next_x, flipped(give_x, "fsdp", 1), *after_second
    )

    def order_body(keep, given, first, second):
        high = lax.axis_index("fsdp") >> 2
        swap = high == 1
        first[...] = jnp.where(swap, given[...].astype(F32), keep[...].astype(F32)).astype(BF16)
        second[...] = jnp.where(swap, keep[...].astype(F32), given[...].astype(F32)).astype(BF16)

    blocks = call(order_body, (block, block), limit=SMALL_LIMIT)(keep, flipped(give, "ctx", 2))
    arrived = [lax.ppermute(value, ("fsdp", "ctx"), final_pairs(flip)) for flip, value in enumerate(blocks)]

    def last_body(first, second, out):
        out[...] = (first[...].astype(F32) + second[...].astype(F32)).astype(BF16)

    return call(last_body, block, limit=SMALL_LIMIT)(*arrived), blocks[0]


def turned(pieces):
    part, depth = pieces[0].shape

    def body(a, b, c, d, out):
        me = lax.axis_index("ctx")
        side = lax.axis_index("fsdp") & 1
        for mask, piece in ((0, a), (1, b), (2 ^ side, c), (3 ^ side, d)):
            out[:, block_at(me ^ mask, part)] = piece[...].T

    return call(body, jax.ShapeDtypeStruct((depth, 4 * part), pieces[0].dtype), us=0.4, limit=SMALL_LIMIT)(*pieces)


def weight_gradient(rows, values, after=()):
    depth, length = rows.shape
    groups, _, channels = values.shape
    tile = 256
    steps = [(j, i) for j in range(groups) for i in range(depth // tile)]

    def body(rows, values, *refs):
        out, mark, ready, written = refs[len(after) :]
        copies = []
        for n, (j, i) in enumerate(steps):
            at = slice(i * tile, (i + 1) * tile)
            ready[j, at, :] = dot(rows[at, :], values[j], (1, 0))
            copies.append(pltpu.make_async_copy(ready.at[j, at, :], out.at[j, at, :], written.at[n]))
            copies[-1].start()
        mark[...] = jnp.zeros_like(mark)
        for copy in copies:
            copy.wait()

    gradient = jax.ShapeDtypeStruct((groups, depth, channels), F32)
    return pl.pallas_call(
        body,
        out_shape=(gradient, jax.ShapeDtypeStruct((8, LANES), F32)),
        in_specs=[VMEM] * 2 + [HBM] * len(after),
        out_specs=(HBM, VMEM),
        scratch_shapes=[pltpu.VMEM(gradient.shape, F32), pltpu.SemaphoreType.DMA((len(steps),))],
        compiler_params=pltpu.CompilerParams(vmem_limit_bytes=VMEM_LIMIT),
        cost_estimate=cost(1.0 * groups),
    )(rows, values, *after)


def four_by_eight(tokens, weights, tables, out_weight, grad_mixed):
    length, width = 4 * tokens.shape[0], weights.shape[2] // 4
    own, near, far = column_blocks(tokens)
    (weights,) = loaded((weights,), near)
    here = (own, flipped(near, "ctx", 1))
    feats_here, passed = channel_sums(here, 0, weights)
    far = later(fetched(far), passed)
    there = (far, flipped(far, "fsdp", 1))
    grad_own, grad_near, grad_far = column_blocks(grad_mixed)
    grad_here = (grad_own, flipped(grad_near, "ctx", 1))
    grad_far = fetched(later(grad_far, far))
    grad_there = (grad_far, flipped(grad_far, "fsdp", 1))
    feats_there, _ = channel_sums(there, 1, weights, feats_here[2:])
    grads_here, _ = channel_sums(grad_here, 0, out_weight[None])
    grads_there, passed_there = channel_sums(grad_there, 1, out_weight[None])
    feats = by_token(feats_here, feats_there)
    *saved, gated = filter_forward(feats, sum_of_three, tables, length, width, (grads_here[2], passed_there))
    gated = gated[None]
    gated_far = flipped(gated, "ctx", 2)
    all_gated = all_channels(gated, gated_far)
    whole_gated, keeps, gives = output_pieces(all_gated, out_weight[None])
    givens = exchange(gives)
    mixed_halves = keeps, givens
    grads = filter_backward(by_token(grads_here, grads_there), sum_of_three, tables, saved, length, width)
    grads = later(grads, gated_far)
    grad_out, mark = weight_gradient(turned(grad_here + grad_there), whole_gated)
    token_rows = turned(here + there)
    grads_far = later(flipped(grads, "ctx", 2), *givens, keeps[0], token_rows, mark)
    whole_grads, keeps, gives = output_pieces(all_channels(grads, grads_far), weights)
    mixed, mixed_block = block_sums(*mixed_halves, (), gives[:1])
    grad_in, mark = weight_gradient(token_rows, whole_grads, (mixed_block,))
    grad_tokens, _ = block_sums(keeps, exchange(gives), (mark,))
    return mixed, grad_tokens, grad_in, grad_out[0]


def any_mesh(tokens, weights, tables, out_weight, grad_mixed):
    count = lax.axis_size("ctx")
    columns = lambda rows: lax.all_to_all(rows, "ctx", split_axis=1, concat_axis=0, tiled=True)
    whole_tokens, whole_cotangents = columns(tokens), columns(grad_mixed)
    length, width = whole_tokens.shape[0], weights.shape[2] // count

    def channel_sums(rows, weight):
        partial = jnp.einsum("td,jdc->jtc", rows, weight, preferred_element_type=F32)
        return lax.psum_scatter(partial.astype(BF16), "ctx", scatter_dimension=2, tiled=True)

    def block_sums(values, weight):
        partial = jnp.einsum("jtc,jdc->td", values, weight, preferred_element_type=F32)
        ratio = lax.axis_size("fsdp") // count
        pieces = partial.astype(BF16).reshape(count, length // count, ratio, -1).transpose(0, 2, 1, 3)
        pieces = pieces.reshape(count * ratio, length // count, -1)
        return to_placement(lax.psum_scatter(pieces, "fsdp", scatter_dimension=0, tiled=True)[0])

    feats = channel_sums(whole_tokens, weights)
    grad_gated = channel_sums(whole_cotangents, out_weight[None])
    *saved, gated = filter_forward((feats,), plain, tables, length, width)
    grads = filter_backward((grad_gated,), plain, tables, saved, length, width)
    whole_gated = lax.all_gather(gated, "ctx", axis=1, tiled=True)
    whole_grads = lax.all_gather(grads, "ctx", axis=2, tiled=True)
    mixed = block_sums(whole_gated[None], out_weight[None])
    grad_tokens = block_sums(whole_grads, weights)
    grad_in = jnp.einsum("td,jtc->jdc", whole_tokens, whole_grads, preferred_element_type=F32)
    grad_out = jnp.einsum("td,tc->dc", whole_cotangents, whole_gated, preferred_element_type=F32)
    return mixed, grad_tokens, grad_in, grad_out


def per_device(tokens, in_weight, conv_taps, decay_rate, residue, skip_gain, out_weight, grad_mixed):
    count, blocks = lax.axis_size("ctx"), lax.axis_size("fsdp")
    weights = in_weight.transpose(1, 0, 2)
    length = count * tokens.shape[0]
    width = weights.shape[2] // count
    mine = lambda table: lax.dynamic_slice_in_dim(table, lax.axis_index("ctx") * width, width, table.ndim - 1)
    rate = mine(decay_rate)
    gain = mine(residue) * jnp.sqrt(-jnp.expm1(-2.0 * rate))
    tables = (mine(conv_taps.transpose(1, 0, 2)), jnp.exp(-rate), jnp.exp(-rate * (length // CHUNKS)), gain, mine(skip_gain[None]))
    tuned = count == 4 and blocks == 8 and width % LANES == 0 and tokens.shape[0] % LANES == 0
    plan = four_by_eight if tuned else any_mesh
    mixed, grad_tokens, grad_in, grad_out = plan(tokens, weights, tables, out_weight, grad_mixed)
    return mixed, grad_tokens, grad_in.transpose(1, 0, 2), grad_out


def solution(mesh):
    return jax.shard_map(
        per_device,
        mesh=mesh,
        in_specs=(
            P("ctx", None),
            P("ctx", None, "fsdp"),
            P(None, None, "fsdp"),
            P(None, "fsdp"),
            P(None, "fsdp"),
            P("fsdp"),
            P("ctx", "fsdp"),
            P("ctx", None),
        ),
        out_specs=(P("ctx", "fsdp"), P("ctx", "fsdp"), P("ctx", None, "fsdp"), P("ctx", "fsdp")),
        check_vma=False,
    )
```

```python
import functools

import jax
import jax.numpy as jnp
from jax import lax
from jax.experimental import pallas as pl
from jax.experimental.pallas import tpu as pltpu
from jax.sharding import PartitionSpec as P

BF16 = jnp.bfloat16
F32 = jnp.float32
LANES = 128
CHUNKS = 8
MARGIN = 8
VMEM_LIMIT = 12 * 1024 * 1024
SMALL_LIMIT = 4 * 1024 * 1024
FLOPS_PER_US = 1_150_000_000


VMEM = pl.BlockSpec(memory_space=pltpu.VMEM)
HBM = pl.BlockSpec(memory_space=pl.ANY)


def cost(us):
    return pl.CostEstimate(flops=int(us * FLOPS_PER_US), bytes_accessed=0, transcendentals=0)


def call(body, outs, scratch=(), in_specs=None, us=0.5, limit=VMEM_LIMIT):
    return pl.pallas_call(
        body,
        out_shape=outs,
        **({} if in_specs is None else {"in_specs": in_specs}),
        scratch_shapes=list(scratch),
        compiler_params=pltpu.CompilerParams(vmem_limit_bytes=limit),
        cost_estimate=cost(us),
    )


def flipped(value, axis, mask):
    count = lax.axis_size(axis)
    return lax.ppermute(value, axis, [(source, source ^ mask) for source in range(count)])


def block_at(index, size):
    return pl.ds(pl.multiple_of(index * size, size), size)


def to_placement(value):
    count = lax.axis_size("ctx")
    ratio = lax.axis_size("fsdp") // count
    pairs = []
    for f in range(ratio * count):
        for k in range(count):
            target = (k * ratio + f % ratio, f // ratio)
            pairs.append((f * count + k, target[0] * count + target[1]))
    return lax.ppermute(value, ("fsdp", "ctx"), pairs)


def dot(left, right, contract):
    return lax.dot_general(left, right, ((contract[:1], contract[1:]), ((), ())), preferred_element_type=F32)


def shifted(value, steps, backward):
    rows = lax.broadcasted_iota(jnp.int32, value.shape, 0)
    if backward:
        return jnp.where(rows < CHUNKS - steps, pltpu.roll(value, CHUNKS - steps, 0), 0.0)
    return jnp.where(rows >= steps, pltpu.roll(value, steps, 0), 0.0)


def modal_scan(source, target, decay, spread, gain, backward):
    poles, width = decay.shape
    steps = source.shape[0] // CHUNKS
    wide = lambda table, n: jnp.broadcast_to(table[n : n + 1, :], (CHUNKS, width))
    decays = [wide(decay, n) for n in range(poles)]

    def rows(i):
        return pl.ds(steps - 1 - i if backward else i, CHUNKS, stride=steps)

    def gather_up(i, states):
        entry = source[rows(i), :]
        return tuple(d * s + entry for d, s in zip(decays, states))

    zero = jnp.zeros((CHUNKS, width), F32)
    ends = lax.fori_loop(0, steps, gather_up, (zero,) * poles, unroll=4)
    states = []
    for n in range(poles):
        factor = wide(spread, n)
        state = shifted(ends[n], 1, backward)
        reach = 1
        while reach < CHUNKS:
            state = state + factor * shifted(state, reach, backward)
            factor = factor * factor
            reach *= 2
        states.append(state)
    gains = [wide(gain, n) for n in range(poles)]

    def advance(i, states):
        entry = source[rows(i), :]
        states = tuple(d * s + entry for d, s in zip(decays, states))
        terms = [g * s for g, s in zip(gains, states)]
        while len(terms) > 1:
            terms = [a + b for a, b in zip(terms[::2], terms[1::2])]
        target[rows(i), :] = terms[0]
        return states

    lax.fori_loop(0, steps, advance, tuple(states), unroll=2)


def row_blocks(length):
    size = 64 if length % 64 == 0 else length
    return [(start, size) for start in range(0, length, size)]


def forward_body(parts, kinds, taps, decay, spread, gain, skip, query, key, value, long_out, gated, feats, signal, summed):
    length, width = query.shape
    blocks = row_blocks(length)
    for j in range(3):
        feats[j, :MARGIN, :] = jnp.zeros((MARGIN, width), F32)
        for start, size in blocks:
            row, total = kinds(parts, j, start, size)
            feats[j, pl.ds(MARGIN + row, size), :] = total.astype(BF16).astype(F32)
    for start, size in blocks:
        mixed = []
        for j in range(3):
            total = taps[j, 0:1, :] * feats[j, MARGIN + start : MARGIN + start + size, :]
            for lag in range(1, taps.shape[1]):
                first = MARGIN + start - lag
                total = total + taps[j, lag : lag + 1, :] * feats[j, first : first + size, :]
            mixed.append(total)
        at = slice(start, start + size)
        query[at, :], key[at, :], value[at, :] = mixed
        signal[at, :] = mixed[1] * mixed[2]
    modal_scan(signal, summed, decay[...], spread[...], gain[...], False)
    for start, size in blocks:
        at = slice(start, start + size)
        result = summed[at, :] + skip[...] * signal[at, :]
        long_out[at, :] = result
        gated[at, :] = (query[at, :] * result).astype(BF16)


def backward_body(parts, kinds, taps, decay, spread, gain, skip, query, key, value, long_out, grads, mixin, grad_long, summed):
    length, width = query.shape
    blocks = row_blocks(length)
    for start, size in blocks:
        row, grad_gated = kinds(parts, 0, start, size)
        at = pl.ds(row, size)
        mixin[0, at, :] = grad_gated * long_out[at, :]
        grad_long[at, :] = grad_gated * query[at, :]
    modal_scan(grad_long, summed, decay[...], spread[...], gain[...], True)
    for start, size in blocks:
        at = slice(start, start + size)
        grad_signal = summed[at, :] + skip[...] * grad_long[at, :]
        mixin[1, at, :] = grad_signal * value[at, :]
        mixin[2, at, :] = grad_signal * key[at, :]
    for j in range(3):
        mixin[j, length : length + MARGIN, :] = jnp.zeros((MARGIN, width), F32)
        for start, size in blocks:
            total = taps[j, 0:1, :] * mixin[j, start : start + size, :]
            for lag in range(1, taps.shape[1]):
                total = total + taps[j, lag : lag + 1, :] * mixin[j, start + lag : start + lag + size, :]
            grads[j, start : start + size, :] = total.astype(BF16)


def sum_of_three(parts, j, start, size):
    half = parts[0].shape[1]
    other, local = divmod(start, half)
    own, near, far = parts[3 * other : 3 * other + 3]
    at = slice(local, local + size)
    total = own[j, at, :] + near[j, at, :].astype(F32) + far[j, at, :].astype(F32)
    return pl.multiple_of(((lax.axis_index("ctx") >> 1) ^ other) * half + local, MARGIN), total


def plain(parts, j, start, size):
    return start, parts[0][j, start : start + size, :].astype(F32)


def filter_forward(parts, kinds, tables, length, width, after=()):
    count = len(parts)
    inputs = count + len(tables)

    def body(*refs):
        forward_body(refs[:count], kinds, *refs[count:inputs], *refs[inputs + len(after) :])

    wide = jax.ShapeDtypeStruct((length, width), F32)
    return call(
        body,
        (wide, wide, wide, wide, jax.ShapeDtypeStruct((length, width), BF16)),
        [
            pltpu.VMEM((3, MARGIN + length, width), F32),
            pltpu.VMEM((length, width), F32),
            pltpu.VMEM((length, width), F32),
        ],
        in_specs=[VMEM] * inputs + [HBM] * len(after),
        us=2.1,
    )(*parts, *tables, *after)


def filter_backward(parts, kinds, tables, saved, length, width, after=()):
    count = len(parts)
    inputs = count + len(tables) + len(saved)

    def body(*refs):
        backward_body(refs[:count], kinds, *refs[count:inputs], *refs[inputs + len(after) :])

    return call(
        body,
        jax.ShapeDtypeStruct((3, length, width), BF16),
        [
            pltpu.VMEM((3, length + MARGIN, width), F32),
            pltpu.VMEM((length, width), F32),
            pltpu.VMEM((length, width), F32),
        ],
        in_specs=[VMEM] * inputs + [HBM] * len(after),
        us=2.1,
    )(*parts, *tables, *saved, *after)


def later(value, *after):
    def body(*refs):
        pass

    return pl.pallas_call(
        body,
        out_shape=jax.ShapeDtypeStruct(value.shape, value.dtype),
        in_specs=[HBM] * (1 + len(after)),
        out_specs=HBM,
        input_output_aliases={0: 0},
        compiler_params=pltpu.CompilerParams(vmem_limit_bytes=SMALL_LIMIT),
        cost_estimate=cost(0.05),
    )(value, *after)


def column_blocks(rows):
    length, width = rows.shape[0], rows.shape[1] // 4

    def body(rows, own, near, far, arrived):
        me = lax.axis_index("ctx")
        side = lax.axis_index("fsdp") & 1
        copies = []
        for n, (mask, out) in enumerate(((2 ^ side, far), (1, near), (0, own))):
            copies.append(pltpu.make_async_copy(rows.at[:, block_at(me ^ mask, width)], out, arrived.at[n]))
            copies[-1].start()
        for copy in copies:
            copy.wait()

    block = jax.ShapeDtypeStruct((length, width), rows.dtype)
    return call(body, (block,) * 3, [pltpu.SemaphoreType.DMA((3,))], in_specs=[HBM], us=0.7, limit=SMALL_LIMIT)(
        pltpu.with_memory_space_constraint(rows, pltpu.HBM)
    )


def fetched(block):
    pairs = [(4 * f + k, 4 * f + (k ^ 2 ^ (f & 1))) for f in range(8) for k in range(4)]
    return lax.ppermute(block, ("fsdp", "ctx"), pairs)


def project(pieces, other, weight, after=()):
    groups, depth, channels = weight.shape
    part = pieces[0].shape[0]
    length = 2 * part
    width = channels // 4

    def body(first, second, weight, *refs):
        own, far, give, give_far, held, product = refs[len(after) :]
        me = lax.axis_index("ctx")
        core = (me ^ lax.axis_index("fsdp")) & 1 if other else me & 1
        held[block_at(core, part), :] = first[...]
        held[block_at(1 - core, part), :] = second[...]
        for j in range(groups):
            product[...] = dot(held[...], weight[j], (1, 0))
            own[j] = product[:, block_at(me, width)]
            far[j] = product[:, block_at(me ^ 2, width)].astype(BF16)
            give[j] = product[:, block_at(me ^ 1, width)].astype(BF16)
            give_far[j] = product[:, block_at(me ^ 3, width)].astype(BF16)

    sums = jax.ShapeDtypeStruct((groups, length, width), BF16)
    return call(
        body,
        (jax.ShapeDtypeStruct((groups, length, width), F32), sums, sums, sums),
        [pltpu.VMEM((length, depth), BF16), pltpu.VMEM((length, channels), F32)],
        in_specs=[VMEM] * 3 + [HBM] * len(after),
        us=0.45 * groups,
    )(*pieces, weight, *after)


def add_far(left, right):
    def body(left, right, out):
        out[...] = (left[...].astype(F32) + right[...].astype(F32)).astype(BF16)

    return call(body, jax.ShapeDtypeStruct(left.shape, BF16), limit=SMALL_LIMIT)(left, right)


def channel_sums(pieces, other, weight, after=()):
    own, far, give, give_far = project(pieces, other, weight, after)
    passed = add_far(far, flipped(give_far, "ctx", 1))
    return (own, flipped(give, "ctx", 1), flipped(passed, "ctx", 2)), passed


def by_token(here, there):
    return here[0], here[1], there[2], there[0], there[1], here[2]


def all_channels(value, far):
    return value, far, flipped(value, "ctx", 1), flipped(far, "ctx", 1)


def output_pieces(gathered, weight, after=()):
    groups, length, width = gathered[0].shape
    piece = weight.shape[1] // 4
    part = length // 4
    channels = 4 * width

    def product(whole, weight, at, index):
        total = None
        for j in range(groups):
            term = dot(whole[j, at, :], weight[j, block_at(index, piece), :], (1, 1))
            total = term if total is None else total + term
        return total.astype(BF16)

    def pieces(whole, weight, side, low, first, second):
        first[...] = product(whole, weight, slice(None), 2 * side)
        for high in range(2):
            rows = slice(high * part, (high + 1) * part)
            for s in range(2):
                columns = slice(s * piece, (s + 1) * piece)
                second[rows, columns] = product(whole, weight, block_at(2 * high + low, part), 2 * s + 1)

    def first_body(own, far, near, near_far, weight, *refs):
        whole, first, second = refs[len(after) :]
        me = lax.axis_index("ctx")
        place = lax.axis_index("fsdp")
        for j in range(groups):
            for mask, value in ((0, own), (2, far), (1, near), (3, near_far)):
                whole[j, :, block_at(me ^ mask, width)] = value[j]
        pieces(whole, weight, 1 - (place & 1), 1 - ((place >> 1) & 1), first, second)

    def second_body(whole, weight, first, second):
        place = lax.axis_index("fsdp")
        pieces(whole, weight, place & 1, (place >> 1) & 1, first, second)

    parts = (jax.ShapeDtypeStruct((length, piece), BF16), jax.ShapeDtypeStruct((2 * part, 2 * piece), BF16))
    whole, *gives = call(
        first_body,
        (jax.ShapeDtypeStruct((groups, length, channels), BF16), *parts),
        in_specs=[VMEM] * 5 + [HBM] * len(after),
        us=0.6 * groups,
    )(*gathered, weight, *after)
    keeps = call(second_body, parts, us=0.4 * groups)(whole, weight)
    return whole, keeps, gives


def exchange(gives):
    return flipped(gives[0], "fsdp", 1), flipped(gives[1], "fsdp", 2)


def final_pairs(flip):
    pairs = []
    for f in range(8):
        for k in range(4):
            high, low, x, y, core = f >> 2, (f >> 1) & 1, f & 1, k >> 1, k & 1
            pairs.append((4 * f + k, 4 * (4 * (y ^ high ^ flip) + 2 * core + x) + 2 * y + low))
    return pairs


def block_sums(keeps, givens, after=(), after_second=()):
    length, piece = keeps[0].shape
    part = length // 4
    both = lambda keep, given, rows, columns: keep[rows, columns].astype(F32) + given[rows, columns].astype(F32)

    def second_body(keep_x, given_x, keep_z, given_z, *refs):
        give_z, give_x, next_z, next_x = refs[len(after) :]
        place = lax.axis_index("fsdp")
        side, low = place & 1, (place >> 1) & 1
        for high in range(2):
            rows = slice(high * part, (high + 1) * part)
            take = lambda bit: both(keep_x, given_x, block_at(2 * high + bit, part), slice(None))
            give_z[rows, :] = take(1 - low).astype(BF16)
            next_z[rows, :] = take(low)
        take = lambda bit: both(keep_z, given_z, slice(None), block_at(bit, piece))
        give_x[...] = take(1 - side).astype(BF16)
        next_x[...] = take(side)

    square = lambda kind: jax.ShapeDtypeStruct((2 * part, piece), kind)
    give_z, give_x, next_z, next_x = call(
        second_body,
        (square(BF16), square(BF16), square(F32), square(F32)),
        in_specs=[VMEM] * 4 + [HBM] * len(after),
        limit=SMALL_LIMIT,
    )(keeps[0], givens[0], keeps[1], givens[1], *after)

    def third_body(keep_z, given_z, keep_x, given_x, *refs):
        give, keep = refs[len(after_second) :]
        y = lax.axis_index("ctx") >> 1
        for bit, out in ((1 - y, give), (y, keep)):
            at = block_at(bit, part)
            for half, (mine, other) in enumerate(((keep_z, given_z), (keep_x, given_x))):
                columns = slice(half * piece, (half + 1) * piece)
                out[:, columns] = both(mine, other, at, slice(None)).astype(BF16)

    block = jax.ShapeDtypeStruct((part, 2 * piece), BF16)
    give, keep = call(third_body, (block, block), in_specs=[VMEM] * 4 + [HBM] * len(after_second), limit=SMALL_LIMIT)(
        next_z, flipped(give_z, "fsdp", 2), next_x, flipped(give_x, "fsdp", 1), *after_second
    )

    def order_body(keep, given, first, second):
        high = lax.axis_index("fsdp") >> 2
        swap = high == 1
        first[...] = jnp.where(swap, given[...].astype(F32), keep[...].astype(F32)).astype(BF16)
        second[...] = jnp.where(swap, keep[...].astype(F32), given[...].astype(F32)).astype(BF16)

    blocks = call(order_body, (block, block), limit=SMALL_LIMIT)(keep, flipped(give, "ctx", 2))
    arrived = [lax.ppermute(value, ("fsdp", "ctx"), final_pairs(flip)) for flip, value in enumerate(blocks)]

    def last_body(first, second, out):
        out[...] = (first[...].astype(F32) + second[...].astype(F32)).astype(BF16)

    return call(last_body, block, limit=SMALL_LIMIT)(*arrived), give


def turned(pieces):
    part, depth = pieces[0].shape

    def body(a, b, c, d, out):
        me = lax.axis_index("ctx")
        side = lax.axis_index("fsdp") & 1
        for mask, piece in ((0, a), (1, b), (2 ^ side, c), (3 ^ side, d)):
            out[:, block_at(me ^ mask, part)] = piece[...].T

    return call(body, jax.ShapeDtypeStruct((depth, 4 * part), pieces[0].dtype), us=0.4, limit=SMALL_LIMIT)(*pieces)


def weight_gradient(rows, values, after=()):
    depth, length = rows.shape
    groups, _, channels = values.shape
    tile = 256
    steps = [(j, i) for j in range(groups) for i in range(depth // tile)]
    slots = min(4, len(steps))

    def body(rows, values, *refs):
        out, mark, ready, written = refs[len(after) :]
        copies = []
        for n, (j, i) in enumerate(steps):
            slot = n % slots
            if n >= slots:
                copies[n - slots].wait()
            at = slice(i * tile, (i + 1) * tile)
            ready[slot] = dot(rows[at, :], values[j], (1, 0))
            copies.append(pltpu.make_async_copy(ready.at[slot], out.at[j, at, :], written.at[slot]))
            copies[-1].start()
        mark[...] = jnp.zeros_like(mark)
        for copy in copies[-slots:]:
            copy.wait()

    gradient = jax.ShapeDtypeStruct((groups, depth, channels), F32)
    return pl.pallas_call(
        body,
        out_shape=(gradient, jax.ShapeDtypeStruct((8, LANES), F32)),
        in_specs=[VMEM] * 2 + [HBM] * len(after),
        out_specs=(HBM, VMEM),
        scratch_shapes=[pltpu.VMEM((slots, tile, channels), F32), pltpu.SemaphoreType.DMA((slots,))],
        compiler_params=pltpu.CompilerParams(vmem_limit_bytes=VMEM_LIMIT),
        cost_estimate=cost(1.0 * groups),
    )(rows, values, *after)


def four_by_eight(tokens, weights, tables, out_weight, grad_mixed):
    length, width = 4 * tokens.shape[0], weights.shape[2] // 4
    own, near, far = column_blocks(tokens)
    read_weights = pltpu.with_memory_space_constraint(weights, pltpu.HBM)
    here = (own, flipped(near, "ctx", 1))
    feats_here, passed = channel_sums(here, 0, read_weights)
    far = later(fetched(far), passed)
    there = (far, flipped(far, "fsdp", 1))
    grad_own, grad_near, grad_far = column_blocks(grad_mixed)
    grad_here = (grad_own, flipped(grad_near, "ctx", 1))
    grad_far = later(grad_far, far)
    early = feats_here[2], grad_far
    grad_far = fetched(grad_far)
    grad_there = (grad_far, flipped(grad_far, "fsdp", 1))
    feats_there, passed = channel_sums(there, 1, read_weights, early)
    grads_here, _ = channel_sums(grad_here, 0, out_weight[None], (passed,))
    feats = by_token(feats_here, feats_there)
    *saved, gated = filter_forward(feats, sum_of_three, tables, length, width, grads_here[2:])
    grads_there, _ = channel_sums(grad_there, 1, out_weight[None], (gated,))
    gated = gated[None]
    gated_far = flipped(gated, "ctx", 2)
    all_gated = all_channels(gated, gated_far)
    whole_gated, keeps, gives = output_pieces(all_gated, out_weight[None])
    givens = exchange(gives)
    mixed_halves = keeps, givens
    grads = filter_backward(by_token(grads_here, grads_there), sum_of_three, tables, saved, length, width)
    grads = later(grads, gated_far)
    grad_out, mark = weight_gradient(turned(grad_here + grad_there), whole_gated)
    token_rows = turned(here + there)
    grads_far = later(flipped(grads, "ctx", 2), *givens, keeps[0], token_rows, mark)
    whole_grads, keeps, gives = output_pieces(all_channels(grads, grads_far), weights)
    mixed, mixed_give = block_sums(*mixed_halves, (), gives[:1])
    grad_in, mark = weight_gradient(token_rows, whole_grads, (mixed_give,))
    grad_tokens, _ = block_sums(keeps, exchange(gives), (mark,))
    return mixed, grad_tokens, grad_in, grad_out[0]


def any_mesh(tokens, weights, tables, out_weight, grad_mixed):
    count = lax.axis_size("ctx")
    columns = lambda rows: lax.all_to_all(rows, "ctx", split_axis=1, concat_axis=0, tiled=True)
    whole_tokens, whole_cotangents = columns(tokens), columns(grad_mixed)
    length, width = whole_tokens.shape[0], weights.shape[2] // count

    def channel_sums(rows, weight):
        partial = jnp.einsum("td,jdc->jtc", rows, weight, preferred_element_type=F32)
        return lax.psum_scatter(partial.astype(BF16), "ctx", scatter_dimension=2, tiled=True)

    def block_sums(values, weight):
        partial = jnp.einsum("jtc,jdc->td", values, weight, preferred_element_type=F32)
        ratio = lax.axis_size("fsdp") // count
        pieces = partial.astype(BF16).reshape(count, length // count, ratio, -1).transpose(0, 2, 1, 3)
        pieces = pieces.reshape(count * ratio, length // count, -1)
        return to_placement(lax.psum_scatter(pieces, "fsdp", scatter_dimension=0, tiled=True)[0])

    feats = channel_sums(whole_tokens, weights)
    grad_gated = channel_sums(whole_cotangents, out_weight[None])
    *saved, gated = filter_forward((feats,), plain, tables, length, width)
    grads = filter_backward((grad_gated,), plain, tables, saved, length, width)
    whole_gated = lax.all_gather(gated, "ctx", axis=1, tiled=True)
    whole_grads = lax.all_gather(grads, "ctx", axis=2, tiled=True)
    mixed = block_sums(whole_gated[None], out_weight[None])
    grad_tokens = block_sums(whole_grads, weights)
    grad_in = jnp.einsum("td,jtc->jdc", whole_tokens, whole_grads, preferred_element_type=F32)
    grad_out = jnp.einsum("td,tc->dc", whole_cotangents, whole_gated, preferred_element_type=F32)
    return mixed, grad_tokens, grad_in, grad_out


def per_device(tokens, in_weight, conv_taps, decay_rate, residue, skip_gain, out_weight, grad_mixed):
    count, blocks = lax.axis_size("ctx"), lax.axis_size("fsdp")
    weights = in_weight.transpose(1, 0, 2)
    length = count * tokens.shape[0]
    width = weights.shape[2] // count
    mine = lambda table: lax.dynamic_slice_in_dim(table, lax.axis_index("ctx") * width, width, table.ndim - 1)
    rate = mine(decay_rate)
    gain = mine(residue) * jnp.sqrt(-jnp.expm1(-2.0 * rate))
    tables = (mine(conv_taps.transpose(1, 0, 2)), jnp.exp(-rate), jnp.exp(-rate * (length // CHUNKS)), gain, mine(skip_gain[None]))
    tuned = count == 4 and blocks == 8 and width % LANES == 0 and tokens.shape[0] % LANES == 0
    plan = four_by_eight if tuned else any_mesh
    mixed, grad_tokens, grad_in, grad_out = plan(tokens, weights, tables, out_weight, grad_mixed)
    return mixed, grad_tokens, grad_in.transpose(1, 0, 2), grad_out


def solution(mesh):
    return jax.shard_map(
        per_device,
        mesh=mesh,
        in_specs=(
            P("ctx", None),
            P("ctx", None, "fsdp"),
            P(None, None, "fsdp"),
            P(None, "fsdp"),
            P(None, "fsdp"),
            P("fsdp"),
            P("ctx", "fsdp"),
            P("ctx", None),
        ),
        out_specs=(P("ctx", "fsdp"), P("ctx", "fsdp"), P("ctx", None, "fsdp"), P("ctx", "fsdp")),
        check_vma=False,
    )
```

```python
import functools

import jax
import jax.numpy as jnp
from jax import lax
from jax.experimental import pallas as pl
from jax.experimental.pallas import tpu as pltpu
from jax.sharding import PartitionSpec as P

BF16 = jnp.bfloat16
F32 = jnp.float32
LANES = 128
CHUNKS = 8
MARGIN = 8
VMEM_LIMIT = 16 * 1024 * 1024
SMALL_LIMIT = 4 * 1024 * 1024
FLOPS_PER_US = 1_150_000_000


VMEM = pl.BlockSpec(memory_space=pltpu.VMEM)
HBM = pl.BlockSpec(memory_space=pl.ANY)


def cost(us):
    return pl.CostEstimate(flops=int(us * FLOPS_PER_US), bytes_accessed=0, transcendentals=0)


def call(body, outs, scratch=(), in_specs=None, us=0.5):
    return pl.pallas_call(
        body,
        out_shape=outs,
        **({} if in_specs is None else {"in_specs": in_specs}),
        scratch_shapes=list(scratch),
        compiler_params=pltpu.CompilerParams(vmem_limit_bytes=VMEM_LIMIT),
        cost_estimate=cost(us),
    )


def flipped(value, axis, mask):
    count = lax.axis_size(axis)
    return lax.ppermute(value, axis, [(source, source ^ mask) for source in range(count)])


def block_at(index, size):
    return pl.ds(pl.multiple_of(index * size, size), size)


def to_placement(value):
    count = lax.axis_size("ctx")
    ratio = lax.axis_size("fsdp") // count
    pairs = []
    for f in range(ratio * count):
        for k in range(count):
            target = (k * ratio + f % ratio, f // ratio)
            pairs.append((f * count + k, target[0] * count + target[1]))
    return lax.ppermute(value, ("fsdp", "ctx"), pairs)


def dot(left, right, contract):
    return lax.dot_general(left, right, ((contract[:1], contract[1:]), ((), ())), preferred_element_type=F32)


def shifted(value, steps, backward):
    rows = lax.broadcasted_iota(jnp.int32, value.shape, 0)
    if backward:
        return jnp.where(rows < CHUNKS - steps, pltpu.roll(value, CHUNKS - steps, 0), 0.0)
    return jnp.where(rows >= steps, pltpu.roll(value, steps, 0), 0.0)


def modal_scan(source, target, decay, spread, gain, backward):
    poles, width = decay.shape
    steps = source.shape[0] // CHUNKS
    wide = lambda table, n: jnp.broadcast_to(table[n : n + 1, :], (CHUNKS, width))
    decays = [wide(decay, n) for n in range(poles)]

    def rows(i):
        return pl.ds(steps - 1 - i if backward else i, CHUNKS, stride=steps)

    def gather_up(i, states):
        entry = source[rows(i), :]
        return tuple(d * s + entry for d, s in zip(decays, states))

    zero = jnp.zeros((CHUNKS, width), F32)
    ends = lax.fori_loop(0, steps, gather_up, (zero,) * poles, unroll=4)
    states = []
    for n in range(poles):
        factor = wide(spread, n)
        state = shifted(ends[n], 1, backward)
        reach = 1
        while reach < CHUNKS:
            state = state + factor * shifted(state, reach, backward)
            factor = factor * factor
            reach *= 2
        states.append(state)
    gains = [wide(gain, n) for n in range(poles)]

    def advance(i, states):
        entry = source[rows(i), :]
        states = tuple(d * s + entry for d, s in zip(decays, states))
        terms = [g * s for g, s in zip(gains, states)]
        while len(terms) > 1:
            terms = [a + b for a, b in zip(terms[::2], terms[1::2])]
        target[rows(i), :] = terms[0]
        return states

    lax.fori_loop(0, steps, advance, tuple(states), unroll=2)


def row_blocks(length):
    size = 64 if length % 64 == 0 else length
    return [(start, size) for start in range(0, length, size)]


def forward_body(parts, kinds, taps, decay, spread, gain, skip, query, key, value, long_out, gated, feats, signal, summed):
    length, width = query.shape
    blocks = row_blocks(length)
    for j in range(3):
        feats[j, :MARGIN, :] = jnp.zeros((MARGIN, width), F32)
        for start, size in blocks:
            row, total = kinds(parts, j, start, size)
            feats[j, pl.ds(MARGIN + row, size), :] = total.astype(BF16).astype(F32)
    for start, size in blocks:
        mixed = []
        for j in range(3):
            total = taps[j, 0:1, :] * feats[j, MARGIN + start : MARGIN + start + size, :]
            for lag in range(1, taps.shape[1]):
                first = MARGIN + start - lag
                total = total + taps[j, lag : lag + 1, :] * feats[j, first : first + size, :]
            mixed.append(total)
        at = slice(start, start + size)
        query[at, :], key[at, :], value[at, :] = mixed
        signal[at, :] = mixed[1] * mixed[2]
    modal_scan(signal, summed, decay[...], spread[...], gain[...], False)
    for start, size in blocks:
        at = slice(start, start + size)
        result = summed[at, :] + skip[...] * signal[at, :]
        long_out[at, :] = result
        gated[at, :] = (query[at, :] * result).astype(BF16)


def backward_body(parts, kinds, taps, decay, spread, gain, skip, query, key, value, long_out, grads, mixin, grad_long, summed):
    length, width = query.shape
    blocks = row_blocks(length)
    for start, size in blocks:
        row, grad_gated = kinds(parts, 0, start, size)
        at = pl.ds(row, size)
        mixin[0, at, :] = grad_gated * long_out[at, :]
        grad_long[at, :] = grad_gated * query[at, :]
    modal_scan(grad_long, summed, decay[...], spread[...], gain[...], True)
    for start, size in blocks:
        at = slice(start, start + size)
        grad_signal = summed[at, :] + skip[...] * grad_long[at, :]
        mixin[1, at, :] = grad_signal * value[at, :]
        mixin[2, at, :] = grad_signal * key[at, :]
    for j in range(3):
        mixin[j, length : length + MARGIN, :] = jnp.zeros((MARGIN, width), F32)
        for start, size in blocks:
            total = taps[j, 0:1, :] * mixin[j, start : start + size, :]
            for lag in range(1, taps.shape[1]):
                total = total + taps[j, lag : lag + 1, :] * mixin[j, start + lag : start + lag + size, :]
            grads[j, start : start + size, :] = total.astype(BF16)


def sum_of_three(parts, j, start, size):
    half = parts[0].shape[1]
    other, local = divmod(start, half)
    own, near, far = parts[3 * other : 3 * other + 3]
    at = slice(local, local + size)
    total = own[j, at, :] + near[j, at, :].astype(F32) + far[j, at, :].astype(F32)
    return pl.multiple_of(((lax.axis_index("ctx") >> 1) ^ other) * half + local, MARGIN), total


def plain(parts, j, start, size):
    return start, parts[0][j, start : start + size, :].astype(F32)


def filter_forward(parts, kinds, tables, length, width, after=()):
    count = len(parts)
    inputs = count + len(tables)

    def body(*refs):
        forward_body(refs[:count], kinds, *refs[count:inputs], *refs[inputs + len(after) :])

    wide = jax.ShapeDtypeStruct((length, width), F32)
    return call(
        body,
        (wide, wide, wide, wide, jax.ShapeDtypeStruct((length, width), BF16)),
        [
            pltpu.VMEM((3, MARGIN + length, width), F32),
            pltpu.VMEM((length, width), F32),
            pltpu.VMEM((length, width), F32),
        ],
        in_specs=[VMEM] * inputs + [HBM] * len(after),
        us=2.1,
    )(*parts, *tables, *after)


def filter_backward(parts, kinds, tables, saved, length, width, after=()):
    count = len(parts)
    inputs = count + len(tables) + len(saved)

    def body(*refs):
        backward_body(refs[:count], kinds, *refs[count:inputs], *refs[inputs + len(after) :])

    return call(
        body,
        jax.ShapeDtypeStruct((3, length, width), BF16),
        [
            pltpu.VMEM((3, length + MARGIN, width), F32),
            pltpu.VMEM((length, width), F32),
            pltpu.VMEM((length, width), F32),
        ],
        in_specs=[VMEM] * inputs + [HBM] * len(after),
        us=2.1,
    )(*parts, *tables, *saved, *after)


def later(value, *after):
    def body(*refs):
        pass

    return pl.pallas_call(
        body,
        out_shape=jax.ShapeDtypeStruct(value.shape, value.dtype),
        in_specs=[HBM] * (1 + len(after)),
        out_specs=HBM,
        input_output_aliases={0: 0},
        compiler_params=pltpu.CompilerParams(vmem_limit_bytes=SMALL_LIMIT),
        cost_estimate=cost(0.05),
    )(value, *after)


def column_blocks(rows):
    length, width = rows.shape[0], rows.shape[1] // 4

    def body(rows, own, near, far, arrived):
        me = lax.axis_index("ctx")
        side = lax.axis_index("fsdp") & 1
        copies = []
        for n, (mask, out) in enumerate(((2 ^ side, far), (1, near), (0, own))):
            copies.append(pltpu.make_async_copy(rows.at[:, block_at(me ^ mask, width)], out, arrived.at[n]))
            copies[-1].start()
        for copy in copies:
            copy.wait()

    block = jax.ShapeDtypeStruct((length, width), rows.dtype)
    return call(body, (block,) * 3, [pltpu.SemaphoreType.DMA((3,))], in_specs=[HBM], us=0.7)(rows)


def fetched(block):
    pairs = [(4 * f + k, 4 * f + (k ^ 2 ^ (f & 1))) for f in range(8) for k in range(4)]
    return lax.ppermute(block, ("fsdp", "ctx"), pairs)


def project(pieces, other, weight, after=()):
    groups, depth, channels = weight.shape
    part = pieces[0].shape[0]
    length = 2 * part
    width = channels // 4

    def body(first, second, weight, *refs):
        own, far, give, give_far, held, product = refs[len(after) :]
        me = lax.axis_index("ctx")
        core = (me ^ lax.axis_index("fsdp")) & 1 if other else me & 1
        held[block_at(core, part), :] = first[...]
        held[block_at(1 - core, part), :] = second[...]
        for j in range(groups):
            product[...] = dot(held[...], weight[j], (1, 0))
            own[j] = product[:, block_at(me, width)]
            far[j] = product[:, block_at(me ^ 2, width)].astype(BF16)
            give[j] = product[:, block_at(me ^ 1, width)].astype(BF16)
            give_far[j] = product[:, block_at(me ^ 3, width)].astype(BF16)

    sums = jax.ShapeDtypeStruct((groups, length, width), BF16)
    return call(
        body,
        (jax.ShapeDtypeStruct((groups, length, width), F32), sums, sums, sums),
        [pltpu.VMEM((length, depth), BF16), pltpu.VMEM((length, channels), F32)],
        in_specs=[VMEM] * 3 + [HBM] * len(after),
        us=0.45 * groups,
    )(*pieces, weight, *after)


def add_far(left, right, after):
    def body(left, right, *refs):
        refs[-1][...] = (left[...].astype(F32) + right[...].astype(F32)).astype(BF16)

    specs = [VMEM] * 2 + [HBM] * len(after)
    return call(body, jax.ShapeDtypeStruct(left.shape, BF16), in_specs=specs)(left, right, *after)


def channel_sums(pieces, other, weight, after=(), after_add=()):
    own, far, give, give_far = project(pieces, other, weight, after)
    passed = add_far(far, flipped(give_far, "ctx", 1), after_add)
    return (own, flipped(give, "ctx", 1), flipped(passed, "ctx", 2)), passed


def by_token(here, there):
    return here[0], here[1], there[2], there[0], there[1], here[2]


def all_channels(value, far):
    return value, far, flipped(value, "ctx", 1), flipped(far, "ctx", 1)


def output_pieces(gathered, weight, after=()):
    groups, length, width = gathered[0].shape
    piece = weight.shape[1] // 4
    part = length // 4
    channels = 4 * width

    def product(whole, weight, at, index):
        total = None
        for j in range(groups):
            term = dot(whole[j, at, :], weight[j, block_at(index, piece), :], (1, 1))
            total = term if total is None else total + term
        return total.astype(BF16)

    def pieces(whole, weight, side, low, first, second):
        first[...] = product(whole, weight, slice(None), 2 * side)
        for high in range(2):
            rows = slice(high * part, (high + 1) * part)
            for s in range(2):
                columns = slice(s * piece, (s + 1) * piece)
                second[rows, columns] = product(whole, weight, block_at(2 * high + low, part), 2 * s + 1)

    def first_body(own, far, near, near_far, weight, *refs):
        whole, first, second = refs[len(after) :]
        me = lax.axis_index("ctx")
        place = lax.axis_index("fsdp")
        for j in range(groups):
            for mask, value in ((0, own), (2, far), (1, near), (3, near_far)):
                whole[j, :, block_at(me ^ mask, width)] = value[j]
        pieces(whole, weight, 1 - (place & 1), 1 - ((place >> 1) & 1), first, second)

    def second_body(whole, weight, first, second):
        place = lax.axis_index("fsdp")
        pieces(whole, weight, place & 1, (place >> 1) & 1, first, second)

    parts = (jax.ShapeDtypeStruct((length, piece), BF16), jax.ShapeDtypeStruct((2 * part, 2 * piece), BF16))
    whole, *gives = call(
        first_body,
        (jax.ShapeDtypeStruct((groups, length, channels), BF16), *parts),
        in_specs=[VMEM] * 5 + [HBM] * len(after),
        us=0.6 * groups,
    )(*gathered, weight, *after)
    keeps = call(second_body, parts, us=0.4 * groups)(whole, weight)
    return whole, keeps, gives


def exchange(gives):
    return flipped(gives[0], "fsdp", 1), flipped(gives[1], "fsdp", 2)


def final_pairs(flip):
    pairs = []
    for f in range(8):
        for k in range(4):
            high, low, x, y, core = f >> 2, (f >> 1) & 1, f & 1, k >> 1, k & 1
            pairs.append((4 * f + k, 4 * (4 * (y ^ high ^ flip) + 2 * core + x) + 2 * y + low))
    return pairs


def block_sums(keeps, givens, after=(), after_second=()):
    length, piece = keeps[0].shape
    part = length // 4
    both = lambda keep, given, rows, columns: keep[rows, columns].astype(F32) + given[rows, columns].astype(F32)

    def second_body(keep_x, given_x, keep_z, given_z, *refs):
        give_z, give_x, next_z, next_x = refs[len(after) :]
        place = lax.axis_index("fsdp")
        side, low = place & 1, (place >> 1) & 1
        for high in range(2):
            rows = slice(high * part, (high + 1) * part)
            take = lambda bit: both(keep_x, given_x, block_at(2 * high + bit, part), slice(None))
            give_z[rows, :] = take(1 - low).astype(BF16)
            next_z[rows, :] = take(low)
        take = lambda bit: both(keep_z, given_z, slice(None), block_at(bit, piece))
        give_x[...] = take(1 - side).astype(BF16)
        next_x[...] = take(side)

    square = lambda kind: jax.ShapeDtypeStruct((2 * part, piece), kind)
    give_z, give_x, next_z, next_x = call(
        second_body,
        (square(BF16), square(BF16), square(F32), square(F32)),
        in_specs=[VMEM] * 4 + [HBM] * len(after),
    )(keeps[0], givens[0], keeps[1], givens[1], *after)

    def third_body(keep_z, given_z, keep_x, given_x, *refs):
        give, keep = refs[len(after_second) :]
        y = lax.axis_index("ctx") >> 1
        for bit, out in ((1 - y, give), (y, keep)):
            at = block_at(bit, part)
            for half, (mine, other) in enumerate(((keep_z, given_z), (keep_x, given_x))):
                columns = slice(half * piece, (half + 1) * piece)
                out[:, columns] = both(mine, other, at, slice(None)).astype(BF16)

    block = jax.ShapeDtypeStruct((part, 2 * piece), BF16)
    give, keep = call(third_body, (block, block), in_specs=[VMEM] * 4 + [HBM] * len(after_second))(
        next_z, flipped(give_z, "fsdp", 2), next_x, flipped(give_x, "fsdp", 1), *after_second
    )

    def order_body(keep, given, first, second):
        high = lax.axis_index("fsdp") >> 2
        swap = high == 1
        first[...] = jnp.where(swap, given[...].astype(F32), keep[...].astype(F32)).astype(BF16)
        second[...] = jnp.where(swap, keep[...].astype(F32), given[...].astype(F32)).astype(BF16)

    blocks = call(order_body, (block, block))(keep, flipped(give, "ctx", 2))
    arrived = [lax.ppermute(value, ("fsdp", "ctx"), final_pairs(flip)) for flip, value in enumerate(blocks)]

    def last_body(first, second, out):
        out[...] = (first[...].astype(F32) + second[...].astype(F32)).astype(BF16)

    return call(last_body, block)(*arrived), give


def turned(pieces):
    part, depth = pieces[0].shape

    def body(a, b, c, d, out):
        me = lax.axis_index("ctx")
        side = lax.axis_index("fsdp") & 1
        for mask, piece in ((0, a), (1, b), (2 ^ side, c), (3 ^ side, d)):
            out[:, block_at(me ^ mask, part)] = piece[...].T

    return call(body, jax.ShapeDtypeStruct((depth, 4 * part), pieces[0].dtype), us=0.4)(*pieces)


def weight_gradient(rows, values, after=()):
    depth, length = rows.shape
    groups, _, channels = values.shape
    tile = depth // 2

    def body(rows, values, *refs):
        out, mark = refs[len(after) :]
        out[0] = dot(rows[...], values[0], (1, 0))
        mark[...] = jnp.zeros_like(mark)

    return pl.pallas_call(
        body,
        out_shape=(jax.ShapeDtypeStruct((groups, depth, channels), F32), jax.ShapeDtypeStruct((8, LANES), F32)),
        grid=(groups, depth // tile),
        in_specs=[
            pl.BlockSpec((tile, length), lambda j, i: (i, 0)),
            pl.BlockSpec((1, length, channels), lambda j, i: (j, 0, 0)),
        ]
        + [HBM] * len(after),
        out_specs=(pl.BlockSpec((1, tile, channels), lambda j, i: (j, i, 0)), pl.BlockSpec((8, LANES), lambda j, i: (0, 0))),
        compiler_params=pltpu.CompilerParams(vmem_limit_bytes=VMEM_LIMIT),
        cost_estimate=cost(1.5 * groups),
    )(rows, values, *after)


def four_by_eight(tokens, weights, tables, out_weight, grad_mixed):
    length, width = 4 * tokens.shape[0], weights.shape[2] // 4
    own, near, far = column_blocks(tokens)
    here = (own, flipped(near, "ctx", 1))
    feats_here, passed = channel_sums(here, 0, weights)
    far = later(fetched(far), passed)
    there = (far, flipped(far, "fsdp", 1))
    grad_own, grad_near, grad_far = column_blocks(grad_mixed)
    grad_here = (grad_own, flipped(grad_near, "ctx", 1))
    grad_far = fetched(later(grad_far, far))
    grad_there = (grad_far, flipped(grad_far, "fsdp", 1))
    feats_there, passed = channel_sums(there, 1, weights, feats_here[2:], (grad_far,))
    grads_here, _ = channel_sums(grad_here, 0, out_weight[None], (passed,))
    feats = by_token(feats_here, feats_there)
    *saved, gated = filter_forward(feats, sum_of_three, tables, length, width, grads_here[2:])
    grads_there, _ = channel_sums(grad_there, 1, out_weight[None], (gated,))
    gated = gated[None]
    gated_far = flipped(gated, "ctx", 2)
    all_gated = all_channels(gated, gated_far)
    whole_gated, keeps, gives = output_pieces(all_gated, out_weight[None])
    givens = exchange(gives)
    mixed_halves = keeps, givens
    grads = filter_backward(by_token(grads_here, grads_there), sum_of_three, tables, saved, length, width)
    grads = later(grads, gated_far)
    grad_out, mark = weight_gradient(turned(grad_here + grad_there), whole_gated)
    token_rows = turned(here + there)
    grads_far = later(flipped(grads, "ctx", 2), *givens, keeps[0], token_rows, mark)
    whole_grads, keeps, gives = output_pieces(all_channels(grads, grads_far), weights)
    mixed, mixed_give = block_sums(*mixed_halves, (), gives[:1])
    grad_in, mark = weight_gradient(token_rows, whole_grads, (mixed_give,))
    grad_tokens, _ = block_sums(keeps, exchange(gives), (mark,))
    return mixed, grad_tokens, grad_in, grad_out[0]


def any_mesh(tokens, weights, tables, out_weight, grad_mixed):
    count = lax.axis_size("ctx")
    columns = lambda rows: lax.all_to_all(rows, "ctx", split_axis=1, concat_axis=0, tiled=True)
    whole_tokens, whole_cotangents = columns(tokens), columns(grad_mixed)
    length, width = whole_tokens.shape[0], weights.shape[2] // count

    def channel_sums(rows, weight):
        partial = jnp.einsum("td,jdc->jtc", rows, weight, preferred_element_type=F32)
        return lax.psum_scatter(partial.astype(BF16), "ctx", scatter_dimension=2, tiled=True)

    def block_sums(values, weight):
        partial = jnp.einsum("jtc,jdc->td", values, weight, preferred_element_type=F32)
        ratio = lax.axis_size("fsdp") // count
        pieces = partial.astype(BF16).reshape(count, length // count, ratio, -1).transpose(0, 2, 1, 3)
        pieces = pieces.reshape(count * ratio, length // count, -1)
        return to_placement(lax.psum_scatter(pieces, "fsdp", scatter_dimension=0, tiled=True)[0])

    feats = channel_sums(whole_tokens, weights)
    grad_gated = channel_sums(whole_cotangents, out_weight[None])
    *saved, gated = filter_forward((feats,), plain, tables, length, width)
    grads = filter_backward((grad_gated,), plain, tables, saved, length, width)
    whole_gated = lax.all_gather(gated, "ctx", axis=1, tiled=True)
    whole_grads = lax.all_gather(grads, "ctx", axis=2, tiled=True)
    mixed = block_sums(whole_gated[None], out_weight[None])
    grad_tokens = block_sums(whole_grads, weights)
    grad_in = jnp.einsum("td,jtc->jdc", whole_tokens, whole_grads, preferred_element_type=F32)
    grad_out = jnp.einsum("td,tc->dc", whole_cotangents, whole_gated, preferred_element_type=F32)
    return mixed, grad_tokens, grad_in, grad_out


def per_device(tokens, in_weight, conv_taps, decay_rate, residue, skip_gain, out_weight, grad_mixed):
    count, blocks = lax.axis_size("ctx"), lax.axis_size("fsdp")
    weights = in_weight.transpose(1, 0, 2)
    length = count * tokens.shape[0]
    width = weights.shape[2] // count
    mine = lambda table: lax.dynamic_slice_in_dim(table, lax.axis_index("ctx") * width, width, table.ndim - 1)
    rate = mine(decay_rate)
    gain = mine(residue) * jnp.sqrt(-jnp.expm1(-2.0 * rate))
    tables = (mine(conv_taps.transpose(1, 0, 2)), jnp.exp(-rate), jnp.exp(-rate * (length // CHUNKS)), gain, mine(skip_gain[None]))
    tuned = count == 4 and blocks == 8 and width % LANES == 0 and tokens.shape[0] % LANES == 0
    plan = four_by_eight if tuned else any_mesh
    mixed, grad_tokens, grad_in, grad_out = plan(tokens, weights, tables, out_weight, grad_mixed)
    return mixed, grad_tokens, grad_in.transpose(1, 0, 2), grad_out


def solution(mesh):
    return jax.shard_map(
        per_device,
        mesh=mesh,
        in_specs=(
            P("ctx", None),
            P("ctx", None, "fsdp"),
            P(None, None, "fsdp"),
            P(None, "fsdp"),
            P(None, "fsdp"),
            P("fsdp"),
            P("ctx", "fsdp"),
            P("ctx", None),
        ),
        out_specs=(P("ctx", "fsdp"), P("ctx", "fsdp"), P("ctx", None, "fsdp"), P("ctx", "fsdp")),
        check_vma=False,
    )
```

```python
import functools

import jax
import jax.numpy as jnp
from jax import lax
from jax.experimental import pallas as pl
from jax.experimental.pallas import tpu as pltpu
from jax.sharding import PartitionSpec as P

BF16 = jnp.bfloat16
F32 = jnp.float32
LANES = 128
CHUNKS = 8
MARGIN = 8
VMEM_LIMIT = 16 * 1024 * 1024
SMALL_LIMIT = 4 * 1024 * 1024
FLOPS_PER_US = 1_150_000_000


VMEM = pl.BlockSpec(memory_space=pltpu.VMEM)
HBM = pl.BlockSpec(memory_space=pl.ANY)


def cost(us):
    return pl.CostEstimate(flops=int(us * FLOPS_PER_US), bytes_accessed=0, transcendentals=0)


def call(body, outs, scratch=(), in_specs=None, us=0.5):
    return pl.pallas_call(
        body,
        out_shape=outs,
        **({} if in_specs is None else {"in_specs": in_specs}),
        scratch_shapes=list(scratch),
        compiler_params=pltpu.CompilerParams(vmem_limit_bytes=VMEM_LIMIT),
        cost_estimate=cost(us),
    )


def flipped(value, axis, mask):
    count = lax.axis_size(axis)
    return lax.ppermute(value, axis, [(source, source ^ mask) for source in range(count)])


def block_at(index, size):
    return pl.ds(pl.multiple_of(index * size, size), size)


def to_placement(value):
    count = lax.axis_size("ctx")
    ratio = lax.axis_size("fsdp") // count
    pairs = []
    for f in range(ratio * count):
        for k in range(count):
            target = (k * ratio + f % ratio, f // ratio)
            pairs.append((f * count + k, target[0] * count + target[1]))
    return lax.ppermute(value, ("fsdp", "ctx"), pairs)


def dot(left, right, contract):
    return lax.dot_general(left, right, ((contract[:1], contract[1:]), ((), ())), preferred_element_type=F32)


def shifted(value, steps, backward):
    rows = lax.broadcasted_iota(jnp.int32, value.shape, 0)
    if backward:
        return jnp.where(rows < CHUNKS - steps, pltpu.roll(value, CHUNKS - steps, 0), 0.0)
    return jnp.where(rows >= steps, pltpu.roll(value, steps, 0), 0.0)


def modal_scan(source, target, decay, spread, gain, backward):
    poles, width = decay.shape
    steps = source.shape[0] // CHUNKS
    wide = lambda table, n: jnp.broadcast_to(table[n : n + 1, :], (CHUNKS, width))
    decays = [wide(decay, n) for n in range(poles)]

    def rows(i):
        return pl.ds(steps - 1 - i if backward else i, CHUNKS, stride=steps)

    def gather_up(i, states):
        entry = source[rows(i), :]
        return tuple(d * s + entry for d, s in zip(decays, states))

    zero = jnp.zeros((CHUNKS, width), F32)
    ends = lax.fori_loop(0, steps, gather_up, (zero,) * poles, unroll=4)
    states = []
    for n in range(poles):
        factor = wide(spread, n)
        state = shifted(ends[n], 1, backward)
        reach = 1
        while reach < CHUNKS:
            state = state + factor * shifted(state, reach, backward)
            factor = factor * factor
            reach *= 2
        states.append(state)
    gains = [wide(gain, n) for n in range(poles)]

    def advance(i, states):
        entry = source[rows(i), :]
        states = tuple(d * s + entry for d, s in zip(decays, states))
        terms = [g * s for g, s in zip(gains, states)]
        while len(terms) > 1:
            terms = [a + b for a, b in zip(terms[::2], terms[1::2])]
        target[rows(i), :] = terms[0]
        return states

    lax.fori_loop(0, steps, advance, tuple(states), unroll=2)


def row_blocks(length):
    size = 64 if length % 64 == 0 else length
    return [(start, size) for start in range(0, length, size)]


def forward_body(parts, kinds, taps, decay, spread, gain, skip, query, key, value, long_out, gated, feats, signal, summed):
    length, width = query.shape
    blocks = row_blocks(length)
    for j in range(3):
        feats[j, :MARGIN, :] = jnp.zeros((MARGIN, width), F32)
        for start, size in blocks:
            row, total = kinds(parts, j, start, size)
            feats[j, pl.ds(MARGIN + row, size), :] = total.astype(BF16).astype(F32)
    for start, size in blocks:
        mixed = []
        for j in range(3):
            total = taps[j, 0:1, :] * feats[j, MARGIN + start : MARGIN + start + size, :]
            for lag in range(1, taps.shape[1]):
                first = MARGIN + start - lag
                total = total + taps[j, lag : lag + 1, :] * feats[j, first : first + size, :]
            mixed.append(total)
        at = slice(start, start + size)
        query[at, :], key[at, :], value[at, :] = mixed
        signal[at, :] = mixed[1] * mixed[2]
    modal_scan(signal, summed, decay[...], spread[...], gain[...], False)
    for start, size in blocks:
        at = slice(start, start + size)
        result = summed[at, :] + skip[...] * signal[at, :]
        long_out[at, :] = result
        gated[at, :] = (query[at, :] * result).astype(BF16)


def backward_body(parts, kinds, taps, decay, spread, gain, skip, query, key, value, long_out, grads, mixin, grad_long, summed):
    length, width = query.shape
    blocks = row_blocks(length)
    for start, size in blocks:
        row, grad_gated = kinds(parts, 0, start, size)
        at = pl.ds(row, size)
        mixin[0, at, :] = grad_gated * long_out[at, :]
        grad_long[at, :] = grad_gated * query[at, :]
    modal_scan(grad_long, summed, decay[...], spread[...], gain[...], True)
    for start, size in blocks:
        at = slice(start, start + size)
        grad_signal = summed[at, :] + skip[...] * grad_long[at, :]
        mixin[1, at, :] = grad_signal * value[at, :]
        mixin[2, at, :] = grad_signal * key[at, :]
    for j in range(3):
        mixin[j, length : length + MARGIN, :] = jnp.zeros((MARGIN, width), F32)
        for start, size in blocks:
            total = taps[j, 0:1, :] * mixin[j, start : start + size, :]
            for lag in range(1, taps.shape[1]):
                total = total + taps[j, lag : lag + 1, :] * mixin[j, start + lag : start + lag + size, :]
            grads[j, start : start + size, :] = total.astype(BF16)


def sum_of_three(parts, j, start, size):
    half = parts[0].shape[1]
    other, local = divmod(start, half)
    own, near, far = parts[3 * other : 3 * other + 3]
    at = slice(local, local + size)
    total = own[j, at, :] + near[j, at, :].astype(F32) + far[j, at, :].astype(F32)
    return pl.multiple_of(((lax.axis_index("ctx") >> 1) ^ other) * half + local, MARGIN), total


def plain(parts, j, start, size):
    return start, parts[0][j, start : start + size, :].astype(F32)


def filter_forward(parts, kinds, tables, length, width, after=()):
    count = len(parts)
    inputs = count + len(tables)

    def body(*refs):
        forward_body(refs[:count], kinds, *refs[count:inputs], *refs[inputs + len(after) :])

    wide = jax.ShapeDtypeStruct((length, width), F32)
    return call(
        body,
        (wide, wide, wide, wide, jax.ShapeDtypeStruct((length, width), BF16)),
        [
            pltpu.VMEM((3, MARGIN + length, width), F32),
            pltpu.VMEM((length, width), F32),
            pltpu.VMEM((length, width), F32),
        ],
        in_specs=[VMEM] * inputs + [HBM] * len(after),
        us=2.1,
    )(*parts, *tables, *after)


def filter_backward(parts, kinds, tables, saved, length, width, after=()):
    count = len(parts)
    inputs = count + len(tables) + len(saved)

    def body(*refs):
        backward_body(refs[:count], kinds, *refs[count:inputs], *refs[inputs + len(after) :])

    return call(
        body,
        jax.ShapeDtypeStruct((3, length, width), BF16),
        [
            pltpu.VMEM((3, length + MARGIN, width), F32),
            pltpu.VMEM((length, width), F32),
            pltpu.VMEM((length, width), F32),
        ],
        in_specs=[VMEM] * inputs + [HBM] * len(after),
        us=2.1,
    )(*parts, *tables, *saved, *after)


def later(value, *after):
    def body(*refs):
        pass

    return pl.pallas_call(
        body,
        out_shape=jax.ShapeDtypeStruct(value.shape, value.dtype),
        in_specs=[HBM] * (1 + len(after)),
        out_specs=HBM,
        input_output_aliases={0: 0},
        compiler_params=pltpu.CompilerParams(vmem_limit_bytes=SMALL_LIMIT),
        cost_estimate=cost(0.05),
    )(value, *after)


def column_blocks(rows):
    length, width = rows.shape[0], rows.shape[1] // 4

    def body(rows, own, near, far, arrived):
        me = lax.axis_index("ctx")
        side = lax.axis_index("fsdp") & 1
        copies = []
        for n, (mask, out) in enumerate(((2 ^ side, far), (1, near), (0, own))):
            copies.append(pltpu.make_async_copy(rows.at[:, block_at(me ^ mask, width)], out, arrived.at[n]))
            copies[-1].start()
        for copy in copies:
            copy.wait()

    block = jax.ShapeDtypeStruct((length, width), rows.dtype)
    return call(body, (block,) * 3, [pltpu.SemaphoreType.DMA((3,))], in_specs=[HBM], us=0.7)(rows)


def fetched(block):
    pairs = [(4 * f + k, 4 * f + (k ^ 2 ^ (f & 1))) for f in range(8) for k in range(4)]
    return lax.ppermute(block, ("fsdp", "ctx"), pairs)


def project(pieces, other, weight, after=()):
    groups, depth, channels = weight.shape
    part = pieces[0].shape[0]
    length = 2 * part
    width = channels // 4

    def body(first, second, weight, *refs):
        own, far, give, give_far, held, product = refs[len(after) :]
        me = lax.axis_index("ctx")
        core = (me ^ lax.axis_index("fsdp")) & 1 if other else me & 1
        held[block_at(core, part), :] = first[...]
        held[block_at(1 - core, part), :] = second[...]
        for j in range(groups):
            product[...] = dot(held[...], weight[j], (1, 0))
            own[j] = product[:, block_at(me, width)]
            far[j] = product[:, block_at(me ^ 2, width)].astype(BF16)
            give[j] = product[:, block_at(me ^ 1, width)].astype(BF16)
            give_far[j] = product[:, block_at(me ^ 3, width)].astype(BF16)

    sums = jax.ShapeDtypeStruct((groups, length, width), BF16)
    return call(
        body,
        (jax.ShapeDtypeStruct((groups, length, width), F32), sums, sums, sums),
        [pltpu.VMEM((length, depth), BF16), pltpu.VMEM((length, channels), F32)],
        in_specs=[VMEM] * 3 + [HBM] * len(after),
        us=0.45 * groups,
    )(*pieces, weight, *after)


def add_far(left, right, after):
    def body(left, right, *refs):
        refs[-1][...] = (left[...].astype(F32) + right[...].astype(F32)).astype(BF16)

    specs = [VMEM] * 2 + [HBM] * len(after)
    return call(body, jax.ShapeDtypeStruct(left.shape, BF16), in_specs=specs)(left, right, *after)


def channel_sums(pieces, other, weight, after=(), after_add=()):
    own, far, give, give_far = project(pieces, other, weight, after)
    passed = add_far(far, flipped(give_far, "ctx", 1), after_add)
    return (own, flipped(give, "ctx", 1), flipped(passed, "ctx", 2)), passed


def by_token(here, there):
    return here[0], here[1], there[2], there[0], there[1], here[2]


def all_channels(value, far):
    return value, far, flipped(value, "ctx", 1), flipped(far, "ctx", 1)


def output_pieces(gathered, weight, after=()):
    groups, length, width = gathered[0].shape
    piece = weight.shape[1] // 4
    part = length // 4
    channels = 4 * width

    def product(whole, weight, at, index):
        total = None
        for j in range(groups):
            term = dot(whole[j, at, :], weight[j, block_at(index, piece), :], (1, 1))
            total = term if total is None else total + term
        return total.astype(BF16)

    def pieces(whole, weight, side, low, first, second):
        first[...] = product(whole, weight, slice(None), 2 * side)
        for high in range(2):
            rows = slice(high * part, (high + 1) * part)
            for s in range(2):
                columns = slice(s * piece, (s + 1) * piece)
                second[rows, columns] = product(whole, weight, block_at(2 * high + low, part), 2 * s + 1)

    def first_body(own, far, near, near_far, weight, *refs):
        whole, first, second = refs[len(after) :]
        me = lax.axis_index("ctx")
        place = lax.axis_index("fsdp")
        for j in range(groups):
            for mask, value in ((0, own), (2, far), (1, near), (3, near_far)):
                whole[j, :, block_at(me ^ mask, width)] = value[j]
        pieces(whole, weight, 1 - (place & 1), 1 - ((place >> 1) & 1), first, second)

    def second_body(whole, weight, first, second):
        place = lax.axis_index("fsdp")
        pieces(whole, weight, place & 1, (place >> 1) & 1, first, second)

    parts = (jax.ShapeDtypeStruct((length, piece), BF16), jax.ShapeDtypeStruct((2 * part, 2 * piece), BF16))
    whole, *gives = call(
        first_body,
        (jax.ShapeDtypeStruct((groups, length, channels), BF16), *parts),
        in_specs=[VMEM] * 5 + [HBM] * len(after),
        us=0.6 * groups,
    )(*gathered, weight, *after)
    keeps = call(second_body, parts, us=0.4 * groups)(whole, weight)
    return whole, keeps, gives


def exchange(gives):
    return flipped(gives[0], "fsdp", 1), flipped(gives[1], "fsdp", 2)


def final_pairs(flip):
    pairs = []
    for f in range(8):
        for k in range(4):
            high, low, x, y, core = f >> 2, (f >> 1) & 1, f & 1, k >> 1, k & 1
            pairs.append((4 * f + k, 4 * (4 * (y ^ high ^ flip) + 2 * core + x) + 2 * y + low))
    return pairs


def block_sums(keeps, givens, after=(), after_second=()):
    length, piece = keeps[0].shape
    part = length // 4
    both = lambda keep, given, rows, columns: keep[rows, columns].astype(F32) + given[rows, columns].astype(F32)

    def second_body(keep_x, given_x, keep_z, given_z, *refs):
        give_z, give_x, next_z, next_x = refs[len(after) :]
        place = lax.axis_index("fsdp")
        side, low = place & 1, (place >> 1) & 1
        for high in range(2):
            rows = slice(high * part, (high + 1) * part)
            take = lambda bit: both(keep_x, given_x, block_at(2 * high + bit, part), slice(None))
            give_z[rows, :] = take(1 - low).astype(BF16)
            next_z[rows, :] = take(low)
        take = lambda bit: both(keep_z, given_z, slice(None), block_at(bit, piece))
        give_x[...] = take(1 - side).astype(BF16)
        next_x[...] = take(side)

    square = lambda kind: jax.ShapeDtypeStruct((2 * part, piece), kind)
    give_z, give_x, next_z, next_x = call(
        second_body,
        (square(BF16), square(BF16), square(F32), square(F32)),
        in_specs=[VMEM] * 4 + [HBM] * len(after),
    )(keeps[0], givens[0], keeps[1], givens[1], *after)

    def third_body(keep_z, given_z, keep_x, given_x, *refs):
        give, keep = refs[len(after_second) :]
        y = lax.axis_index("ctx") >> 1
        for bit, out in ((1 - y, give), (y, keep)):
            at = block_at(bit, part)
            for half, (mine, other) in enumerate(((keep_z, given_z), (keep_x, given_x))):
                columns = slice(half * piece, (half + 1) * piece)
                out[:, columns] = both(mine, other, at, slice(None)).astype(BF16)

    block = jax.ShapeDtypeStruct((part, 2 * piece), BF16)
    give, keep = call(third_body, (block, block), in_specs=[VMEM] * 4 + [HBM] * len(after_second))(
        next_z, flipped(give_z, "fsdp", 2), next_x, flipped(give_x, "fsdp", 1), *after_second
    )

    def order_body(keep, given, first, second):
        high = lax.axis_index("fsdp") >> 2
        swap = high == 1
        first[...] = jnp.where(swap, given[...].astype(F32), keep[...].astype(F32)).astype(BF16)
        second[...] = jnp.where(swap, keep[...].astype(F32), given[...].astype(F32)).astype(BF16)

    blocks = call(order_body, (block, block))(keep, flipped(give, "ctx", 2))
    arrived = [lax.ppermute(value, ("fsdp", "ctx"), final_pairs(flip)) for flip, value in enumerate(blocks)]

    def last_body(first, second, out):
        out[...] = (first[...].astype(F32) + second[...].astype(F32)).astype(BF16)

    return call(last_body, block)(*arrived), give


def turned(pieces):
    part, depth = pieces[0].shape

    def body(a, b, c, d, out):
        me = lax.axis_index("ctx")
        side = lax.axis_index("fsdp") & 1
        for mask, piece in ((0, a), (1, b), (2 ^ side, c), (3 ^ side, d)):
            out[:, block_at(me ^ mask, part)] = piece[...].T

    return call(body, jax.ShapeDtypeStruct((depth, 4 * part), pieces[0].dtype), us=0.4)(*pieces)


def weight_gradient(rows, values, after=()):
    depth, length = rows.shape
    groups, _, channels = values.shape
    tile = depth // 2

    def body(rows, values, *refs):
        out, mark = refs[len(after) :]
        out[0] = dot(rows[...], values[0], (1, 0))
        mark[...] = jnp.zeros_like(mark)

    return pl.pallas_call(
        body,
        out_shape=(jax.ShapeDtypeStruct((groups, depth, channels), F32), jax.ShapeDtypeStruct((8, LANES), F32)),
        grid=(groups, depth // tile),
        in_specs=[
            pl.BlockSpec((tile, length), lambda j, i: (i, 0)),
            pl.BlockSpec((1, length, channels), lambda j, i: (j, 0, 0)),
        ]
        + [HBM] * len(after),
        out_specs=(pl.BlockSpec((1, tile, channels), lambda j, i: (j, i, 0)), pl.BlockSpec((8, LANES), lambda j, i: (0, 0))),
        compiler_params=pltpu.CompilerParams(vmem_limit_bytes=VMEM_LIMIT),
        cost_estimate=cost(1.5 * groups),
    )(rows, values, *after)


def four_by_eight(tokens, weights, tables, out_weight, grad_mixed):
    length, width = 4 * tokens.shape[0], weights.shape[2] // 4
    own, near, far = column_blocks(tokens)
    here = (own, flipped(near, "ctx", 1))
    feats_here, passed = channel_sums(here, 0, weights)
    far = later(fetched(far), passed, *tables)
    there = (far, flipped(far, "fsdp", 1))
    grad_own, grad_near, grad_far = column_blocks(grad_mixed)
    grad_here = (grad_own, flipped(grad_near, "ctx", 1))
    grad_far = fetched(later(grad_far, far))
    grad_there = (grad_far, flipped(grad_far, "fsdp", 1))
    feats_there, passed = channel_sums(there, 1, weights, feats_here[2:], (grad_far,))
    grads_here, _ = channel_sums(grad_here, 0, out_weight[None], (passed,))
    feats = by_token(feats_here, feats_there)
    *saved, gated = filter_forward(feats, sum_of_three, tables, length, width, grads_here[2:])
    grads_there, _ = channel_sums(grad_there, 1, out_weight[None], (gated,))
    gated = gated[None]
    gated_far = flipped(gated, "ctx", 2)
    all_gated = all_channels(gated, gated_far)
    whole_gated, keeps, gives = output_pieces(all_gated, out_weight[None])
    givens = exchange(gives)
    mixed_halves = keeps, givens
    grads = filter_backward(by_token(grads_here, grads_there), sum_of_three, tables, saved, length, width)
    grads = later(grads, gated_far)
    grad_out, mark = weight_gradient(turned(grad_here + grad_there), whole_gated)
    token_rows = turned(here + there)
    grads_far = later(flipped(grads, "ctx", 2), *givens, keeps[0], token_rows, mark)
    whole_grads, keeps, gives = output_pieces(all_channels(grads, grads_far), weights)
    mixed, mixed_give = block_sums(*mixed_halves, (), gives[:1])
    grad_in, mark = weight_gradient(token_rows, whole_grads, (mixed_give,))
    grad_tokens, _ = block_sums(keeps, exchange(gives), (mark,))
    return mixed, grad_tokens, grad_in, grad_out[0]


def any_mesh(tokens, weights, tables, out_weight, grad_mixed):
    count = lax.axis_size("ctx")
    columns = lambda rows: lax.all_to_all(rows, "ctx", split_axis=1, concat_axis=0, tiled=True)
    whole_tokens, whole_cotangents = columns(tokens), columns(grad_mixed)
    length, width = whole_tokens.shape[0], weights.shape[2] // count

    def channel_sums(rows, weight):
        partial = jnp.einsum("td,jdc->jtc", rows, weight, preferred_element_type=F32)
        return lax.psum_scatter(partial.astype(BF16), "ctx", scatter_dimension=2, tiled=True)

    def block_sums(values, weight):
        partial = jnp.einsum("jtc,jdc->td", values, weight, preferred_element_type=F32)
        ratio = lax.axis_size("fsdp") // count
        pieces = partial.astype(BF16).reshape(count, length // count, ratio, -1).transpose(0, 2, 1, 3)
        pieces = pieces.reshape(count * ratio, length // count, -1)
        return to_placement(lax.psum_scatter(pieces, "fsdp", scatter_dimension=0, tiled=True)[0])

    feats = channel_sums(whole_tokens, weights)
    grad_gated = channel_sums(whole_cotangents, out_weight[None])
    *saved, gated = filter_forward((feats,), plain, tables, length, width)
    grads = filter_backward((grad_gated,), plain, tables, saved, length, width)
    whole_gated = lax.all_gather(gated, "ctx", axis=1, tiled=True)
    whole_grads = lax.all_gather(grads, "ctx", axis=2, tiled=True)
    mixed = block_sums(whole_gated[None], out_weight[None])
    grad_tokens = block_sums(whole_grads, weights)
    grad_in = jnp.einsum("td,jtc->jdc", whole_tokens, whole_grads, preferred_element_type=F32)
    grad_out = jnp.einsum("td,tc->dc", whole_cotangents, whole_gated, preferred_element_type=F32)
    return mixed, grad_tokens, grad_in, grad_out


def per_device(tokens, in_weight, conv_taps, decay_rate, residue, skip_gain, out_weight, grad_mixed):
    count, blocks = lax.axis_size("ctx"), lax.axis_size("fsdp")
    weights = in_weight.transpose(1, 0, 2)
    length = count * tokens.shape[0]
    width = weights.shape[2] // count
    mine = lambda table: lax.dynamic_slice_in_dim(table, lax.axis_index("ctx") * width, width, table.ndim - 1)
    rate = mine(decay_rate)
    gain = mine(residue) * jnp.sqrt(-jnp.expm1(-2.0 * rate))
    tables = (mine(conv_taps.transpose(1, 0, 2)), jnp.exp(-rate), jnp.exp(-rate * (length // CHUNKS)), gain, mine(skip_gain[None]))
    tuned = count == 4 and blocks == 8 and width % LANES == 0 and tokens.shape[0] % LANES == 0
    plan = four_by_eight if tuned else any_mesh
    mixed, grad_tokens, grad_in, grad_out = plan(tokens, weights, tables, out_weight, grad_mixed)
    return mixed, grad_tokens, grad_in.transpose(1, 0, 2), grad_out


def solution(mesh):
    return jax.shard_map(
        per_device,
        mesh=mesh,
        in_specs=(
            P("ctx", None),
            P("ctx", None, "fsdp"),
            P(None, None, "fsdp"),
            P(None, "fsdp"),
            P(None, "fsdp"),
            P("fsdp"),
            P("ctx", "fsdp"),
            P("ctx", None),
        ),
        out_specs=(P("ctx", "fsdp"), P("ctx", "fsdp"), P("ctx", None, "fsdp"), P("ctx", "fsdp")),
        check_vma=False,
    )
```

```python
import functools

import jax
import jax.numpy as jnp
from jax import lax
from jax.experimental import pallas as pl
from jax.experimental.pallas import tpu as pltpu
from jax.sharding import PartitionSpec as P

BF16 = jnp.bfloat16
F32 = jnp.float32
LANES = 128
CHUNKS = 8
MARGIN = 8
VMEM_LIMIT = 16 * 1024 * 1024
SMALL_LIMIT = 4 * 1024 * 1024
FLOPS_PER_US = 1_150_000_000


VMEM = pl.BlockSpec(memory_space=pltpu.VMEM)
HBM = pl.BlockSpec(memory_space=pl.ANY)


def cost(us):
    return pl.CostEstimate(flops=int(us * FLOPS_PER_US), bytes_accessed=0, transcendentals=0)


def call(body, outs, scratch=(), in_specs=None, us=0.5):
    return pl.pallas_call(
        body,
        out_shape=outs,
        **({} if in_specs is None else {"in_specs": in_specs}),
        scratch_shapes=list(scratch),
        compiler_params=pltpu.CompilerParams(vmem_limit_bytes=VMEM_LIMIT),
        cost_estimate=cost(us),
    )


def flipped(value, axis, mask):
    count = lax.axis_size(axis)
    return lax.ppermute(value, axis, [(source, source ^ mask) for source in range(count)])


def block_at(index, size):
    return pl.ds(pl.multiple_of(index * size, size), size)


def to_placement(value):
    count = lax.axis_size("ctx")
    ratio = lax.axis_size("fsdp") // count
    pairs = []
    for f in range(ratio * count):
        for k in range(count):
            target = (k * ratio + f % ratio, f // ratio)
            pairs.append((f * count + k, target[0] * count + target[1]))
    return lax.ppermute(value, ("fsdp", "ctx"), pairs)


def dot(left, right, contract):
    return lax.dot_general(left, right, ((contract[:1], contract[1:]), ((), ())), preferred_element_type=F32)


def shifted(value, steps, backward):
    rows = lax.broadcasted_iota(jnp.int32, value.shape, 0)
    if backward:
        return jnp.where(rows < CHUNKS - steps, pltpu.roll(value, CHUNKS - steps, 0), 0.0)
    return jnp.where(rows >= steps, pltpu.roll(value, steps, 0), 0.0)


def modal_scan(source, target, decay, spread, gain, backward):
    poles, width = decay.shape
    steps = source.shape[0] // CHUNKS
    wide = lambda table, n: jnp.broadcast_to(table[n : n + 1, :], (CHUNKS, width))
    decays = [wide(decay, n) for n in range(poles)]

    def rows(i):
        return pl.ds(steps - 1 - i if backward else i, CHUNKS, stride=steps)

    def gather_up(i, states):
        entry = source[rows(i), :]
        return tuple(d * s + entry for d, s in zip(decays, states))

    zero = jnp.zeros((CHUNKS, width), F32)
    ends = lax.fori_loop(0, steps, gather_up, (zero,) * poles, unroll=4)
    states = []
    for n in range(poles):
        factor = wide(spread, n)
        state = shifted(ends[n], 1, backward)
        reach = 1
        while reach < CHUNKS:
            state = state + factor * shifted(state, reach, backward)
            factor = factor * factor
            reach *= 2
        states.append(state)
    gains = [wide(gain, n) for n in range(poles)]

    def advance(i, states):
        entry = source[rows(i), :]
        states = tuple(d * s + entry for d, s in zip(decays, states))
        terms = [g * s for g, s in zip(gains, states)]
        while len(terms) > 1:
            terms = [a + b for a, b in zip(terms[::2], terms[1::2])]
        target[rows(i), :] = terms[0]
        return states

    lax.fori_loop(0, steps, advance, tuple(states), unroll=2)


def row_blocks(length):
    size = 64 if length % 64 == 0 else length
    return [(start, size) for start in range(0, length, size)]


def forward_body(parts, kinds, taps, decay, spread, gain, skip, query, key, value, long_out, gated, feats, signal, summed):
    length, width = query.shape
    blocks = row_blocks(length)
    for j in range(3):
        feats[j, :MARGIN, :] = jnp.zeros((MARGIN, width), F32)
        for start, size in blocks:
            row, total = kinds(parts, j, start, size)
            feats[j, pl.ds(MARGIN + row, size), :] = total.astype(BF16).astype(F32)
    for start, size in blocks:
        mixed = []
        for j in range(3):
            total = taps[j, 0:1, :] * feats[j, MARGIN + start : MARGIN + start + size, :]
            for lag in range(1, taps.shape[1]):
                first = MARGIN + start - lag
                total = total + taps[j, lag : lag + 1, :] * feats[j, first : first + size, :]
            mixed.append(total)
        at = slice(start, start + size)
        query[at, :], key[at, :], value[at, :] = mixed
        signal[at, :] = mixed[1] * mixed[2]
    modal_scan(signal, summed, decay[...], spread[...], gain[...], False)
    for start, size in blocks:
        at = slice(start, start + size)
        result = summed[at, :] + skip[...] * signal[at, :]
        long_out[at, :] = result
        gated[at, :] = (query[at, :] * result).astype(BF16)


def backward_body(parts, kinds, taps, decay, spread, gain, skip, query, key, value, long_out, grads, mixin, grad_long, summed):
    length, width = query.shape
    blocks = row_blocks(length)
    for start, size in blocks:
        row, grad_gated = kinds(parts, 0, start, size)
        at = pl.ds(row, size)
        mixin[0, at, :] = grad_gated * long_out[at, :]
        grad_long[at, :] = grad_gated * query[at, :]
    modal_scan(grad_long, summed, decay[...], spread[...], gain[...], True)
    for start, size in blocks:
        at = slice(start, start + size)
        grad_signal = summed[at, :] + skip[...] * grad_long[at, :]
        mixin[1, at, :] = grad_signal * value[at, :]
        mixin[2, at, :] = grad_signal * key[at, :]
    for j in range(3):
        mixin[j, length : length + MARGIN, :] = jnp.zeros((MARGIN, width), F32)
        for start, size in blocks:
            total = taps[j, 0:1, :] * mixin[j, start : start + size, :]
            for lag in range(1, taps.shape[1]):
                total = total + taps[j, lag : lag + 1, :] * mixin[j, start + lag : start + lag + size, :]
            grads[j, start : start + size, :] = total.astype(BF16)


def sum_of_three(parts, j, start, size):
    half = parts[0].shape[1]
    other, local = divmod(start, half)
    own, near, far = parts[3 * other : 3 * other + 3]
    at = slice(local, local + size)
    total = own[j, at, :] + near[j, at, :].astype(F32) + far[j, at, :].astype(F32)
    return pl.multiple_of(((lax.axis_index("ctx") >> 1) ^ other) * half + local, MARGIN), total


def plain(parts, j, start, size):
    return start, parts[0][j, start : start + size, :].astype(F32)


def filter_forward(parts, kinds, tables, length, width, after=()):
    count = len(parts)
    inputs = count + len(tables)

    def body(*refs):
        forward_body(refs[:count], kinds, *refs[count:inputs], *refs[inputs + len(after) :])

    wide = jax.ShapeDtypeStruct((length, width), F32)
    return call(
        body,
        (wide, wide, wide, wide, jax.ShapeDtypeStruct((length, width), BF16)),
        [
            pltpu.VMEM((3, MARGIN + length, width), F32),
            pltpu.VMEM((length, width), F32),
            pltpu.VMEM((length, width), F32),
        ],
        in_specs=[VMEM] * inputs + [HBM] * len(after),
        us=2.1,
    )(*parts, *tables, *after)


def filter_backward(parts, kinds, tables, saved, length, width, after=()):
    count = len(parts)
    inputs = count + len(tables) + len(saved)

    def body(*refs):
        backward_body(refs[:count], kinds, *refs[count:inputs], *refs[inputs + len(after) :])

    return call(
        body,
        jax.ShapeDtypeStruct((3, length, width), BF16),
        [
            pltpu.VMEM((3, length + MARGIN, width), F32),
            pltpu.VMEM((length, width), F32),
            pltpu.VMEM((length, width), F32),
        ],
        in_specs=[VMEM] * inputs + [HBM] * len(after),
        us=2.1,
    )(*parts, *tables, *saved, *after)


def later(value, *after):
    def body(*refs):
        pass

    return pl.pallas_call(
        body,
        out_shape=jax.ShapeDtypeStruct(value.shape, value.dtype),
        in_specs=[HBM] * (1 + len(after)),
        out_specs=HBM,
        input_output_aliases={0: 0},
        compiler_params=pltpu.CompilerParams(vmem_limit_bytes=SMALL_LIMIT),
        cost_estimate=cost(0.05),
    )(value, *after)


def column_blocks(rows):
    length, width = rows.shape[0], rows.shape[1] // 4

    def body(rows, own, near, far, arrived):
        me = lax.axis_index("ctx")
        side = lax.axis_index("fsdp") & 1
        copies = []
        for n, (mask, out) in enumerate(((2 ^ side, far), (1, near), (0, own))):
            copies.append(pltpu.make_async_copy(rows.at[:, block_at(me ^ mask, width)], out, arrived.at[n]))
            copies[-1].start()
        for copy in copies:
            copy.wait()

    block = jax.ShapeDtypeStruct((length, width), rows.dtype)
    return call(body, (block,) * 3, [pltpu.SemaphoreType.DMA((3,))], in_specs=[HBM], us=0.7)(rows)


def fetched(block):
    pairs = [(4 * f + k, 4 * f + (k ^ 2 ^ (f & 1))) for f in range(8) for k in range(4)]
    return lax.ppermute(block, ("fsdp", "ctx"), pairs)


def project(pieces, other, weight, after=()):
    groups, depth, channels = weight.shape
    part = pieces[0].shape[0]
    length = 2 * part
    width = channels // 4

    def body(first, second, weight, *refs):
        own, far, give, give_far, held, product = refs[len(after) :]
        me = lax.axis_index("ctx")
        core = (me ^ lax.axis_index("fsdp")) & 1 if other else me & 1
        held[block_at(core, part), :] = first[...]
        held[block_at(1 - core, part), :] = second[...]
        for j in range(groups):
            product[...] = dot(held[...], weight[j], (1, 0))
            own[j] = product[:, block_at(me, width)]
            far[j] = product[:, block_at(me ^ 2, width)].astype(BF16)
            give[j] = product[:, block_at(me ^ 1, width)].astype(BF16)
            give_far[j] = product[:, block_at(me ^ 3, width)].astype(BF16)

    sums = jax.ShapeDtypeStruct((groups, length, width), BF16)
    return call(
        body,
        (jax.ShapeDtypeStruct((groups, length, width), F32), sums, sums, sums),
        [pltpu.VMEM((length, depth), BF16), pltpu.VMEM((length, channels), F32)],
        in_specs=[VMEM] * 3 + [HBM] * len(after),
        us=0.45 * groups,
    )(*pieces, weight, *after)


def add_far(left, right, after):
    def body(left, right, *refs):
        refs[-1][...] = (left[...].astype(F32) + right[...].astype(F32)).astype(BF16)

    specs = [VMEM] * 2 + [HBM] * len(after)
    return call(body, jax.ShapeDtypeStruct(left.shape, BF16), in_specs=specs)(left, right, *after)


def channel_sums(pieces, other, weight, after=(), after_add=()):
    own, far, give, give_far = project(pieces, other, weight, after)
    passed = add_far(far, flipped(give_far, "ctx", 1), after_add)
    return (own, flipped(give, "ctx", 1), flipped(passed, "ctx", 2)), passed


def by_token(here, there):
    return here[0], here[1], there[2], there[0], there[1], here[2]


def all_channels(value, far):
    return value, far, flipped(value, "ctx", 1), flipped(far, "ctx", 1)


def output_pieces(gathered, weight, after=()):
    groups, length, width = gathered[0].shape
    piece = weight.shape[1] // 4
    part = length // 4
    channels = 4 * width

    def product(whole, weight, at, index):
        total = None
        for j in range(groups):
            term = dot(whole[j, at, :], weight[j, block_at(index, piece), :], (1, 1))
            total = term if total is None else total + term
        return total.astype(BF16)

    def pieces(whole, weight, side, low, first, second):
        first[...] = product(whole, weight, slice(None), 2 * side)
        for high in range(2):
            rows = slice(high * part, (high + 1) * part)
            for s in range(2):
                columns = slice(s * piece, (s + 1) * piece)
                second[rows, columns] = product(whole, weight, block_at(2 * high + low, part), 2 * s + 1)

    def first_body(own, far, near, near_far, weight, *refs):
        whole, first, second = refs[len(after) :]
        me = lax.axis_index("ctx")
        place = lax.axis_index("fsdp")
        for j in range(groups):
            for mask, value in ((0, own), (2, far), (1, near), (3, near_far)):
                whole[j, :, block_at(me ^ mask, width)] = value[j]
        pieces(whole, weight, 1 - (place & 1), 1 - ((place >> 1) & 1), first, second)

    def second_body(whole, weight, first, second):
        place = lax.axis_index("fsdp")
        pieces(whole, weight, place & 1, (place >> 1) & 1, first, second)

    parts = (jax.ShapeDtypeStruct((length, piece), BF16), jax.ShapeDtypeStruct((2 * part, 2 * piece), BF16))
    whole, *gives = call(
        first_body,
        (jax.ShapeDtypeStruct((groups, length, channels), BF16), *parts),
        in_specs=[VMEM] * 5 + [HBM] * len(after),
        us=0.6 * groups,
    )(*gathered, weight, *after)
    keeps = call(second_body, parts, us=0.4 * groups)(whole, weight)
    return whole, keeps, gives


def exchange(gives):
    return flipped(gives[0], "fsdp", 1), flipped(gives[1], "fsdp", 2)


def final_pairs(flip):
    pairs = []
    for f in range(8):
        for k in range(4):
            high, low, x, y, core = f >> 2, (f >> 1) & 1, f & 1, k >> 1, k & 1
            pairs.append((4 * f + k, 4 * (4 * (y ^ high ^ flip) + 2 * core + x) + 2 * y + low))
    return pairs


def block_sums(keeps, givens, after=(), after_second=()):
    length, piece = keeps[0].shape
    part = length // 4
    both = lambda keep, given, rows, columns: keep[rows, columns].astype(F32) + given[rows, columns].astype(F32)

    def second_body(keep_x, given_x, keep_z, given_z, *refs):
        give_z, give_x, next_z, next_x = refs[len(after) :]
        place = lax.axis_index("fsdp")
        side, low = place & 1, (place >> 1) & 1
        for high in range(2):
            rows = slice(high * part, (high + 1) * part)
            take = lambda bit: both(keep_x, given_x, block_at(2 * high + bit, part), slice(None))
            give_z[rows, :] = take(1 - low).astype(BF16)
            next_z[rows, :] = take(low)
        take = lambda bit: both(keep_z, given_z, slice(None), block_at(bit, piece))
        give_x[...] = take(1 - side).astype(BF16)
        next_x[...] = take(side)

    square = lambda kind: jax.ShapeDtypeStruct((2 * part, piece), kind)
    give_z, give_x, next_z, next_x = call(
        second_body,
        (square(BF16), square(BF16), square(F32), square(F32)),
        in_specs=[VMEM] * 4 + [HBM] * len(after),
    )(keeps[0], givens[0], keeps[1], givens[1], *after)

    def third_body(keep_z, given_z, keep_x, given_x, *refs):
        give, keep = refs[len(after_second) :]
        y = lax.axis_index("ctx") >> 1
        for bit, out in ((1 - y, give), (y, keep)):
            at = block_at(bit, part)
            for half, (mine, other) in enumerate(((keep_z, given_z), (keep_x, given_x))):
                columns = slice(half * piece, (half + 1) * piece)
                out[:, columns] = both(mine, other, at, slice(None)).astype(BF16)

    block = jax.ShapeDtypeStruct((part, 2 * piece), BF16)
    give, keep = call(third_body, (block, block), in_specs=[VMEM] * 4 + [HBM] * len(after_second))(
        next_z, flipped(give_z, "fsdp", 2), next_x, flipped(give_x, "fsdp", 1), *after_second
    )

    def order_body(keep, given, first, second):
        high = lax.axis_index("fsdp") >> 2
        swap = high == 1
        first[...] = jnp.where(swap, given[...].astype(F32), keep[...].astype(F32)).astype(BF16)
        second[...] = jnp.where(swap, keep[...].astype(F32), given[...].astype(F32)).astype(BF16)

    blocks = call(order_body, (block, block))(keep, flipped(give, "ctx", 2))
    arrived = [lax.ppermute(value, ("fsdp", "ctx"), final_pairs(flip)) for flip, value in enumerate(blocks)]

    def last_body(first, second, out):
        out[...] = (first[...].astype(F32) + second[...].astype(F32)).astype(BF16)

    return call(last_body, block)(*arrived), give


def turned(pieces):
    part, depth = pieces[0].shape

    def body(a, b, c, d, out):
        me = lax.axis_index("ctx")
        side = lax.axis_index("fsdp") & 1
        for mask, piece in ((0, a), (1, b), (2 ^ side, c), (3 ^ side, d)):
            out[:, block_at(me ^ mask, part)] = piece[...].T

    return call(body, jax.ShapeDtypeStruct((depth, 4 * part), pieces[0].dtype), us=0.4)(*pieces)


def weight_gradient(rows, values, after=()):
    depth, length = rows.shape
    groups, _, channels = values.shape
    tile = 256
    steps = [(j, i) for j in range(groups) for i in range(depth // tile)]

    def body(rows, values, *refs):
        out, mark, ready, written = refs[len(after) :]
        copies = []
        for n, (j, i) in enumerate(steps):
            at = slice(i * tile, (i + 1) * tile)
            ready[j, at, :] = dot(rows[at, :], values[j], (1, 0))
            copies.append(pltpu.make_async_copy(ready.at[j, at, :], out.at[j, at, :], written.at[n]))
            copies[-1].start()
        mark[...] = jnp.zeros_like(mark)
        for copy in copies:
            copy.wait()

    gradient = jax.ShapeDtypeStruct((groups, depth, channels), F32)
    return pl.pallas_call(
        body,
        out_shape=(gradient, jax.ShapeDtypeStruct((8, LANES), F32)),
        in_specs=[VMEM] * 2 + [HBM] * len(after),
        out_specs=(HBM, VMEM),
        scratch_shapes=[pltpu.VMEM(gradient.shape, F32), pltpu.SemaphoreType.DMA((len(steps),))],
        compiler_params=pltpu.CompilerParams(vmem_limit_bytes=VMEM_LIMIT),
        cost_estimate=cost(1.0 * groups),
    )(rows, values, *after)


def four_by_eight(tokens, weights, tables, out_weight, grad_mixed):
    length, width = 4 * tokens.shape[0], weights.shape[2] // 4
    own, near, far = column_blocks(tokens)
    here = (own, flipped(near, "ctx", 1))
    feats_here, passed = channel_sums(here, 0, weights)
    far = later(fetched(far), passed, *tables)
    there = (far, flipped(far, "fsdp", 1))
    grad_own, grad_near, grad_far = column_blocks(grad_mixed)
    grad_here = (grad_own, flipped(grad_near, "ctx", 1))
    grad_far = fetched(later(grad_far, far))
    grad_there = (grad_far, flipped(grad_far, "fsdp", 1))
    feats_there, passed = channel_sums(there, 1, weights, feats_here[2:], (grad_far,))
    grads_here, _ = channel_sums(grad_here, 0, out_weight[None], (passed,))
    feats = by_token(feats_here, feats_there)
    *saved, gated = filter_forward(feats, sum_of_three, tables, length, width, grads_here[2:])
    grads_there, _ = channel_sums(grad_there, 1, out_weight[None], (gated,))
    gated = gated[None]
    gated_far = flipped(gated, "ctx", 2)
    grads = filter_backward(by_token(grads_here, grads_there), sum_of_three, tables, saved, length, width)
    grads = later(grads, gated_far)
    whole_gated, keeps, gives = output_pieces(all_channels(gated, later(gated_far, grads)), out_weight[None])
    givens = exchange(gives)
    mixed_halves = keeps, givens
    grad_out, mark = weight_gradient(turned(grad_here + grad_there), whole_gated)
    token_rows = turned(here + there)
    grads_far = later(flipped(grads, "ctx", 2), *givens, keeps[0], token_rows, mark)
    whole_grads, keeps, gives = output_pieces(all_channels(grads, grads_far), weights)
    mixed, mixed_give = block_sums(*mixed_halves, (), gives[:1])
    grad_in, mark = weight_gradient(token_rows, whole_grads, (mixed_give,))
    grad_tokens, _ = block_sums(keeps, exchange(gives), (mark,))
    return mixed, grad_tokens, grad_in, grad_out[0]


def any_mesh(tokens, weights, tables, out_weight, grad_mixed):
    count = lax.axis_size("ctx")
    columns = lambda rows: lax.all_to_all(rows, "ctx", split_axis=1, concat_axis=0, tiled=True)
    whole_tokens, whole_cotangents = columns(tokens), columns(grad_mixed)
    length, width = whole_tokens.shape[0], weights.shape[2] // count

    def channel_sums(rows, weight):
        partial = jnp.einsum("td,jdc->jtc", rows, weight, preferred_element_type=F32)
        return lax.psum_scatter(partial.astype(BF16), "ctx", scatter_dimension=2, tiled=True)

    def block_sums(values, weight):
        partial = jnp.einsum("jtc,jdc->td", values, weight, preferred_element_type=F32)
        ratio = lax.axis_size("fsdp") // count
        pieces = partial.astype(BF16).reshape(count, length // count, ratio, -1).transpose(0, 2, 1, 3)
        pieces = pieces.reshape(count * ratio, length // count, -1)
        return to_placement(lax.psum_scatter(pieces, "fsdp", scatter_dimension=0, tiled=True)[0])

    feats = channel_sums(whole_tokens, weights)
    grad_gated = channel_sums(whole_cotangents, out_weight[None])
    *saved, gated = filter_forward((feats,), plain, tables, length, width)
    grads = filter_backward((grad_gated,), plain, tables, saved, length, width)
    whole_gated = lax.all_gather(gated, "ctx", axis=1, tiled=True)
    whole_grads = lax.all_gather(grads, "ctx", axis=2, tiled=True)
    mixed = block_sums(whole_gated[None], out_weight[None])
    grad_tokens = block_sums(whole_grads, weights)
    grad_in = jnp.einsum("td,jtc->jdc", whole_tokens, whole_grads, preferred_element_type=F32)
    grad_out = jnp.einsum("td,tc->dc", whole_cotangents, whole_gated, preferred_element_type=F32)
    return mixed, grad_tokens, grad_in, grad_out


def per_device(tokens, in_weight, conv_taps, decay_rate, residue, skip_gain, out_weight, grad_mixed):
    count, blocks = lax.axis_size("ctx"), lax.axis_size("fsdp")
    weights = in_weight.transpose(1, 0, 2)
    length = count * tokens.shape[0]
    width = weights.shape[2] // count
    mine = lambda table: lax.dynamic_slice_in_dim(table, lax.axis_index("ctx") * width, width, table.ndim - 1)
    rate = mine(decay_rate)
    gain = mine(residue) * jnp.sqrt(-jnp.expm1(-2.0 * rate))
    tables = (mine(conv_taps.transpose(1, 0, 2)), jnp.exp(-rate), jnp.exp(-rate * (length // CHUNKS)), gain, mine(skip_gain[None]))
    tuned = count == 4 and blocks == 8 and width % LANES == 0 and tokens.shape[0] % LANES == 0
    plan = four_by_eight if tuned else any_mesh
    mixed, grad_tokens, grad_in, grad_out = plan(tokens, weights, tables, out_weight, grad_mixed)
    return mixed, grad_tokens, grad_in.transpose(1, 0, 2), grad_out


def solution(mesh):
    return jax.shard_map(
        per_device,
        mesh=mesh,
        in_specs=(
            P("ctx", None),
            P("ctx", None, "fsdp"),
            P(None, None, "fsdp"),
            P(None, "fsdp"),
            P(None, "fsdp"),
            P("fsdp"),
            P("ctx", "fsdp"),
            P("ctx", None),
        ),
        out_specs=(P("ctx", "fsdp"), P("ctx", "fsdp"), P("ctx", None, "fsdp"), P("ctx", "fsdp")),
        check_vma=False,
    )
```

```python
import functools

import jax
import jax.numpy as jnp
from jax import lax
from jax.experimental import pallas as pl
from jax.experimental.pallas import tpu as pltpu
from jax.sharding import PartitionSpec as P

BF16 = jnp.bfloat16
F32 = jnp.float32
LANES = 128
CHUNKS = 8
MARGIN = 8
VMEM_LIMIT = 16 * 1024 * 1024
SMALL_LIMIT = 4 * 1024 * 1024
FLOPS_PER_US = 1_150_000_000


VMEM = pl.BlockSpec(memory_space=pltpu.VMEM)
HBM = pl.BlockSpec(memory_space=pl.ANY)


def cost(us):
    return pl.CostEstimate(flops=int(us * FLOPS_PER_US), bytes_accessed=0, transcendentals=0)


def call(body, outs, scratch=(), in_specs=None, us=0.5):
    return pl.pallas_call(
        body,
        out_shape=outs,
        **({} if in_specs is None else {"in_specs": in_specs}),
        scratch_shapes=list(scratch),
        compiler_params=pltpu.CompilerParams(vmem_limit_bytes=VMEM_LIMIT),
        cost_estimate=cost(us),
    )


def flipped(value, axis, mask):
    count = lax.axis_size(axis)
    return lax.ppermute(value, axis, [(source, source ^ mask) for source in range(count)])


def block_at(index, size):
    return pl.ds(pl.multiple_of(index * size, size), size)


def to_placement(value):
    count = lax.axis_size("ctx")
    ratio = lax.axis_size("fsdp") // count
    pairs = []
    for f in range(ratio * count):
        for k in range(count):
            target = (k * ratio + f % ratio, f // ratio)
            pairs.append((f * count + k, target[0] * count + target[1]))
    return lax.ppermute(value, ("fsdp", "ctx"), pairs)


def dot(left, right, contract):
    return lax.dot_general(left, right, ((contract[:1], contract[1:]), ((), ())), preferred_element_type=F32)


def shifted(value, steps, backward):
    rows = lax.broadcasted_iota(jnp.int32, value.shape, 0)
    if backward:
        return jnp.where(rows < CHUNKS - steps, pltpu.roll(value, CHUNKS - steps, 0), 0.0)
    return jnp.where(rows >= steps, pltpu.roll(value, steps, 0), 0.0)


def modal_scan(source, target, decay, spread, gain, backward):
    poles, width = decay.shape
    steps = source.shape[0] // CHUNKS
    wide = lambda table, n: jnp.broadcast_to(table[n : n + 1, :], (CHUNKS, width))
    decays = [wide(decay, n) for n in range(poles)]

    def rows(i):
        return pl.ds(steps - 1 - i if backward else i, CHUNKS, stride=steps)

    def gather_up(i, states):
        entry = source[rows(i), :]
        return tuple(d * s + entry for d, s in zip(decays, states))

    zero = jnp.zeros((CHUNKS, width), F32)
    ends = lax.fori_loop(0, steps, gather_up, (zero,) * poles, unroll=4)
    states = []
    for n in range(poles):
        factor = wide(spread, n)
        state = shifted(ends[n], 1, backward)
        reach = 1
        while reach < CHUNKS:
            state = state + factor * shifted(state, reach, backward)
            factor = factor * factor
            reach *= 2
        states.append(state)
    gains = [wide(gain, n) for n in range(poles)]

    def advance(i, states):
        entry = source[rows(i), :]
        states = tuple(d * s + entry for d, s in zip(decays, states))
        terms = [g * s for g, s in zip(gains, states)]
        while len(terms) > 1:
            terms = [a + b for a, b in zip(terms[::2], terms[1::2])]
        target[rows(i), :] = terms[0]
        return states

    lax.fori_loop(0, steps, advance, tuple(states), unroll=2)


def row_blocks(length):
    size = 64 if length % 64 == 0 else length
    return [(start, size) for start in range(0, length, size)]


def forward_body(parts, kinds, taps, decay, spread, gain, skip, query, key, value, long_out, gated, feats, signal, summed):
    length, width = query.shape
    blocks = row_blocks(length)
    for j in range(3):
        feats[j, :MARGIN, :] = jnp.zeros((MARGIN, width), F32)
        for start, size in blocks:
            row, total = kinds(parts, j, start, size)
            feats[j, pl.ds(MARGIN + row, size), :] = total.astype(BF16).astype(F32)
    for start, size in blocks:
        mixed = []
        for j in range(3):
            total = taps[j, 0:1, :] * feats[j, MARGIN + start : MARGIN + start + size, :]
            for lag in range(1, taps.shape[1]):
                first = MARGIN + start - lag
                total = total + taps[j, lag : lag + 1, :] * feats[j, first : first + size, :]
            mixed.append(total)
        at = slice(start, start + size)
        query[at, :], key[at, :], value[at, :] = mixed
        signal[at, :] = mixed[1] * mixed[2]
    modal_scan(signal, summed, decay[...], spread[...], gain[...], False)
    for start, size in blocks:
        at = slice(start, start + size)
        result = summed[at, :] + skip[...] * signal[at, :]
        long_out[at, :] = result
        gated[at, :] = (query[at, :] * result).astype(BF16)


def backward_body(parts, kinds, taps, decay, spread, gain, skip, query, key, value, long_out, grads, mixin, grad_long, summed):
    length, width = query.shape
    blocks = row_blocks(length)
    for start, size in blocks:
        row, grad_gated = kinds(parts, 0, start, size)
        at = pl.ds(row, size)
        mixin[0, at, :] = grad_gated * long_out[at, :]
        grad_long[at, :] = grad_gated * query[at, :]
    modal_scan(grad_long, summed, decay[...], spread[...], gain[...], True)
    for start, size in blocks:
        at = slice(start, start + size)
        grad_signal = summed[at, :] + skip[...] * grad_long[at, :]
        mixin[1, at, :] = grad_signal * value[at, :]
        mixin[2, at, :] = grad_signal * key[at, :]
    for j in range(3):
        mixin[j, length : length + MARGIN, :] = jnp.zeros((MARGIN, width), F32)
        for start, size in blocks:
            total = taps[j, 0:1, :] * mixin[j, start : start + size, :]
            for lag in range(1, taps.shape[1]):
                total = total + taps[j, lag : lag + 1, :] * mixin[j, start + lag : start + lag + size, :]
            grads[j, start : start + size, :] = total.astype(BF16)


def sum_of_three(parts, j, start, size):
    half = parts[0].shape[1]
    other, local = divmod(start, half)
    own, near, far = parts[3 * other : 3 * other + 3]
    at = slice(local, local + size)
    total = own[j, at, :] + near[j, at, :].astype(F32) + far[j, at, :].astype(F32)
    return pl.multiple_of(((lax.axis_index("ctx") >> 1) ^ other) * half + local, MARGIN), total


def plain(parts, j, start, size):
    return start, parts[0][j, start : start + size, :].astype(F32)


def filter_forward(parts, kinds, tables, length, width, after=()):
    count = len(parts)
    inputs = count + len(tables)

    def body(*refs):
        forward_body(refs[:count], kinds, *refs[count:inputs], *refs[inputs + len(after) :])

    wide = jax.ShapeDtypeStruct((length, width), F32)
    return call(
        body,
        (wide, wide, wide, wide, jax.ShapeDtypeStruct((length, width), BF16)),
        [
            pltpu.VMEM((3, MARGIN + length, width), F32),
            pltpu.VMEM((length, width), F32),
            pltpu.VMEM((length, width), F32),
        ],
        in_specs=[VMEM] * inputs + [HBM] * len(after),
        us=2.1,
    )(*parts, *tables, *after)


def filter_backward(parts, kinds, tables, saved, length, width, after=()):
    count = len(parts)
    inputs = count + len(tables) + len(saved)

    def body(*refs):
        backward_body(refs[:count], kinds, *refs[count:inputs], *refs[inputs + len(after) :])

    return call(
        body,
        jax.ShapeDtypeStruct((3, length, width), BF16),
        [
            pltpu.VMEM((3, length + MARGIN, width), F32),
            pltpu.VMEM((length, width), F32),
            pltpu.VMEM((length, width), F32),
        ],
        in_specs=[VMEM] * inputs + [HBM] * len(after),
        us=2.1,
    )(*parts, *tables, *saved, *after)


def later(value, *after):
    def body(*refs):
        pass

    return pl.pallas_call(
        body,
        out_shape=jax.ShapeDtypeStruct(value.shape, value.dtype),
        in_specs=[HBM] * (1 + len(after)),
        out_specs=HBM,
        input_output_aliases={0: 0},
        compiler_params=pltpu.CompilerParams(vmem_limit_bytes=SMALL_LIMIT),
        cost_estimate=cost(0.05),
    )(value, *after)


def column_blocks(rows):
    length, width = rows.shape[0], rows.shape[1] // 4

    def body(rows, own, near, far, arrived):
        me = lax.axis_index("ctx")
        side = lax.axis_index("fsdp") & 1
        copies = []
        for n, (mask, out) in enumerate(((2 ^ side, far), (1, near), (0, own))):
            copies.append(pltpu.make_async_copy(rows.at[:, block_at(me ^ mask, width)], out, arrived.at[n]))
            copies[-1].start()
        for copy in copies:
            copy.wait()

    block = jax.ShapeDtypeStruct((length, width), rows.dtype)
    return call(body, (block,) * 3, [pltpu.SemaphoreType.DMA((3,))], in_specs=[HBM], us=0.7)(rows)


def fetched(block):
    pairs = [(4 * f + k, 4 * f + (k ^ 2 ^ (f & 1))) for f in range(8) for k in range(4)]
    return lax.ppermute(block, ("fsdp", "ctx"), pairs)


def project(pieces, other, weight, after=()):
    groups, depth, channels = weight.shape
    part = pieces[0].shape[0]
    length = 2 * part
    width = channels // 4

    def body(first, second, weight, *refs):
        own, far, give, give_far, held, product = refs[len(after) :]
        me = lax.axis_index("ctx")
        core = (me ^ lax.axis_index("fsdp")) & 1 if other else me & 1
        held[block_at(core, part), :] = first[...]
        held[block_at(1 - core, part), :] = second[...]
        for j in range(groups):
            product[...] = dot(held[...], weight[j], (1, 0))
            own[j] = product[:, block_at(me, width)]
            far[j] = product[:, block_at(me ^ 2, width)].astype(BF16)
            give[j] = product[:, block_at(me ^ 1, width)].astype(BF16)
            give_far[j] = product[:, block_at(me ^ 3, width)].astype(BF16)

    sums = jax.ShapeDtypeStruct((groups, length, width), BF16)
    return call(
        body,
        (jax.ShapeDtypeStruct((groups, length, width), F32), sums, sums, sums),
        [pltpu.VMEM((length, depth), BF16), pltpu.VMEM((length, channels), F32)],
        in_specs=[VMEM] * 3 + [HBM] * len(after),
        us=0.45 * groups,
    )(*pieces, weight, *after)


def add_far(left, right, after):
    def body(left, right, *refs):
        refs[-1][...] = (left[...].astype(F32) + right[...].astype(F32)).astype(BF16)

    specs = [VMEM] * 2 + [HBM] * len(after)
    return call(body, jax.ShapeDtypeStruct(left.shape, BF16), in_specs=specs)(left, right, *after)


def channel_sums(pieces, other, weight, after=(), after_add=()):
    own, far, give, give_far = project(pieces, other, weight, after)
    passed = add_far(far, flipped(give_far, "ctx", 1), after_add)
    return (own, flipped(give, "ctx", 1), flipped(passed, "ctx", 2)), passed


def by_token(here, there):
    return here[0], here[1], there[2], there[0], there[1], here[2]


def all_channels(value, far):
    return value, far, flipped(value, "ctx", 1), flipped(far, "ctx", 1)


def output_pieces(gathered, weight, after=()):
    groups, length, width = gathered[0].shape
    piece = weight.shape[1] // 4
    part = length // 4
    channels = 4 * width

    def product(whole, weight, at, index):
        total = None
        for j in range(groups):
            term = dot(whole[j, at, :], weight[j, block_at(index, piece), :], (1, 1))
            total = term if total is None else total + term
        return total.astype(BF16)

    def pieces(whole, weight, side, low, first, second):
        first[...] = product(whole, weight, slice(None), 2 * side)
        for high in range(2):
            rows = slice(high * part, (high + 1) * part)
            for s in range(2):
                columns = slice(s * piece, (s + 1) * piece)
                second[rows, columns] = product(whole, weight, block_at(2 * high + low, part), 2 * s + 1)

    def first_body(own, far, near, near_far, weight, *refs):
        whole, first, second = refs[len(after) :]
        me = lax.axis_index("ctx")
        place = lax.axis_index("fsdp")
        for j in range(groups):
            for mask, value in ((0, own), (2, far), (1, near), (3, near_far)):
                whole[j, :, block_at(me ^ mask, width)] = value[j]
        pieces(whole, weight, 1 - (place & 1), 1 - ((place >> 1) & 1), first, second)

    def second_body(whole, weight, first, second):
        place = lax.axis_index("fsdp")
        pieces(whole, weight, place & 1, (place >> 1) & 1, first, second)

    parts = (jax.ShapeDtypeStruct((length, piece), BF16), jax.ShapeDtypeStruct((2 * part, 2 * piece), BF16))
    whole, *gives = call(
        first_body,
        (jax.ShapeDtypeStruct((groups, length, channels), BF16), *parts),
        in_specs=[VMEM] * 5 + [HBM] * len(after),
        us=0.6 * groups,
    )(*gathered, weight, *after)
    keeps = call(second_body, parts, us=0.4 * groups)(whole, weight)
    return whole, keeps, gives


def exchange(gives):
    return flipped(gives[0], "fsdp", 1), flipped(gives[1], "fsdp", 2)


def final_pairs(flip):
    pairs = []
    for f in range(8):
        for k in range(4):
            high, low, x, y, core = f >> 2, (f >> 1) & 1, f & 1, k >> 1, k & 1
            pairs.append((4 * f + k, 4 * (4 * (y ^ high ^ flip) + 2 * core + x) + 2 * y + low))
    return pairs


def block_sums(keeps, givens, after=(), after_second=()):
    length, piece = keeps[0].shape
    part = length // 4
    both = lambda keep, given, rows, columns: keep[rows, columns].astype(F32) + given[rows, columns].astype(F32)

    def second_body(keep_x, given_x, keep_z, given_z, *refs):
        give_z, give_x, next_z, next_x = refs[len(after) :]
        place = lax.axis_index("fsdp")
        side, low = place & 1, (place >> 1) & 1
        for high in range(2):
            rows = slice(high * part, (high + 1) * part)
            take = lambda bit: both(keep_x, given_x, block_at(2 * high + bit, part), slice(None))
            give_z[rows, :] = take(1 - low).astype(BF16)
            next_z[rows, :] = take(low)
        take = lambda bit: both(keep_z, given_z, slice(None), block_at(bit, piece))
        give_x[...] = take(1 - side).astype(BF16)
        next_x[...] = take(side)

    square = lambda kind: jax.ShapeDtypeStruct((2 * part, piece), kind)
    give_z, give_x, next_z, next_x = call(
        second_body,
        (square(BF16), square(BF16), square(F32), square(F32)),
        in_specs=[VMEM] * 4 + [HBM] * len(after),
    )(keeps[0], givens[0], keeps[1], givens[1], *after)

    def third_body(keep_z, given_z, keep_x, given_x, *refs):
        give, keep = refs[len(after_second) :]
        y = lax.axis_index("ctx") >> 1
        for bit, out in ((1 - y, give), (y, keep)):
            at = block_at(bit, part)
            for half, (mine, other) in enumerate(((keep_z, given_z), (keep_x, given_x))):
                columns = slice(half * piece, (half + 1) * piece)
                out[:, columns] = both(mine, other, at, slice(None)).astype(BF16)

    block = jax.ShapeDtypeStruct((part, 2 * piece), BF16)
    give, keep = call(third_body, (block, block), in_specs=[VMEM] * 4 + [HBM] * len(after_second))(
        next_z, flipped(give_z, "fsdp", 2), next_x, flipped(give_x, "fsdp", 1), *after_second
    )

    def order_body(keep, given, first, second):
        high = lax.axis_index("fsdp") >> 2
        swap = high == 1
        first[...] = jnp.where(swap, given[...].astype(F32), keep[...].astype(F32)).astype(BF16)
        second[...] = jnp.where(swap, keep[...].astype(F32), given[...].astype(F32)).astype(BF16)

    blocks = call(order_body, (block, block))(keep, flipped(give, "ctx", 2))
    arrived = [lax.ppermute(value, ("fsdp", "ctx"), final_pairs(flip)) for flip, value in enumerate(blocks)]

    def last_body(first, second, out):
        out[...] = (first[...].astype(F32) + second[...].astype(F32)).astype(BF16)

    return call(last_body, block)(*arrived), give


def turned(pieces):
    part, depth = pieces[0].shape

    def body(a, b, c, d, out):
        me = lax.axis_index("ctx")
        side = lax.axis_index("fsdp") & 1
        for mask, piece in ((0, a), (1, b), (2 ^ side, c), (3 ^ side, d)):
            out[:, block_at(me ^ mask, part)] = piece[...].T

    return call(body, jax.ShapeDtypeStruct((depth, 4 * part), pieces[0].dtype), us=0.4)(*pieces)


def weight_gradient(rows, values, after=()):
    depth, length = rows.shape
    groups, _, channels = values.shape
    tile = 256
    steps = [(j, i) for j in range(groups) for i in range(depth // tile)]

    def body(rows, values, *refs):
        out, mark, ready, written = refs[len(after) :]
        copies = []
        for n, (j, i) in enumerate(steps):
            at = slice(i * tile, (i + 1) * tile)
            ready[j, at, :] = dot(rows[at, :], values[j], (1, 0))
            copies.append(pltpu.make_async_copy(ready.at[j, at, :], out.at[j, at, :], written.at[n]))
            copies[-1].start()
        mark[...] = jnp.zeros_like(mark)
        for copy in copies:
            copy.wait()

    gradient = jax.ShapeDtypeStruct((groups, depth, channels), F32)
    return pl.pallas_call(
        body,
        out_shape=(gradient, jax.ShapeDtypeStruct((8, LANES), F32)),
        in_specs=[VMEM] * 2 + [HBM] * len(after),
        out_specs=(HBM, VMEM),
        scratch_shapes=[pltpu.VMEM(gradient.shape, F32), pltpu.SemaphoreType.DMA((len(steps),))],
        compiler_params=pltpu.CompilerParams(vmem_limit_bytes=VMEM_LIMIT),
        cost_estimate=cost(1.0 * groups),
    )(rows, values, *after)


def four_by_eight(tokens, weights, tables, out_weight, grad_mixed):
    length, width = 4 * tokens.shape[0], weights.shape[2] // 4
    own, near, far = column_blocks(tokens)
    here = (own, flipped(near, "ctx", 1))
    feats_here, passed = channel_sums(here, 0, weights)
    far = later(fetched(far), passed, *tables)
    there = (far, flipped(far, "fsdp", 1))
    grad_own, grad_near, grad_far = column_blocks(grad_mixed)
    grad_here = (grad_own, flipped(grad_near, "ctx", 1))
    grad_far = fetched(later(grad_far, far))
    grad_there = (grad_far, flipped(grad_far, "fsdp", 1))
    feats_there, passed = channel_sums(there, 1, weights, feats_here[2:], (grad_far,))
    grads_here, _ = channel_sums(grad_here, 0, out_weight[None], (passed,))
    feats = by_token(feats_here, feats_there)
    *saved, gated = filter_forward(feats, sum_of_three, tables, length, width, (grads_here[2], grad_there[1]))
    grads_there, _ = channel_sums(grad_there, 1, out_weight[None], (gated,))
    gated = gated[None]
    gated_far = flipped(gated, "ctx", 2)
    grads = filter_backward(by_token(grads_here, grads_there), sum_of_three, tables, saved, length, width)
    grads = later(grads, gated_far)
    whole_gated, keeps, gives = output_pieces(all_channels(gated, later(gated_far, grads)), out_weight[None])
    givens = exchange(gives)
    mixed_halves = keeps, givens
    grad_out, mark = weight_gradient(turned(grad_here + grad_there), whole_gated)
    token_rows = turned(here + there)
    grads_far = later(flipped(grads, "ctx", 2), *givens, keeps[0], token_rows, mark)
    whole_grads, keeps, gives = output_pieces(all_channels(grads, grads_far), weights)
    mixed, mixed_give = block_sums(*mixed_halves, (), gives[:1])
    grad_in, mark = weight_gradient(token_rows, whole_grads, (mixed_give,))
    grad_tokens, _ = block_sums(keeps, exchange(gives), (mark,))
    return mixed, grad_tokens, grad_in, grad_out[0]


def any_mesh(tokens, weights, tables, out_weight, grad_mixed):
    count = lax.axis_size("ctx")
    columns = lambda rows: lax.all_to_all(rows, "ctx", split_axis=1, concat_axis=0, tiled=True)
    whole_tokens, whole_cotangents = columns(tokens), columns(grad_mixed)
    length, width = whole_tokens.shape[0], weights.shape[2] // count

    def channel_sums(rows, weight):
        partial = jnp.einsum("td,jdc->jtc", rows, weight, preferred_element_type=F32)
        return lax.psum_scatter(partial.astype(BF16), "ctx", scatter_dimension=2, tiled=True)

    def block_sums(values, weight):
        partial = jnp.einsum("jtc,jdc->td", values, weight, preferred_element_type=F32)
        ratio = lax.axis_size("fsdp") // count
        pieces = partial.astype(BF16).reshape(count, length // count, ratio, -1).transpose(0, 2, 1, 3)
        pieces = pieces.reshape(count * ratio, length // count, -1)
        return to_placement(lax.psum_scatter(pieces, "fsdp", scatter_dimension=0, tiled=True)[0])

    feats = channel_sums(whole_tokens, weights)
    grad_gated = channel_sums(whole_cotangents, out_weight[None])
    *saved, gated = filter_forward((feats,), plain, tables, length, width)
    grads = filter_backward((grad_gated,), plain, tables, saved, length, width)
    whole_gated = lax.all_gather(gated, "ctx", axis=1, tiled=True)
    whole_grads = lax.all_gather(grads, "ctx", axis=2, tiled=True)
    mixed = block_sums(whole_gated[None], out_weight[None])
    grad_tokens = block_sums(whole_grads, weights)
    grad_in = jnp.einsum("td,jtc->jdc", whole_tokens, whole_grads, preferred_element_type=F32)
    grad_out = jnp.einsum("td,tc->dc", whole_cotangents, whole_gated, preferred_element_type=F32)
    return mixed, grad_tokens, grad_in, grad_out


def per_device(tokens, in_weight, conv_taps, decay_rate, residue, skip_gain, out_weight, grad_mixed):
    count, blocks = lax.axis_size("ctx"), lax.axis_size("fsdp")
    weights = in_weight.transpose(1, 0, 2)
    length = count * tokens.shape[0]
    width = weights.shape[2] // count
    mine = lambda table: lax.dynamic_slice_in_dim(table, lax.axis_index("ctx") * width, width, table.ndim - 1)
    rate = mine(decay_rate)
    gain = mine(residue) * jnp.sqrt(-jnp.expm1(-2.0 * rate))
    tables = (mine(conv_taps.transpose(1, 0, 2)), jnp.exp(-rate), jnp.exp(-rate * (length // CHUNKS)), gain, mine(skip_gain[None]))
    tuned = count == 4 and blocks == 8 and width % LANES == 0 and tokens.shape[0] % LANES == 0
    plan = four_by_eight if tuned else any_mesh
    mixed, grad_tokens, grad_in, grad_out = plan(tokens, weights, tables, out_weight, grad_mixed)
    return mixed, grad_tokens, grad_in.transpose(1, 0, 2), grad_out


def solution(mesh):
    return jax.shard_map(
        per_device,
        mesh=mesh,
        in_specs=(
            P("ctx", None),
            P("ctx", None, "fsdp"),
            P(None, None, "fsdp"),
            P(None, "fsdp"),
            P(None, "fsdp"),
            P("fsdp"),
            P("ctx", "fsdp"),
            P("ctx", None),
        ),
        out_specs=(P("ctx", "fsdp"), P("ctx", "fsdp"), P("ctx", None, "fsdp"), P("ctx", "fsdp")),
        check_vma=False,
    )
```

```python
import functools

import jax
import jax.numpy as jnp
from jax import lax
from jax.experimental import pallas as pl
from jax.experimental.pallas import tpu as pltpu
from jax.sharding import PartitionSpec as P

BF16 = jnp.bfloat16
F32 = jnp.float32
LANES = 128
CHUNKS = 8
MARGIN = 8
VMEM_LIMIT = 16 * 1024 * 1024
SMALL_LIMIT = 4 * 1024 * 1024
FLOPS_PER_US = 1_150_000_000


VMEM = pl.BlockSpec(memory_space=pltpu.VMEM)
HBM = pl.BlockSpec(memory_space=pl.ANY)


def cost(us):
    return pl.CostEstimate(flops=int(us * FLOPS_PER_US), bytes_accessed=0, transcendentals=0)


def call(body, outs, scratch=(), in_specs=None, us=0.5):
    return pl.pallas_call(
        body,
        out_shape=outs,
        **({} if in_specs is None else {"in_specs": in_specs}),
        scratch_shapes=list(scratch),
        compiler_params=pltpu.CompilerParams(vmem_limit_bytes=VMEM_LIMIT),
        cost_estimate=cost(us),
    )


def flipped(value, axis, mask):
    count = lax.axis_size(axis)
    return lax.ppermute(value, axis, [(source, source ^ mask) for source in range(count)])


def block_at(index, size):
    return pl.ds(pl.multiple_of(index * size, size), size)


def to_placement(value):
    count = lax.axis_size("ctx")
    ratio = lax.axis_size("fsdp") // count
    pairs = []
    for f in range(ratio * count):
        for k in range(count):
            target = (k * ratio + f % ratio, f // ratio)
            pairs.append((f * count + k, target[0] * count + target[1]))
    return lax.ppermute(value, ("fsdp", "ctx"), pairs)


def dot(left, right, contract):
    return lax.dot_general(left, right, ((contract[:1], contract[1:]), ((), ())), preferred_element_type=F32)


def shifted(value, steps, backward):
    rows = lax.broadcasted_iota(jnp.int32, value.shape, 0)
    if backward:
        return jnp.where(rows < CHUNKS - steps, pltpu.roll(value, CHUNKS - steps, 0), 0.0)
    return jnp.where(rows >= steps, pltpu.roll(value, steps, 0), 0.0)


def modal_scan(source, target, decay, spread, gain, backward):
    poles, width = decay.shape
    steps = source.shape[0] // CHUNKS
    wide = lambda table, n: jnp.broadcast_to(table[n : n + 1, :], (CHUNKS, width))
    decays = [wide(decay, n) for n in range(poles)]

    def rows(i):
        return pl.ds(steps - 1 - i if backward else i, CHUNKS, stride=steps)

    def gather_up(i, states):
        entry = source[rows(i), :]
        return tuple(d * s + entry for d, s in zip(decays, states))

    zero = jnp.zeros((CHUNKS, width), F32)
    ends = lax.fori_loop(0, steps, gather_up, (zero,) * poles, unroll=4)
    states = []
    for n in range(poles):
        factor = wide(spread, n)
        state = shifted(ends[n], 1, backward)
        reach = 1
        while reach < CHUNKS:
            state = state + factor * shifted(state, reach, backward)
            factor = factor * factor
            reach *= 2
        states.append(state)
    gains = [wide(gain, n) for n in range(poles)]

    def advance(i, states):
        entry = source[rows(i), :]
        states = tuple(d * s + entry for d, s in zip(decays, states))
        terms = [g * s for g, s in zip(gains, states)]
        while len(terms) > 1:
            terms = [a + b for a, b in zip(terms[::2], terms[1::2])]
        target[rows(i), :] = terms[0]
        return states

    lax.fori_loop(0, steps, advance, tuple(states), unroll=2)


def row_blocks(length):
    size = 64 if length % 64 == 0 else length
    return [(start, size) for start in range(0, length, size)]


def forward_body(parts, kinds, taps, decay, spread, gain, skip, query, key, value, long_out, gated, feats, signal, summed):
    length, width = query.shape
    blocks = row_blocks(length)
    for j in range(3):
        feats[j, :MARGIN, :] = jnp.zeros((MARGIN, width), F32)
        for start, size in blocks:
            row, total = kinds(parts, j, start, size)
            feats[j, pl.ds(MARGIN + row, size), :] = total.astype(BF16).astype(F32)
    for start, size in blocks:
        mixed = []
        for j in range(3):
            total = taps[j, 0:1, :] * feats[j, MARGIN + start : MARGIN + start + size, :]
            for lag in range(1, taps.shape[1]):
                first = MARGIN + start - lag
                total = total + taps[j, lag : lag + 1, :] * feats[j, first : first + size, :]
            mixed.append(total)
        at = slice(start, start + size)
        query[at, :], key[at, :], value[at, :] = mixed
        signal[at, :] = mixed[1] * mixed[2]
    modal_scan(signal, summed, decay[...], spread[...], gain[...], False)
    for start, size in blocks:
        at = slice(start, start + size)
        result = summed[at, :] + skip[...] * signal[at, :]
        long_out[at, :] = result
        gated[at, :] = (query[at, :] * result).astype(BF16)


def backward_body(parts, kinds, taps, decay, spread, gain, skip, query, key, value, long_out, grads, mixin, grad_long, summed):
    length, width = query.shape
    blocks = row_blocks(length)
    for start, size in blocks:
        row, grad_gated = kinds(parts, 0, start, size)
        at = pl.ds(row, size)
        mixin[0, at, :] = grad_gated * long_out[at, :]
        grad_long[at, :] = grad_gated * query[at, :]
    modal_scan(grad_long, summed, decay[...], spread[...], gain[...], True)
    for start, size in blocks:
        at = slice(start, start + size)
        grad_signal = summed[at, :] + skip[...] * grad_long[at, :]
        mixin[1, at, :] = grad_signal * value[at, :]
        mixin[2, at, :] = grad_signal * key[at, :]
    for j in range(3):
        mixin[j, length : length + MARGIN, :] = jnp.zeros((MARGIN, width), F32)
        for start, size in blocks:
            total = taps[j, 0:1, :] * mixin[j, start : start + size, :]
            for lag in range(1, taps.shape[1]):
                total = total + taps[j, lag : lag + 1, :] * mixin[j, start + lag : start + lag + size, :]
            grads[j, start : start + size, :] = total.astype(BF16)


def sum_of_three(parts, j, start, size):
    half = parts[0].shape[1]
    other, local = divmod(start, half)
    own, near, far = parts[3 * other : 3 * other + 3]
    at = slice(local, local + size)
    total = own[j, at, :] + near[j, at, :].astype(F32) + far[j, at, :].astype(F32)
    return pl.multiple_of(((lax.axis_index("ctx") >> 1) ^ other) * half + local, MARGIN), total


def plain(parts, j, start, size):
    return start, parts[0][j, start : start + size, :].astype(F32)


def filter_forward(parts, kinds, tables, length, width, after=()):
    count = len(parts)
    inputs = count + len(tables)

    def body(*refs):
        forward_body(refs[:count], kinds, *refs[count:inputs], *refs[inputs + len(after) :])

    wide = jax.ShapeDtypeStruct((length, width), F32)
    return call(
        body,
        (wide, wide, wide, wide, jax.ShapeDtypeStruct((length, width), BF16)),
        [
            pltpu.VMEM((3, MARGIN + length, width), F32),
            pltpu.VMEM((length, width), F32),
            pltpu.VMEM((length, width), F32),
        ],
        in_specs=[VMEM] * inputs + [HBM] * len(after),
        us=2.1,
    )(*parts, *tables, *after)


def filter_backward(parts, kinds, tables, saved, length, width, after=()):
    count = len(parts)
    inputs = count + len(tables) + len(saved)

    def body(*refs):
        backward_body(refs[:count], kinds, *refs[count:inputs], *refs[inputs + len(after) :])

    return call(
        body,
        jax.ShapeDtypeStruct((3, length, width), BF16),
        [
            pltpu.VMEM((3, length + MARGIN, width), F32),
            pltpu.VMEM((length, width), F32),
            pltpu.VMEM((length, width), F32),
        ],
        in_specs=[VMEM] * inputs + [HBM] * len(after),
        us=2.1,
    )(*parts, *tables, *saved, *after)


def later(value, *after):
    def body(*refs):
        pass

    return pl.pallas_call(
        body,
        out_shape=jax.ShapeDtypeStruct(value.shape, value.dtype),
        in_specs=[HBM] * (1 + len(after)),
        out_specs=HBM,
        input_output_aliases={0: 0},
        compiler_params=pltpu.CompilerParams(vmem_limit_bytes=SMALL_LIMIT),
        cost_estimate=cost(0.05),
    )(value, *after)


def column_blocks(rows):
    length, width = rows.shape[0], rows.shape[1] // 4

    def body(rows, own, near, far, arrived):
        me = lax.axis_index("ctx")
        side = lax.axis_index("fsdp") & 1
        copies = []
        for n, (mask, out) in enumerate(((2 ^ side, far), (1, near), (0, own))):
            copies.append(pltpu.make_async_copy(rows.at[:, block_at(me ^ mask, width)], out, arrived.at[n]))
            copies[-1].start()
        for copy in copies:
            copy.wait()

    block = jax.ShapeDtypeStruct((length, width), rows.dtype)
    return call(body, (block,) * 3, [pltpu.SemaphoreType.DMA((3,))], in_specs=[HBM], us=0.7)(
        pltpu.with_memory_space_constraint(rows, pltpu.HBM)
    )


def fetched(block):
    pairs = [(4 * f + k, 4 * f + (k ^ 2 ^ (f & 1))) for f in range(8) for k in range(4)]
    return lax.ppermute(block, ("fsdp", "ctx"), pairs)


def project(pieces, other, weight, after=()):
    groups, depth, channels = weight.shape
    part = pieces[0].shape[0]
    length = 2 * part
    width = channels // 4

    def body(first, second, weight, *refs):
        own, far, give, give_far, held, product = refs[len(after) :]
        me = lax.axis_index("ctx")
        core = (me ^ lax.axis_index("fsdp")) & 1 if other else me & 1
        held[block_at(core, part), :] = first[...]
        held[block_at(1 - core, part), :] = second[...]
        for j in range(groups):
            product[...] = dot(held[...], weight[j], (1, 0))
            own[j] = product[:, block_at(me, width)]
            far[j] = product[:, block_at(me ^ 2, width)].astype(BF16)
            give[j] = product[:, block_at(me ^ 1, width)].astype(BF16)
            give_far[j] = product[:, block_at(me ^ 3, width)].astype(BF16)

    sums = jax.ShapeDtypeStruct((groups, length, width), BF16)
    return call(
        body,
        (jax.ShapeDtypeStruct((groups, length, width), F32), sums, sums, sums),
        [pltpu.VMEM((length, depth), BF16), pltpu.VMEM((length, channels), F32)],
        in_specs=[VMEM] * 3 + [HBM] * len(after),
        us=0.45 * groups,
    )(*pieces, weight, *after)


def add_far(left, right, after):
    def body(left, right, *refs):
        refs[-1][...] = (left[...].astype(F32) + right[...].astype(F32)).astype(BF16)

    specs = [VMEM] * 2 + [HBM] * len(after)
    return call(body, jax.ShapeDtypeStruct(left.shape, BF16), in_specs=specs)(left, right, *after)


def channel_sums(pieces, other, weight, after=(), after_add=()):
    own, far, give, give_far = project(pieces, other, weight, after)
    passed = add_far(far, flipped(give_far, "ctx", 1), after_add)
    return (own, flipped(give, "ctx", 1), flipped(passed, "ctx", 2)), passed


def by_token(here, there):
    return here[0], here[1], there[2], there[0], there[1], here[2]


def all_channels(value, far):
    return value, far, flipped(value, "ctx", 1), flipped(far, "ctx", 1)


def output_pieces(gathered, weight, after=()):
    groups, length, width = gathered[0].shape
    piece = weight.shape[1] // 4
    part = length // 4
    channels = 4 * width

    def product(whole, weight, at, index):
        total = None
        for j in range(groups):
            term = dot(whole[j, at, :], weight[j, block_at(index, piece), :], (1, 1))
            total = term if total is None else total + term
        return total.astype(BF16)

    def pieces(whole, weight, side, low, first, second):
        first[...] = product(whole, weight, slice(None), 2 * side)
        for high in range(2):
            rows = slice(high * part, (high + 1) * part)
            for s in range(2):
                columns = slice(s * piece, (s + 1) * piece)
                second[rows, columns] = product(whole, weight, block_at(2 * high + low, part), 2 * s + 1)

    def first_body(own, far, near, near_far, weight, *refs):
        whole, first, second = refs[len(after) :]
        me = lax.axis_index("ctx")
        place = lax.axis_index("fsdp")
        for j in range(groups):
            for mask, value in ((0, own), (2, far), (1, near), (3, near_far)):
                whole[j, :, block_at(me ^ mask, width)] = value[j]
        pieces(whole, weight, 1 - (place & 1), 1 - ((place >> 1) & 1), first, second)

    def second_body(whole, weight, first, second):
        place = lax.axis_index("fsdp")
        pieces(whole, weight, place & 1, (place >> 1) & 1, first, second)

    parts = (jax.ShapeDtypeStruct((length, piece), BF16), jax.ShapeDtypeStruct((2 * part, 2 * piece), BF16))
    whole, *gives = call(
        first_body,
        (jax.ShapeDtypeStruct((groups, length, channels), BF16), *parts),
        in_specs=[VMEM] * 5 + [HBM] * len(after),
        us=0.6 * groups,
    )(*gathered, weight, *after)
    keeps = call(second_body, parts, us=0.4 * groups)(whole, weight)
    return whole, keeps, gives


def exchange(gives):
    return flipped(gives[0], "fsdp", 1), flipped(gives[1], "fsdp", 2)


def final_pairs(flip):
    pairs = []
    for f in range(8):
        for k in range(4):
            high, low, x, y, core = f >> 2, (f >> 1) & 1, f & 1, k >> 1, k & 1
            pairs.append((4 * f + k, 4 * (4 * (y ^ high ^ flip) + 2 * core + x) + 2 * y + low))
    return pairs


def block_sums(keeps, givens, after=(), after_second=()):
    length, piece = keeps[0].shape
    part = length // 4
    both = lambda keep, given, rows, columns: keep[rows, columns].astype(F32) + given[rows, columns].astype(F32)

    def second_body(keep_x, given_x, keep_z, given_z, *refs):
        give_z, give_x, next_z, next_x = refs[len(after) :]
        place = lax.axis_index("fsdp")
        side, low = place & 1, (place >> 1) & 1
        for high in range(2):
            rows = slice(high * part, (high + 1) * part)
            take = lambda bit: both(keep_x, given_x, block_at(2 * high + bit, part), slice(None))
            give_z[rows, :] = take(1 - low).astype(BF16)
            next_z[rows, :] = take(low)
        take = lambda bit: both(keep_z, given_z, slice(None), block_at(bit, piece))
        give_x[...] = take(1 - side).astype(BF16)
        next_x[...] = take(side)

    square = lambda kind: jax.ShapeDtypeStruct((2 * part, piece), kind)
    give_z, give_x, next_z, next_x = call(
        second_body,
        (square(BF16), square(BF16), square(F32), square(F32)),
        in_specs=[VMEM] * 4 + [HBM] * len(after),
    )(keeps[0], givens[0], keeps[1], givens[1], *after)

    def third_body(keep_z, given_z, keep_x, given_x, *refs):
        give, keep = refs[len(after_second) :]
        y = lax.axis_index("ctx") >> 1
        for bit, out in ((1 - y, give), (y, keep)):
            at = block_at(bit, part)
            for half, (mine, other) in enumerate(((keep_z, given_z), (keep_x, given_x))):
                columns = slice(half * piece, (half + 1) * piece)
                out[:, columns] = both(mine, other, at, slice(None)).astype(BF16)

    block = jax.ShapeDtypeStruct((part, 2 * piece), BF16)
    give, keep = call(third_body, (block, block), in_specs=[VMEM] * 4 + [HBM] * len(after_second))(
        next_z, flipped(give_z, "fsdp", 2), next_x, flipped(give_x, "fsdp", 1), *after_second
    )

    def order_body(keep, given, first, second):
        high = lax.axis_index("fsdp") >> 2
        swap = high == 1
        first[...] = jnp.where(swap, given[...].astype(F32), keep[...].astype(F32)).astype(BF16)
        second[...] = jnp.where(swap, keep[...].astype(F32), given[...].astype(F32)).astype(BF16)

    blocks = call(order_body, (block, block))(keep, flipped(give, "ctx", 2))
    arrived = [lax.ppermute(value, ("fsdp", "ctx"), final_pairs(flip)) for flip, value in enumerate(blocks)]

    def last_body(first, second, out):
        out[...] = (first[...].astype(F32) + second[...].astype(F32)).astype(BF16)

    return call(last_body, block)(*arrived), give


def turned(pieces):
    part, depth = pieces[0].shape

    def body(a, b, c, d, out):
        me = lax.axis_index("ctx")
        side = lax.axis_index("fsdp") & 1
        for mask, piece in ((0, a), (1, b), (2 ^ side, c), (3 ^ side, d)):
            out[:, block_at(me ^ mask, part)] = piece[...].T

    return call(body, jax.ShapeDtypeStruct((depth, 4 * part), pieces[0].dtype), us=0.4)(*pieces)


def weight_gradient(rows, values, after=()):
    depth, length = rows.shape
    groups, _, channels = values.shape
    tile = 256
    steps = [(j, i) for j in range(groups) for i in range(depth // tile)]

    def body(rows, values, *refs):
        out, mark, ready, written = refs[len(after) :]
        copies = []
        for n, (j, i) in enumerate(steps):
            at = slice(i * tile, (i + 1) * tile)
            ready[j, at, :] = dot(rows[at, :], values[j], (1, 0))
            copies.append(pltpu.make_async_copy(ready.at[j, at, :], out.at[j, at, :], written.at[n]))
            copies[-1].start()
        mark[...] = jnp.zeros_like(mark)
        for copy in copies:
            copy.wait()

    gradient = jax.ShapeDtypeStruct((groups, depth, channels), F32)
    return pl.pallas_call(
        body,
        out_shape=(gradient, jax.ShapeDtypeStruct((8, LANES), F32)),
        in_specs=[VMEM] * 2 + [HBM] * len(after),
        out_specs=(HBM, VMEM),
        scratch_shapes=[pltpu.VMEM(gradient.shape, F32), pltpu.SemaphoreType.DMA((len(steps),))],
        compiler_params=pltpu.CompilerParams(vmem_limit_bytes=VMEM_LIMIT),
        cost_estimate=cost(1.0 * groups),
    )(rows, values, *after)


def four_by_eight(tokens, weights, tables, out_weight, grad_mixed):
    length, width = 4 * tokens.shape[0], weights.shape[2] // 4
    own, near, far = column_blocks(tokens)
    here = (own, flipped(near, "ctx", 1))
    feats_here, passed = channel_sums(here, 0, weights)
    far = later(fetched(far), passed, *tables)
    there = (far, flipped(far, "fsdp", 1))
    grad_own, grad_near, grad_far = column_blocks(grad_mixed)
    grad_here = (grad_own, flipped(grad_near, "ctx", 1))
    grad_far = fetched(later(grad_far, far))
    grad_there = (grad_far, flipped(grad_far, "fsdp", 1))
    feats_there, passed = channel_sums(there, 1, weights, feats_here[2:], (grad_far,))
    grads_here, _ = channel_sums(grad_here, 0, out_weight[None], (passed,))
    feats = by_token(feats_here, feats_there)
    *saved, gated = filter_forward(feats, sum_of_three, tables, length, width, (grads_here[2], grad_there[1]))
    grads_there, _ = channel_sums(grad_there, 1, out_weight[None], (gated,))
    gated = gated[None]
    gated_far = flipped(gated, "ctx", 2)
    grads = filter_backward(by_token(grads_here, grads_there), sum_of_three, tables, saved, length, width)
    grads = later(grads, gated_far)
    whole_gated, keeps, gives = output_pieces(all_channels(gated, later(gated_far, grads)), out_weight[None])
    givens = exchange(gives)
    mixed_halves = keeps, givens
    grad_out, mark = weight_gradient(turned(grad_here + grad_there), whole_gated)
    token_rows = turned(here + there)
    grads_far = later(flipped(grads, "ctx", 2), *givens, keeps[0], token_rows, mark)
    whole_grads, keeps, gives = output_pieces(all_channels(grads, grads_far), weights)
    mixed, mixed_give = block_sums(*mixed_halves, (), gives[:1])
    grad_in, mark = weight_gradient(token_rows, whole_grads, (mixed_give,))
    grad_tokens, _ = block_sums(keeps, exchange(gives), (mark,))
    return mixed, grad_tokens, grad_in, grad_out[0]


def any_mesh(tokens, weights, tables, out_weight, grad_mixed):
    count = lax.axis_size("ctx")
    columns = lambda rows: lax.all_to_all(rows, "ctx", split_axis=1, concat_axis=0, tiled=True)
    whole_tokens, whole_cotangents = columns(tokens), columns(grad_mixed)
    length, width = whole_tokens.shape[0], weights.shape[2] // count

    def channel_sums(rows, weight):
        partial = jnp.einsum("td,jdc->jtc", rows, weight, preferred_element_type=F32)
        return lax.psum_scatter(partial.astype(BF16), "ctx", scatter_dimension=2, tiled=True)

    def block_sums(values, weight):
        partial = jnp.einsum("jtc,jdc->td", values, weight, preferred_element_type=F32)
        ratio = lax.axis_size("fsdp") // count
        pieces = partial.astype(BF16).reshape(count, length // count, ratio, -1).transpose(0, 2, 1, 3)
        pieces = pieces.reshape(count * ratio, length // count, -1)
        return to_placement(lax.psum_scatter(pieces, "fsdp", scatter_dimension=0, tiled=True)[0])

    feats = channel_sums(whole_tokens, weights)
    grad_gated = channel_sums(whole_cotangents, out_weight[None])
    *saved, gated = filter_forward((feats,), plain, tables, length, width)
    grads = filter_backward((grad_gated,), plain, tables, saved, length, width)
    whole_gated = lax.all_gather(gated, "ctx", axis=1, tiled=True)
    whole_grads = lax.all_gather(grads, "ctx", axis=2, tiled=True)
    mixed = block_sums(whole_gated[None], out_weight[None])
    grad_tokens = block_sums(whole_grads, weights)
    grad_in = jnp.einsum("td,jtc->jdc", whole_tokens, whole_grads, preferred_element_type=F32)
    grad_out = jnp.einsum("td,tc->dc", whole_cotangents, whole_gated, preferred_element_type=F32)
    return mixed, grad_tokens, grad_in, grad_out


def per_device(tokens, in_weight, conv_taps, decay_rate, residue, skip_gain, out_weight, grad_mixed):
    count, blocks = lax.axis_size("ctx"), lax.axis_size("fsdp")
    weights = in_weight.transpose(1, 0, 2)
    length = count * tokens.shape[0]
    width = weights.shape[2] // count
    mine = lambda table: lax.dynamic_slice_in_dim(table, lax.axis_index("ctx") * width, width, table.ndim - 1)
    rate = mine(decay_rate)
    gain = mine(residue) * jnp.sqrt(-jnp.expm1(-2.0 * rate))
    tables = (mine(conv_taps.transpose(1, 0, 2)), jnp.exp(-rate), jnp.exp(-rate * (length // CHUNKS)), gain, mine(skip_gain[None]))
    tuned = count == 4 and blocks == 8 and width % LANES == 0 and tokens.shape[0] % LANES == 0
    plan = four_by_eight if tuned else any_mesh
    mixed, grad_tokens, grad_in, grad_out = plan(tokens, weights, tables, out_weight, grad_mixed)
    return mixed, grad_tokens, grad_in.transpose(1, 0, 2), grad_out


def solution(mesh):
    return jax.shard_map(
        per_device,
        mesh=mesh,
        in_specs=(
            P("ctx", None),
            P("ctx", None, "fsdp"),
            P(None, None, "fsdp"),
            P(None, "fsdp"),
            P(None, "fsdp"),
            P("fsdp"),
            P("ctx", "fsdp"),
            P("ctx", None),
        ),
        out_specs=(P("ctx", "fsdp"), P("ctx", "fsdp"), P("ctx", None, "fsdp"), P("ctx", "fsdp")),
        check_vma=False,
    )
```
